32 devices in a mesh: groups: 2 (over y), row: 4 (over z), col: 4 (over x, core).
Axes of the slice: x: 2, y: 2, z: 4, core: 2. Of those that a mesh axis runs over, the one named last changes fastest.
Arguments:
- node_embed: bfloat16 [384, 256], P(('groups', 'row')), parts along dimension 0, may hold values from -6 to 6
- rotation: float32 [3, 3, 384], P(None, None, 'groups'), parts along dimension 2, may hold values from -1 to 1, as said below
- translation: float32 [3, 384], P(None, 'groups'), parts along dimension 1, may hold values from -8 to 8
- pair_embed: bfloat16 [384, 192, 128], P(('groups', 'row'), 'col'), parts along dimension 0, may hold values from -1300 to 1300
- chain_index: int32 [384], P('groups'), parts along dimension 0, may hold values from 0 to 7, never falling along the last dimension, each value on 1 to 48 neighbouring positions
- residue_mask: int32 [384], P('groups'), parts along dimension 0, may hold values 0 or 1
- step_index: int32 [2], P('groups'), parts along dimension 0, may hold values from 0 to 999
- w_time: bfloat16 [256, 256], replicated, may hold values from -0.375 to 0.375
- w_query: bfloat16 [256, 2048], replicated, may hold values from -0.375 to 0.375
- w_query_points: bfloat16 [256, 192], replicated, may hold values from -0.375 to 0.375
- w_kv: bfloat16 [256, 4096], replicated, may hold values from -0.375 to 0.375
- w_kvp: bfloat16 [256, 480], replicated, may hold values from -0.375 to 0.375
- w_bias: bfloat16 [128, 8], replicated, may hold values from -0.5 to 0.5
- head_weights: float32 [8], replicated, may hold values from -1 to 1.5
- chain_bias: float32 [8], replicated, may hold values from -2 to 2
- w_out: bfloat16 [3456, 256], replicated, may hold values from -0.109375 to 0.109375
- w_mlp_in: bfloat16 [256, 256], replicated, may hold values from -0.375 to 0.375
- w_mlp_out: bfloat16 [256, 256], replicated, may hold values from -0.375 to 0.375
- w_edge_in: bfloat16 [256, 128], replicated, may hold values from -0.375 to 0.375
- w_trunk_in: bfloat16 [384, 384], replicated, may hold values from -0.3125 to 0.3125
- w_trunk_mid: bfloat16 [384, 384], replicated, may hold values from -0.3125 to 0.3125
- w_final: bfloat16 [384, 128], replicated, may hold values from -0.3125 to 0.3125
Outputs:
- node_out: bfloat16 [384, 256], P(('groups', 'row')), parts along dimension 0
- pair_out: bfloat16 [384, 192, 128], P(('groups', 'row'), 'col'), parts along dimension 0
The draws below stay inside these ranges and needn't reach their ends.
There are 2 independent parts, one for each index of `groups`. The reference program is written for one: setup_inputs(seed, part) draws one part's arguments, and reference() takes and returns one part's arrays. A program takes and returns all parts, laid end to end along the dimension named above; an argument that names none is the same for every part. Nothing has to cross between parts.
Inputs may be any that keep to these rules, and one draw needn't show every extreme that they name: Each rotation[:, :, n] is a proper rotation matrix. `chain_index`: chain ids never fall along the residues; each chain has 1 to 48 residues, one exactly that many.
All inputs are finite; a program needn't handle non-finite values.
Results may differ from the reference program's by a relative error of at most 0.012.
Values may be sent and summed in bfloat16 or wider, within the bound.
No kernel may reach another device: no remote copies, remote signals or barrier semaphores. Data moves between devices by JAX's collectives and lax.ppermute only.
A program may use at most 64 MiB of HBM per device.

```python
import math
import jax
import jax.numpy as jnp
import numpy as np
from jax import lax

CS = 256
CZ = 128
HEADS = 8
CH = 256
QP = 8
VP = 12
NH = 128
HID = 384
OUTW = 3456
CHAINS = 8
R_DEV = 48
RES = 192
N_ROW = 4


def draw_rotation(key, part):
    keys_four = jax.random.split(jax.random.fold_in(key, 11), 4)
    real_part = jax.random.uniform(keys_four[0], (RES,), jnp.float32, 1.5, 2.5)
    axis_x = jax.random.uniform(keys_four[1], (RES,), jnp.float32, -1.0, 1.0)
    axis_y = jax.random.uniform(keys_four[2], (RES,), jnp.float32, -1.0, 1.0)
    axis_z = jax.random.uniform(keys_four[3], (RES,), jnp.float32, -1.0, 1.0)
    norm_inv = 1.0 / jnp.sqrt(real_part * real_part + axis_x * axis_x + axis_y * axis_y + axis_z * axis_z)
    real_part = real_part * norm_inv
    axis_x = axis_x * norm_inv
    axis_y = axis_y * norm_inv
    axis_z = axis_z * norm_inv
    row_one = jnp.stack([1.0 - 2.0 * (axis_y * axis_y + axis_z * axis_z), 2.0 * (axis_x * axis_y - real_part * axis_z), 2.0 * (axis_x * axis_z + real_part * axis_y)])
    row_two = jnp.stack([2.0 * (axis_x * axis_y + real_part * axis_z), 1.0 - 2.0 * (axis_x * axis_x + axis_z * axis_z), 2.0 * (axis_y * axis_z - real_part * axis_x)])
    row_three = jnp.stack([2.0 * (axis_x * axis_z - real_part * axis_y), 2.0 * (axis_y * axis_z + real_part * axis_x), 1.0 - 2.0 * (axis_x * axis_x + axis_y * axis_y)])
    return jnp.stack([row_one, row_two, row_three])


def draw_pair_embed(key, part):
    normal_part = jnp.clip(jax.random.normal(key, (RES, RES, CZ), jnp.float32), -6.0, 6.0)
    return normal_part.astype(jnp.bfloat16)


def touch_ends(result, own_key, low, top_value):
    spot = [jax.random.randint(jax.random.fold_in(own_key, axis), (), 0, length) for axis, length in enumerate(result.shape)]
    longest = result.shape.index(max(result.shape))
    next_to = spot[:longest] + [(spot[longest] + 1) % result.shape[longest]] + spot[longest + 1:]
    return result.at[tuple(spot)].set(low).at[tuple(next_to)].set(top_value)


def shard_levels(rng, extent, pieces, low, top_value):
    def one(dim, parts):
        steps = jax.random.uniform(jax.random.fold_in(jax.random.fold_in(rng, 6), dim), (parts,), jnp.float32, low / len(pieces), top_value / len(pieces))
        return jnp.repeat(jnp.exp(steps), extent[dim] // parts).reshape((-1,) + (1,) * (len(extent) - dim - 1))

    gain = one(*pieces[0])
    for cut in pieces[1:]:
        gain = gain * one(*cut)
    return gain


def split_up(amount, total, reach, skew):
    loads = [(1 << 20) // math.isqrt(grade ** skew) + 1 for grade in range(2, amount + 1)]
    rest, given = total - reach - (amount - 1), [1] * (amount - 1)
    while rest > 0:
        movable = [i for i in range(amount - 1) if given[i] < reach]
        pool, budget = sum([loads[i] for i in movable]), rest
        for i in movable:
            addition = min(reach - given[i], max(1, budget * loads[i] // pool), rest)
            given[i] = given[i] + addition
            rest = rest - addition
    return np.array([reach] + given)


def uneven_parts(own_key, number_of, total, most, skew):
    if number_of == 2:
        one = jax.random.randint(own_key, (), max(1, total - most), min(most, total - 1) + 1)
        return jnp.stack([one, total - one])
    lengths = jnp.asarray(split_up(number_of, total, most, skew), jnp.int32)
    twos = (number_of - 1) // 2
    donor, taker = lengths[1:1 + 2 * twos:2], lengths[2:2 + 2 * twos:2]
    margin = jnp.minimum(donor - 1, most - taker)
    moved = jax.random.randint(jax.random.fold_in(own_key, 1), (twos,), 0, 1 << 20) % (margin + 1)
    lengths = lengths.at[1:1 + 2 * twos:2].set(donor - moved).at[2:2 + 2 * twos:2].set(taker + moved)
    return lengths[jax.random.permutation(jax.random.fold_in(own_key, 2), number_of)]


def bell_draw(key, shape, width, most, cuts=(), kind=jnp.bfloat16):
    result = jax.random.normal(key, shape, jnp.float32) * width
    if len(cuts) > 0:
        result = shard_levels(key, shape, cuts, -0.22, 0.18) * result
    return jnp.clip(result, min=-most, max=most).astype(kind)


def setup_inputs(seed: int = 0, part: int = 0) -> dict:
    key_of = jax.random.split(jax.random.key(seed), 23)
    part_splits = jax.random.split(jax.random.fold_in(key_of[22], part), 23)
    node_embed = bell_draw(part_splits[0], (RES, CS), 1.0, 6.0, ((0, 4),))
    rotation = draw_rotation(jax.random.fold_in(jax.random.fold_in(key_of[22], part), 71), part)
    translation = bell_draw(part_splits[2], (3, RES), 2.0, 8.0, (), jnp.float32)
    pair_embed = draw_pair_embed(jax.random.fold_in(jax.random.fold_in(key_of[22], part), 71), part)
    chain_index = jnp.searchsorted(jnp.cumsum(uneven_parts(part_splits[4], CHAINS, RES, RES // 4, 0)), jnp.arange(RES), side="right").astype(jnp.int32)
    residue_mask = touch_ends((jax.random.randint(part_splits[5], (RES,), 0, 8) < 7).astype(jnp.int32), jax.random.fold_in(part_splits[5], 1), 0, 1)
    step_index = jax.random.randint(part_splits[6], (1,), 0, 1000).astype(jnp.int32)
    w_time = bell_draw(key_of[7], (CS, CS), CS ** -0.5, 0.375)
    w_query = bell_draw(key_of[8], (CS, HEADS * CH), CS ** -0.5, 0.375)
    w_query_points = bell_draw(key_of[9], (CS, 3 * HEADS * QP), CS ** -0.5, 0.375)
    w_kv = bell_draw(key_of[10], (CS, 2 * HEADS * CH), CS ** -0.5, 0.375)
    w_kvp = bell_draw(key_of[11], (CS, 3 * HEADS * (QP + VP)), CS ** -0.5, 0.375)
    w_bias = bell_draw(key_of[12], (CZ, HEADS), CZ ** -0.5, 0.5)
    head_weights = jnp.clip(jax.random.uniform(key_of[13], (HEADS,), jnp.float32, -1.0, 1.5), -1.0, 1.5)
    chain_bias = jnp.clip(jax.random.uniform(key_of[14], (HEADS,), jnp.float32, -2.0, 2.0), -2.0, 2.0)
    w_out = bell_draw(key_of[15], (OUTW, CS), OUTW ** -0.5, 0.109375)
    w_mlp_in = bell_draw(key_of[16], (CS, CS), CS ** -0.5, 0.375)
    w_mlp_out = bell_draw(key_of[17], (CS, CS), CS ** -0.5, 0.375)
    w_edge_in = bell_draw(key_of[18], (CS, NH), CS ** -0.5, 0.375)
    w_trunk_in = bell_draw(key_of[19], (HID, HID), HID ** -0.5, 0.3125)
    w_trunk_mid = bell_draw(key_of[20], (HID, HID), HID ** -0.5, 0.3125)
    w_final = bell_draw(key_of[21], (HID, CZ), HID ** -0.5, 0.3125)
    return {"node_embed": node_embed, "rotation": rotation, "translation": translation, "pair_embed": pair_embed, "chain_index": chain_index, "residue_mask": residue_mask, "step_index": step_index, "w_time": w_time, "w_query": w_query, "w_query_points": w_query_points, "w_kv": w_kv, "w_kvp": w_kvp, "w_bias": w_bias, "head_weights": head_weights, "chain_bias": chain_bias, "w_out": w_out, "w_mlp_in": w_mlp_in, "w_mlp_out": w_mlp_out, "w_edge_in": w_edge_in, "w_trunk_in": w_trunk_in, "w_trunk_mid": w_trunk_mid, "w_final": w_final}


norm_epsilon = 1e-05
masked_score = 100000.0
highest = lax.Precision.HIGHEST

def layer_norm(values):
    average = lax.optimization_barrier(jnp.mean(values, -1, keepdims=True))
    centred = values - average
    spread = lax.optimization_barrier(jnp.mean(centred * centred, -1, keepdims=True))
    return centred * lax.rsqrt(spread + norm_epsilon)

def time_embedding(step_index, embed_width):
    half_width = embed_width // 2
    frequency = jnp.exp(-math.log(10000.0) * jnp.arange(half_width, dtype=jnp.float32) / half_width)
    angles = step_index.astype(jnp.float32)[0] * frequency
    return jnp.concatenate([jnp.sin(angles), jnp.cos(angles)])[None, :].astype(jnp.bfloat16)

def to_global(rotation, shift_vec, points):
    turned = jnp.einsum('abn,nbm->nam', rotation, points, precision=highest)
    return turned + jnp.transpose(shift_vec)[:, :, None]

def node_finish(denominator, values_out, points_out, pair_sums, embedded, rotation, shift_vec, mask_rows, w_out, w_mlp_in, w_mlp_out, w_edge_in):
    item_count = embedded.shape[0]
    scale_back = denominator[:, :, None]
    attended = values_out.reshape(item_count, HEADS, CH) / scale_back
    points = points_out.reshape(item_count, 3, HEADS, VP) / denominator[:, None, :, None]
    relative = points - jnp.transpose(shift_vec)[:, :, None, None]
    framed = jnp.einsum('abi,iahv->ibhv', rotation, relative, precision=highest)
    length = jnp.sqrt(jnp.maximum(lax.optimization_barrier(jnp.sum(framed * framed, 1)), 1.0))
    paired = pair_sums.reshape(item_count, HEADS, CZ) / scale_back
    features = jnp.concatenate([attended.reshape(item_count, -1), framed.reshape(item_count, -1), length.reshape(item_count, -1), paired.reshape(item_count, -1)], -1).astype(jnp.bfloat16)
    update = jnp.dot(features, w_out, preferred_element_type=jnp.float32)
    normed = layer_norm(embedded.astype(jnp.float32) + update).astype(jnp.bfloat16)
    normed = lax.optimization_barrier(normed)
    middle = jax.nn.relu(jnp.dot(normed, w_mlp_in, preferred_element_type=jnp.float32)).astype(jnp.bfloat16)
    node_new = layer_norm(normed.astype(jnp.float32) + jnp.dot(middle, w_mlp_out, preferred_element_type=jnp.float32))
    node_new = (node_new * mask_rows.astype(jnp.float32)[:, None]).astype(jnp.bfloat16)
    edge_side = jnp.dot(node_new, w_edge_in, preferred_element_type=jnp.float32).astype(jnp.bfloat16)
    return (node_new, edge_side)

def reference(node_embed, rotation, translation, pair_embed, chain_index, residue_mask, step_index, w_time, w_query, w_query_points, w_kv, w_kvp, w_bias, head_weights, chain_bias, w_out, w_mlp_in, w_mlp_out, w_edge_in, w_trunk_in, w_trunk_mid, w_final):
    embedded = (node_embed.astype(jnp.float32) + jnp.dot(time_embedding(step_index, CS), w_time, preferred_element_type=jnp.float32)).astype(jnp.bfloat16)
    embedded = lax.optimization_barrier(embedded)
    query_feat = jnp.dot(embedded, w_query, preferred_element_type=jnp.float32).astype(jnp.bfloat16).reshape(RES, HEADS, CH)
    query_pts = to_global(rotation, translation, jnp.dot(embedded, w_query_points, preferred_element_type=jnp.float32).reshape(RES, 3, HEADS * QP)).reshape(RES, 3, HEADS, QP)
    key_values = jnp.dot(embedded, w_kv, preferred_element_type=jnp.float32).astype(jnp.bfloat16)
    key_feat = key_values[:, :HEADS * CH].reshape(RES, HEADS, CH)
    value_feat = key_values[:, HEADS * CH:].reshape(RES, HEADS, CH)
    key_points = to_global(rotation, translation, jnp.dot(embedded, w_kvp, preferred_element_type=jnp.float32).reshape(RES, 3, -1)).reshape(RES, 3, HEADS, QP + VP)
    key_pts = key_points[..., :QP]
    value_pts = key_points[..., QP:]
    scaled = math.sqrt(1.0 / 3.0)
    point_weight = math.sqrt(2.0 / (9.0 * QP))
    point_gain = jax.nn.softplus(head_weights)
    key_square = jnp.einsum('jahp,jahp->hj', key_pts, key_pts, precision=highest)
    mask_term = (residue_mask.astype(jnp.float32) - 1.0) * masked_score

    def one_block(block_index):
        row_begin = block_index * R_DEV
        query_rows = lax.dynamic_slice_in_dim(query_feat, row_begin, R_DEV, 0)
        qpts_rows = lax.dynamic_slice_in_dim(query_pts, row_begin, R_DEV, 0)
        pair_rows = lax.dynamic_slice_in_dim(pair_embed, row_begin, R_DEV, 0).astype(jnp.float32)
        chain_rows = lax.dynamic_slice_in_dim(chain_index, row_begin, R_DEV, 0)
        feature_dots = jnp.einsum('ihc,jhc->hij', query_rows.astype(jnp.float32), key_feat.astype(jnp.float32)) / math.sqrt(CH)
        pair_bias = jnp.einsum('ijc,ch->hij', pair_rows, w_bias.astype(jnp.float32))
        same_chain = (chain_rows[:, None] == chain_index[None, :]).astype(jnp.float32)
        query_square = jnp.einsum('iahp,iahp->hi', qpts_rows, qpts_rows, precision=highest)
        cross_term = jnp.einsum('iahp,jahp->hij', qpts_rows, key_pts, precision=highest)
        distance = query_square[:, :, None] + key_square[:, None, :] - 2.0 * cross_term
        scores = scaled * (feature_dots + pair_bias + chain_bias[:, None, None] * same_chain[None]) - scaled * point_weight * 0.5 * point_gain[:, None, None] * distance + mask_term[None, None, :]
        row_peak = lax.optimization_barrier(jnp.max(scores, -1, keepdims=True))
        weights = jnp.exp(scores - row_peak)
        denominator = jnp.transpose(lax.optimization_barrier(jnp.sum(weights, -1)))
        rounded = weights.astype(jnp.bfloat16).astype(jnp.float32)
        values_out = jnp.einsum('hij,jhc->ihc', rounded, value_feat.astype(jnp.float32)).reshape(R_DEV, -1)
        points_out = jnp.einsum('hij,jahv->iahv', weights, value_pts, precision=highest).reshape(R_DEV, -1)
        pair_sums = jnp.einsum('hij,ijc->ihc', rounded, pair_rows).reshape(R_DEV, -1)
        return (denominator, values_out, points_out, pair_sums)
    parts_out = lax.map(one_block, jnp.arange(N_ROW, dtype=jnp.int32))
    denominator = parts_out[0].reshape(RES, HEADS)
    values_out = parts_out[1].reshape(RES, -1)
    points_out = parts_out[2].reshape(RES, -1)
    pair_sums = parts_out[3].reshape(RES, -1)
    node_out, edge_side = node_finish(denominator, values_out, points_out, pair_sums, embedded, rotation, translation, residue_mask, w_out, w_mlp_in, w_mlp_out, w_edge_in)
    mask_all = residue_mask.astype(jnp.float32)

    def edge_block(block_index):
        row_begin = block_index * R_DEV
        pair_rows = lax.dynamic_slice_in_dim(pair_embed, row_begin, R_DEV, 0)
        side_rows = lax.dynamic_slice_in_dim(edge_side, row_begin, R_DEV, 0)
        mask_rows = lax.dynamic_slice_in_dim(mask_all, row_begin, R_DEV, 0)
        stacked = jnp.concatenate([pair_rows, jnp.broadcast_to(side_rows[:, None, :], (R_DEV, RES, NH)), jnp.broadcast_to(edge_side[None, :, :], (R_DEV, RES, NH))], -1).astype(jnp.float32)
        hidden_one = jax.nn.relu(jnp.einsum('ijd,de->ije', stacked, w_trunk_in.astype(jnp.float32))).astype(jnp.bfloat16)
        hidden_two = jax.nn.relu(jnp.einsum('ijd,de->ije', hidden_one.astype(jnp.float32), w_trunk_mid.astype(jnp.float32)))
        joined = (hidden_two + stacked).astype(jnp.bfloat16)
        edge_out = jnp.einsum('ijd,dc->ijc', joined.astype(jnp.float32), w_final.astype(jnp.float32))
        pair_keep = mask_rows[:, None] * mask_all[None, :]
        return (layer_norm(edge_out) * pair_keep[:, :, None]).astype(jnp.bfloat16)
    pair_out = lax.map(edge_block, jnp.arange(N_ROW, dtype=jnp.int32)).reshape(RES, RES, CZ)
    return (node_out, pair_out)
```

```python
import functools
import math

import jax
import jax.numpy as jnp
from jax import lax
from jax.experimental import pallas as pl
from jax.experimental.pallas import tpu as pltpu
from jax.sharding import PartitionSpec as P

CS = 256
CZ = 128
HEADS = 8
CH = 256
QP = 8
VP = 12
NH = 128
HID = 384


norm_epsilon = 1e-05
masked_score = 100000.0
highest = lax.Precision.HIGHEST


def layer_norm(values):
    average = jnp.mean(values, -1, keepdims=True)
    centred = values - average
    spread = jnp.mean(centred * centred, -1, keepdims=True)
    return centred * lax.rsqrt(spread + norm_epsilon)


def time_embedding(step_index, embed_width):
    half_width = embed_width // 2
    frequency = jnp.exp(-math.log(10000.0) * jnp.arange(half_width, dtype=jnp.float32) / half_width)
    angles = step_index.astype(jnp.float32)[0] * frequency
    return jnp.concatenate([jnp.sin(angles), jnp.cos(angles)])[None, :].astype(jnp.bfloat16)


def to_global(rotation, shift_vec, points):
    turned = jnp.einsum("abn,nbm->nam", rotation, points, precision=highest)
    return turned + jnp.transpose(shift_vec)[:, :, None]


def project_keys(embedded, rotation, shift_vec, w_kv, w_kvp):
    item_count = embedded.shape[0]
    key_values = jnp.dot(embedded, w_kv, preferred_element_type=jnp.float32).astype(jnp.bfloat16)
    points = jnp.dot(embedded, w_kvp, preferred_element_type=jnp.float32).reshape(item_count, 3, -1)
    return (key_values, to_global(rotation, shift_vec, points))


def node_finish(
    denominator,
    values_out,
    points_out,
    pair_sums,
    embedded,
    rotation,
    shift_vec,
    mask_rows,
    w_out,
    w_mlp_in,
    w_mlp_out,
    w_edge_in,
):
    item_count = embedded.shape[0]
    scale_back = denominator[:, :, None]
    attended = values_out.reshape(item_count, HEADS, CH) / scale_back
    points = points_out.reshape(item_count, 3, HEADS, VP) / denominator[:, None, :, None]
    relative = points - jnp.transpose(shift_vec)[:, :, None, None]
    framed = jnp.einsum("abi,iahv->ibhv", rotation, relative, precision=highest)
    length = jnp.sqrt(jnp.maximum(jnp.sum(framed * framed, 1), 1.0))
    paired = pair_sums.reshape(item_count, HEADS, CZ) / scale_back
    features = jnp.concatenate(
        [
            attended.reshape(item_count, -1),
            framed.reshape(item_count, -1),
            length.reshape(item_count, -1),
            paired.reshape(item_count, -1),
        ],
        -1,
    ).astype(jnp.bfloat16)
    update = jnp.dot(features, w_out, preferred_element_type=jnp.float32)
    normed = layer_norm(embedded.astype(jnp.float32) + update).astype(jnp.bfloat16)
    normed = lax.optimization_barrier(normed)
    middle = jax.nn.relu(jnp.dot(normed, w_mlp_in, preferred_element_type=jnp.float32)).astype(
        jnp.bfloat16
    )
    node_new = layer_norm(
        normed.astype(jnp.float32) + jnp.dot(middle, w_mlp_out, preferred_element_type=jnp.float32)
    )
    node_new = (node_new * mask_rows.astype(jnp.float32)[:, None]).astype(jnp.bfloat16)
    edge_side = jnp.dot(node_new, w_edge_in, preferred_element_type=jnp.float32).astype(
        jnp.bfloat16
    )
    return (node_new, edge_side)


def body(
    node_embed,
    rotation,
    translation,
    pair_embed,
    chain_index,
    residue_mask,
    step_index,
    w_time,
    w_query,
    w_query_points,
    w_kv,
    w_kvp,
    w_bias,
    head_weights,
    chain_bias,
    w_out,
    w_mlp_in,
    w_mlp_out,
    w_edge_in,
    w_trunk_in,
    w_trunk_mid,
    w_final,
):
    row_count = node_embed.shape[0]
    key_count = pair_embed.shape[1]
    row_start = lax.axis_index("row") * row_count
    key_start = lax.axis_index("col") * key_count
    embedded = (
        node_embed.astype(jnp.float32)
        + jnp.dot(time_embedding(step_index, CS), w_time, preferred_element_type=jnp.float32)
    ).astype(jnp.bfloat16)
    embedded = lax.optimization_barrier(embedded)
    rot_rows = lax.dynamic_slice_in_dim(rotation, row_start, row_count, 2)
    shift_rows = lax.dynamic_slice_in_dim(translation, row_start, row_count, 1)
    mask_rows = lax.dynamic_slice_in_dim(residue_mask, row_start, row_count, 0)
    mask_keys = lax.dynamic_slice_in_dim(residue_mask, key_start, key_count, 0)
    chain_rows = lax.dynamic_slice_in_dim(chain_index, row_start, row_count, 0)
    chain_keys = lax.dynamic_slice_in_dim(chain_index, key_start, key_count, 0)
    query_feat = (
        jnp.dot(embedded, w_query, preferred_element_type=jnp.float32)
        .astype(jnp.bfloat16)
        .reshape(row_count, HEADS, CH)
    )
    query_pts = to_global(
        rot_rows,
        shift_rows,
        jnp.dot(embedded, w_query_points, preferred_element_type=jnp.float32).reshape(
            row_count, 3, HEADS * QP
        ),
    ).reshape(row_count, 3, HEADS, QP)
    all_nodes = lax.all_gather(embedded, "row", axis=0, tiled=True)
    key_nodes = lax.dynamic_slice_in_dim(all_nodes, key_start, key_count, 0)
    rot_keys = lax.dynamic_slice_in_dim(rotation, key_start, key_count, 2)
    shift_keys = lax.dynamic_slice_in_dim(translation, key_start, key_count, 1)
    key_values, key_points = project_keys(key_nodes, rot_keys, shift_keys, w_kv, w_kvp)
    key_feat = key_values[:, : HEADS * CH].reshape(key_count, HEADS, CH)
    value_feat = key_values[:, HEADS * CH :].reshape(key_count, HEADS, CH)
    key_points = key_points.reshape(key_count, 3, HEADS, QP + VP)
    key_pts = key_points[..., :QP]
    value_pts = key_points[..., QP:]
    scaled = math.sqrt(1.0 / 3.0)
    point_weight = math.sqrt(2.0 / (9.0 * QP))
    point_gain = jax.nn.softplus(head_weights)
    feature_dots = jnp.einsum(
        "ihc,jhc->hij", query_feat, key_feat, preferred_element_type=jnp.float32
    ) / math.sqrt(CH)
    pair_bias = jnp.einsum("ijc,ch->hij", pair_embed, w_bias, preferred_element_type=jnp.float32)
    same_chain = (chain_rows[:, None] == chain_keys[None, :]).astype(jnp.float32)
    query_square = jnp.einsum("iahp,iahp->hi", query_pts, query_pts, precision=highest)
    key_square = jnp.einsum("jahp,jahp->hj", key_pts, key_pts, precision=highest)
    cross_term = jnp.einsum("iahp,jahp->hij", query_pts, key_pts, precision=highest)
    distance = query_square[:, :, None] + key_square[:, None, :] - 2.0 * cross_term
    mask_term = (mask_keys.astype(jnp.float32) - 1.0) * masked_score
    scores = (
        scaled * (feature_dots + pair_bias + chain_bias[:, None, None] * same_chain[None])
        - scaled * point_weight * 0.5 * point_gain[:, None, None] * distance
        + mask_term[None, None, :]
    )
    row_peak = lax.pmax(jnp.max(scores, -1), "col")
    weights = jnp.exp(scores - row_peak[:, :, None])
    denominator = jnp.transpose(jnp.sum(weights, -1))
    rounded = weights.astype(jnp.bfloat16)
    values_out = jnp.einsum(
        "hij,jhc->ihc", rounded, value_feat, preferred_element_type=jnp.float32
    ).reshape(row_count, -1)
    points_out = jnp.einsum("hij,jahv->iahv", weights, value_pts, precision=highest).reshape(
        row_count, -1
    )
    pair_sums = jnp.einsum(
        "hij,ijc->ihc", rounded, pair_embed, preferred_element_type=jnp.float32
    ).reshape(row_count, -1)
    summed = lax.psum((denominator, values_out, points_out, pair_sums), "col")
    node_out, edge_side = node_finish(
        summed[0],
        summed[1],
        summed[2],
        summed[3],
        embedded,
        rot_rows,
        shift_rows,
        mask_rows,
        w_out,
        w_mlp_in,
        w_mlp_out,
        w_edge_in,
    )
    side_all = lax.all_gather(edge_side, "row", axis=0, tiled=True)
    side_rows = lax.dynamic_slice_in_dim(side_all, row_start, row_count, 0)
    side_keys = lax.dynamic_slice_in_dim(side_all, key_start, key_count, 0)
    pre_rows = jnp.dot(side_rows, w_trunk_in[CZ : CZ + NH], preferred_element_type=jnp.float32)
    pre_keys = jnp.dot(side_keys, w_trunk_in[CZ + NH :], preferred_element_type=jnp.float32)
    mask_key_f = mask_keys.astype(jnp.float32)
    block_rows = math.gcd(row_count, 8)
    block_count = row_count // block_rows

    def edge_block(inputs):
        pair_block, pre_block, side_block, keep_block = inputs
        lifted = (
            jnp.einsum(
                "ijc,cd->ijd", pair_block, w_trunk_in[:CZ], preferred_element_type=jnp.float32
            )
            + pre_block[:, None, :]
            + pre_keys[None, :, :]
        )
        hidden_one = jax.nn.relu(lifted).astype(jnp.bfloat16)
        hidden_two = jax.nn.relu(
            jnp.einsum("ijd,de->ije", hidden_one, w_trunk_mid, preferred_element_type=jnp.float32)
        )
        stacked = jnp.concatenate(
            [
                pair_block,
                jnp.broadcast_to(side_block[:, None, :], (block_rows, key_count, NH)),
                jnp.broadcast_to(side_keys[None, :, :], (block_rows, key_count, NH)),
            ],
            -1,
        )
        joined = (hidden_two + stacked.astype(jnp.float32)).astype(jnp.bfloat16)
        edge_out = jnp.einsum("ijd,dc->ijc", joined, w_final, preferred_element_type=jnp.float32)
        pair_keep = keep_block.astype(jnp.float32)[:, None] * mask_key_f[None, :]
        return (layer_norm(edge_out) * pair_keep[:, :, None]).astype(jnp.bfloat16)

    pair_out = lax.map(
        edge_block,
        (
            pair_embed.reshape(block_count, block_rows, key_count, CZ),
            pre_rows.reshape(block_count, block_rows, HID),
            side_rows.reshape(block_count, block_rows, NH),
            mask_rows.reshape(block_count, block_rows),
        ),
    )
    return (node_out, pair_out.reshape(row_count, key_count, CZ))


PAD = 64
GAIN = math.sqrt(1.0 / 3.0)
POINT = math.sqrt(2.0 / (9.0 * QP))
f32 = jnp.float32
bf16 = jnp.bfloat16


def dot(a, b, dims=((1,), (0,)), precision=None):
    return lax.dot_general(a, b, (dims, ((), ())), precision=precision, preferred_element_type=f32)


NT = ((1,), (1,))
TN = ((0,), (0,))


def params(mib):
    return pltpu.CompilerParams(vmem_limit_bytes=mib * 1024 * 1024)


def vmem(count):
    return [pl.BlockSpec(memory_space=pltpu.VMEM)] * count


def bias_kernel(pair_ref, w_ref, out_ref):
    w_t = jnp.transpose(w_ref[...].astype(f32)).astype(bf16)
    half = pair_ref.shape[0] // 2
    keys = pair_ref.shape[1]
    gap = jnp.zeros((PAD - keys, CZ), bf16)
    for i in range(half):
        both = jnp.concatenate([pair_ref[i], gap, pair_ref[i + half], gap], 0)
        out_ref[pl.ds(i, HEADS, stride=half), :] = dot(w_t, both, NT) * GAIN


def one_hot(shape, source_dim, offset_of):
    src = lax.broadcasted_iota(jnp.int32, shape, source_dim)
    dst = lax.broadcasted_iota(jnp.int32, shape, 1 - source_dim)
    return (src == offset_of(dst)).astype(f32)


def prepare_kernel(
    step_ref, hw_ref, node_ref, feats_ref, w_time_ref, w_query_ref, w_qp_ref, w_kv_ref, w_kvp_ref, w_out_ref,
    time_ref, own_ref, qk_ref, qpts_ref, w_mix_ref, w_pts_ref, kfeat_ref, rows_ref, keys_ref, w_head_ref, sem,
):
    copy = pltpu.make_async_copy(w_out_ref.at[pl.ds(0, HEADS * CH)], w_head_ref, sem)
    copy.start()
    rows = node_ref.shape[0]
    total = feats_ref.shape[1]
    half = CS // 2
    row = lax.axis_index("row")
    col = lax.axis_index("col")
    lane = lax.broadcasted_iota(jnp.int32, (8, half), 1).astype(f32)
    frequency = jnp.exp(-math.log(10000.0) * lane / half)
    angles = step_ref[0].astype(f32) * frequency
    temb = jnp.concatenate([jnp.sin(angles), jnp.cos(angles)], 1).astype(bf16)
    time = dot(temb, w_time_ref[...])
    time_ref[...] = time
    own = (node_ref[...].astype(f32) + time[0:1]).astype(bf16)
    own_ref[...] = own
    feats = feats_ref[...]

    def key_of(dst):
        part = dst // PAD
        inside = dst - part * PAD
        return jnp.where(inside < rows, (part ^ col) * rows + inside, -1)

    kfeat_ref[...] = dot(feats, one_hot((total, 4 * PAD), 0, key_of), precision=highest)
    own_cols = dot(one_hot((rows, total), 1, lambda d: d + row * rows), feats, NT, precision=highest)
    rows_ref[...] = own_cols
    keys_ref[...] = dot(one_hot((rows, total), 1, lambda d: d + col * rows), feats, NT, precision=highest)
    copy.wait()
    query = dot(own, w_query_ref[...]).astype(bf16)
    for h in range(HEADS):
        taken = dot(query[:, h * CH : (h + 1) * CH], w_kv_ref[:, h * CH : (h + 1) * CH], NT)
        qk_ref[h * rows : (h + 1) * rows, :] = (taken * (GAIN / math.sqrt(CH))).astype(bf16)
        w_mix_ref[h * CH : (h + 1) * CH, :] = dot(
            w_kv_ref[:, (HEADS + h) * CH : (HEADS + h + 1) * CH], w_head_ref[h * CH : (h + 1) * CH, :]
        ).astype(bf16)
    wide = HEADS * QP
    local = dot(own, w_qp_ref[...])
    parts = [local[:, b * wide : (b + 1) * wide] for b in range(3)]
    points = []
    for a in range(3):
        turned = own_cols[:, 9 + a : 10 + a]
        for b in range(3):
            turned = turned + own_cols[:, 3 * a + b : 3 * a + b + 1] * parts[b]
        points.append(turned)
    points = jnp.concatenate(points + [jnp.zeros((rows, wide), f32)], 1)
    lanes = lax.broadcasted_iota(jnp.int32, (1, 4 * wide), 1)
    head_lane = lax.broadcasted_iota(jnp.int32, (1, 128), 1)
    hw = jnp.zeros((1, 128), f32)
    for h in range(HEADS):
        hw = jnp.where(head_lane == h, hw_ref[h], hw)
    gains = GAIN * POINT * 0.5 * (jnp.maximum(hw, 0.0) + jnp.log1p(jnp.exp(-jnp.abs(hw))))
    rows_ref[...] = own_cols
    for h in range(HEADS):
        gain = gains[:, h : h + 1]
        mine = jnp.where((lanes % wide) // QP == h, points, 0.0)
        square = jnp.sum(mine * mine, 1, keepdims=True)
        qpts_ref[h * rows : (h + 1) * rows, :] = jnp.where(lanes == 3 * wide, -square, 2.0 * mine) * gain
    width = w_kvp_ref.shape[1]
    group = HEADS * (QP + VP)
    dst = lax.broadcasted_iota(jnp.int32, (width, width), 0)
    src = lax.broadcasted_iota(jnp.int32, (width, width), 1)
    comp = dst // group
    inside = dst - comp * group
    value = inside - HEADS * QP
    from_key = (inside // QP) * (QP + VP) + inside % QP
    from_value = (value // VP) * (QP + VP) + QP + value % VP
    wanted = comp * group + jnp.where(inside < HEADS * QP, from_key, from_value)
    order = (src == wanted).astype(f32).astype(bf16)
    w_pts_ref[...] = dot(order, w_kvp_ref[...], NT).astype(bf16)


def attention_kernel(
    hw_ref, cb_ref, own_ref, n1_ref, n2_ref, n3_ref, time_ref, qk_ref, qpts_ref, w_mix_ref, w_pts_ref, kfeat_ref,
    rows_ref, b0_ref, b1_ref, b2_ref, b3_ref, pair_ref, w_out_ref,
    out_ref, x_ref, prob_ref, near_ref, opair_ref, w_tail_ref, sem,
):
    rows = own_ref.shape[0]
    half = rows // 2
    row = lax.axis_index("row")
    col = lax.axis_index("col")
    tail = HEADS * CH
    copy = pltpu.make_async_copy(w_out_ref.at[pl.ds(tail, w_out_ref.shape[0] - tail)], w_tail_ref, sem)
    copy.start()
    time = time_ref[0:1]
    x_ref[...] = jnp.zeros(x_ref.shape, bf16)
    x_ref[pl.ds(pl.multiple_of((col ^ row) * PAD, PAD), rows), :] = own_ref[...]
    for k, ref in ((1, n1_ref), (2, n2_ref), (3, n3_ref)):
        place = col ^ ((row + 4 - k) % 4)
        x_ref[pl.ds(pl.multiple_of(place * PAD, PAD), rows), :] = (ref[...].astype(f32) + time).astype(bf16)
    x = x_ref[...]
    keys = x.shape[0]
    kfeat = kfeat_ref[...]
    group = HEADS * (QP + VP)
    wide = HEADS * QP
    local = dot(w_pts_ref[...], x, NT)
    points = []
    for a in range(3):
        turned = kfeat[9 + a : 10 + a]
        for b in range(3):
            turned = turned + kfeat[3 * a + b : 3 * a + b + 1] * local[b * group : (b + 1) * group]
        points.append(turned)
    key_points = [p[:wide] for p in points]
    cross = dot(qpts_ref[...], jnp.concatenate(key_points + [jnp.ones((wide, keys), f32)], 0), precision=highest)
    key_square = key_points[0] * key_points[0] + key_points[1] * key_points[1] + key_points[2] * key_points[2]
    feature = dot(qk_ref[...], x, NT)
    lane = lax.broadcasted_iota(jnp.int32, (1, 128), 1)
    low = lane < PAD
    bias_low, bias_high = [], []
    for left, right in ((b0_ref, b1_ref), (b2_ref, b3_ref)):
        left, right = left[...], right[...]
        bias_low.append(jnp.where(low, left, pltpu.roll(right, PAD, 1)))
        bias_high.append(jnp.where(low, pltpu.roll(left, PAD, 1), right))
    bias_low = jnp.concatenate(bias_low, 1)
    bias_high = jnp.concatenate(bias_high, 1)
    key_lane = lax.broadcasted_iota(jnp.int32, (1, keys), 1)
    blocked = jnp.where(key_lane % PAD < rows, (kfeat[12:13] - 1.0) * masked_score, -1e30)
    own_cols = rows_ref[...]
    same = (own_cols[:, 13:14] == kfeat[13:14]).astype(f32)
    hw = jnp.zeros((1, 128), f32)
    for h in range(HEADS):
        hw = jnp.where(lane == h, hw_ref[h], hw)
    gains = GAIN * POINT * 0.5 * (jnp.maximum(hw, 0.0) + jnp.log1p(jnp.exp(-jnp.abs(hw))))
    for h in range(HEADS):
        at = slice(h * rows, (h + 1) * rows)
        square = jnp.sum(key_square[h * QP : (h + 1) * QP], 0, keepdims=True)
        bias = jnp.concatenate([bias_low[h * half : (h + 1) * half], bias_high[h * half : (h + 1) * half]], 0)
        score = (
            feature[at] + bias + (GAIN * cb_ref[h]) * same + cross[at] + (blocked - gains[:, h : h + 1] * square)
        )
        peak = jnp.max(score, 1, keepdims=True)
        weight = jnp.exp(score - peak)
        weight = weight / jnp.sum(weight, 1, keepdims=True)
        prob_ref[at, :] = weight
        near_ref[at, :] = weight[:, :128]
    prob = prob_ref[...]
    prob_low = prob.astype(bf16)
    mixed = dot(prob_low, x).astype(bf16)
    mixed = jnp.concatenate([mixed[h * rows : (h + 1) * rows] for h in range(HEADS)], 1)
    update = dot(mixed, w_mix_ref[...])
    empty = jnp.zeros((128 - HEADS * VP, keys), f32)
    value_points = jnp.concatenate([x for p in points for x in (p[wide:], empty)], 0)
    gathered = dot(prob, value_points, NT, precision=highest)
    spread = lax.broadcasted_iota(jnp.int32, (1, 3 * 128), 1) % 128 // VP
    kept = jnp.zeros((rows, 3 * 128), f32)
    for h in range(HEADS):
        kept = jnp.where(spread == h, gathered[h * rows : (h + 1) * rows], kept)
    relative = [kept[:, a * 128 : (a + 1) * 128] - own_cols[:, 9 + a : 10 + a] for a in range(3)]
    framed = []
    for b in range(3):
        framed.append(
            own_cols[:, b : b + 1] * relative[0]
            + own_cols[:, 3 + b : 4 + b] * relative[1]
            + own_cols[:, 6 + b : 7 + b] * relative[2]
        )
    length = jnp.sqrt(jnp.maximum(framed[0] * framed[0] + framed[1] * framed[1] + framed[2] * framed[2], 1.0))
    own_keys = pair_ref.shape[1]
    for i in range(rows):
        weight = near_ref[pl.ds(i, HEADS, stride=rows), :][:, :own_keys].astype(bf16)
        opair_ref[pl.ds(i, HEADS, stride=rows), :] = dot(weight, pair_ref[i])
    copy.wait()
    span = HEADS * VP
    for n, part in enumerate(framed + [length]):
        update = update + dot(part[:, :span].astype(bf16), w_tail_ref[n * span : (n + 1) * span])
    paired = jnp.concatenate([opair_ref[h * rows : (h + 1) * rows, :] for h in range(HEADS)], 1).astype(bf16)
    out_ref[...] = (0.25 * update + dot(paired, w_tail_ref[4 * span :])).astype(out_ref.dtype)


def node_kernel(u0_ref, u1_ref, u2_ref, u3_ref, own_ref, rows_ref, w_in_ref, w_back_ref, w_edge_ref, node_ref, side_ref):
    update = (u0_ref[...].astype(f32) + u1_ref[...].astype(f32)) + (u2_ref[...].astype(f32) + u3_ref[...].astype(f32))
    normed = layer_norm(own_ref[...].astype(f32) + update).astype(bf16)
    middle = jnp.maximum(dot(normed, w_in_ref[...]), 0.0).astype(bf16)
    node = layer_norm(normed.astype(f32) + dot(middle, w_back_ref[...]))
    node = (node * rows_ref[:, 12:13]).astype(bf16)
    node_ref[...] = node
    side_ref[...] = dot(node, w_edge_ref[...]).astype(bf16)


def edge_kernel(side_ref, other_ref, rows_ref, keys_ref, pair_ref, w_in_ref, w_mid_ref, w_final_ref, out_ref):
    rows, keys = pair_ref.shape[:2]
    step = 8
    w_in = w_in_ref[...]
    side = side_ref[...]
    other = other_ref[...]
    pre_rows = dot(side, w_in[CZ : CZ + NH])
    pre_keys = dot(other, w_in[CZ + NH :])
    side = side.astype(f32)
    other = other.astype(f32)
    keep_rows = rows_ref[:, 12:13]
    keep_keys = keys_ref[:, 12:13]
    for begin in range(0, rows, step):
        pair = pair_ref[begin : begin + step].reshape(step * keys, CZ)
        lifted = dot(pair, w_in[:CZ])
        first = jnp.concatenate(
            [
                jnp.maximum(lifted[n * keys : (n + 1) * keys] + (pre_keys + pre_rows[begin + n : begin + n + 1]), 0.0).astype(bf16)
                for n in range(step)
            ],
            0,
        )
        second = jnp.maximum(dot(first, w_mid_ref[...]), 0.0)
        stacked = jnp.concatenate(
            [
                pair.astype(f32),
                jnp.concatenate([jnp.broadcast_to(side[begin + n : begin + n + 1], (keys, NH)) for n in range(step)], 0),
                jnp.concatenate([other] * step, 0),
            ],
            1,
        )
        edge = layer_norm(dot((second + stacked).astype(bf16), w_final_ref[...]))
        for n in range(step):
            keep = keep_keys * keep_rows[begin + n : begin + n + 1]
            out_ref[begin + n] = (edge[n * keys : (n + 1) * keys] * keep).astype(bf16)


def tile_body(
    node_embed, rotation, translation, pair_embed, chain_index, residue_mask, step_index, w_time, w_query,
    w_query_points, w_kv, w_kvp, w_bias, head_weights, chain_bias, w_out, w_mlp_in, w_mlp_out, w_edge_in,
    w_trunk_in, w_trunk_mid, w_final,
):
    rows = node_embed.shape[0]
    total = residue_mask.shape[0]
    smem = pl.BlockSpec(memory_space=pltpu.SMEM)
    others = [lax.ppermute(node_embed, "row", [(i, (i + k) % 4) for i in range(4)]) for k in (1, 2, 3)]
    bias = pl.pallas_call(
        bias_kernel,
        out_shape=jax.ShapeDtypeStruct((HEADS * rows // 2, 2 * PAD), f32),
        in_specs=vmem(2),
        out_specs=pl.BlockSpec(memory_space=pltpu.VMEM),
        compiler_params=params(16),
    )(pair_embed, w_bias)
    biases = [lax.ppermute(bias, "col", [(i, i ^ k) for i in range(4)]) for k in (1, 2, 3)]
    feats = jnp.concatenate(
        [
            rotation.reshape(9, total),
            translation,
            residue_mask.astype(f32)[None],
            chain_index.astype(f32)[None],
            jnp.zeros((2, total), f32),
        ],
        0,
    )
    prepared = pl.pallas_call(
        prepare_kernel,
        out_shape=(
            jax.ShapeDtypeStruct((8, CS), f32),
            jax.ShapeDtypeStruct((rows, CS), bf16),
            jax.ShapeDtypeStruct((HEADS * rows, CS), bf16),
            jax.ShapeDtypeStruct((HEADS * rows, 4 * HEADS * QP), f32),
            jax.ShapeDtypeStruct((HEADS * CH, CS), bf16),
            jax.ShapeDtypeStruct((w_kvp.shape[1], CS), bf16),
            jax.ShapeDtypeStruct((16, 4 * PAD), f32),
            jax.ShapeDtypeStruct((rows, 16), f32),
            jax.ShapeDtypeStruct((rows, 16), f32),
        ),
        in_specs=[smem, smem] + vmem(7) + [pl.BlockSpec(memory_space=pl.ANY)],
        out_specs=tuple(vmem(9)),
        scratch_shapes=[pltpu.VMEM((HEADS * CH, CS), bf16), pltpu.SemaphoreType.DMA],
        compiler_params=params(24),
        cost_estimate=pl.CostEstimate(flops=2 * 10**9, bytes_accessed=8 * 10**6, transcendentals=0),
    )(step_index, head_weights, node_embed, feats, w_time, w_query, w_query_points, w_kv, w_kvp, w_out)
    time, own, qk, qpts, w_mix, w_pts, kfeat, row_cols, key_cols = prepared
    partial = pl.pallas_call(
        attention_kernel,
        out_shape=jax.ShapeDtypeStruct((rows, CS), f32),
        in_specs=[smem, smem] + vmem(16) + [pl.BlockSpec(memory_space=pl.ANY)],
        out_specs=pl.BlockSpec(memory_space=pltpu.VMEM),
        scratch_shapes=[
            pltpu.VMEM((4 * PAD, CS), bf16),
            pltpu.VMEM((HEADS * rows, 4 * PAD), f32),
            pltpu.VMEM((HEADS * rows, 2 * PAD), f32),
            pltpu.VMEM((HEADS * rows, CZ), f32),
            pltpu.VMEM((w_out.shape[0] - HEADS * CH, CS), bf16),
            pltpu.SemaphoreType.DMA,
        ],
        compiler_params=params(24),
    )(head_weights, chain_bias, own, *others, time, qk, qpts, w_mix, w_pts, kfeat, row_cols, bias, *biases, pair_embed, w_out)
    partials = [lax.ppermute(partial, "col", [(i, i ^ k) for i in range(4)]) for k in (1, 2, 3)]
    node_out, side = pl.pallas_call(
        node_kernel,
        out_shape=(jax.ShapeDtypeStruct((rows, CS), bf16), jax.ShapeDtypeStruct((rows, NH), bf16)),
        in_specs=vmem(9),
        out_specs=tuple(vmem(2)),
        compiler_params=params(16),
    )(partial, *partials, own, row_cols, w_mlp_in, w_mlp_out, w_edge_in)
    turned = [(c * 4 + r, r * 4 + c) for r in range(4) for c in range(4)]
    other = lax.ppermute(side, ("row", "col"), turned)
    pair_out = pl.pallas_call(
        edge_kernel,
        out_shape=jax.ShapeDtypeStruct(pair_embed.shape, bf16),
        in_specs=vmem(8),
        out_specs=pl.BlockSpec(memory_space=pltpu.VMEM),
        compiler_params=params(24),
    )(side, other, row_cols, key_cols, pair_embed, w_trunk_in, w_trunk_mid, w_final)
    return node_out, pair_out


def dispatch(sizes, *arrays):
    rows, keys = arrays[3].shape[:2]
    square = sizes["row"] == 4 and sizes["col"] == 4 and rows == keys and rows == 48
    return tile_body(*arrays) if square else body(*arrays)


def solution(mesh):
    return jax.shard_map(
        functools.partial(dispatch, dict(mesh.shape)),
        mesh=mesh,
        in_specs=(
            P(("groups", "row"), None),
            P(None, None, "groups"),
            P(None, "groups"),
            P(("groups", "row"), "col", None),
            P("groups"),
            P("groups"),
            P("groups"),
            P(),
            P(),
            P(),
            P(),
            P(),
            P(),
            P(),
            P(),
            P(),
            P(),
            P(),
            P(),
            P(),
            P(),
            P(),
        ),
        out_specs=(P(("groups", "row"), None), P(("groups", "row"), "col", None)),
        check_vma=False,
    )
```

```python
import functools
import math

import jax
import jax.numpy as jnp
from jax import lax
from jax.experimental import pallas as pl
from jax.experimental.pallas import tpu as pltpu
from jax.sharding import PartitionSpec as P

CS = 256
CZ = 128
HEADS = 8
CH = 256
QP = 8
VP = 12
NH = 128
HID = 384


norm_epsilon = 1e-05
masked_score = 100000.0
highest = lax.Precision.HIGHEST


def layer_norm(values):
    average = jnp.mean(values, -1, keepdims=True)
    centred = values - average
    spread = jnp.mean(centred * centred, -1, keepdims=True)
    return centred * lax.rsqrt(spread + norm_epsilon)


def time_embedding(step_index, embed_width):
    half_width = embed_width // 2
    frequency = jnp.exp(-math.log(10000.0) * jnp.arange(half_width, dtype=jnp.float32) / half_width)
    angles = step_index.astype(jnp.float32)[0] * frequency
    return jnp.concatenate([jnp.sin(angles), jnp.cos(angles)])[None, :].astype(jnp.bfloat16)


def to_global(rotation, shift_vec, points):
    turned = jnp.einsum("abn,nbm->nam", rotation, points, precision=highest)
    return turned + jnp.transpose(shift_vec)[:, :, None]


def project_keys(embedded, rotation, shift_vec, w_kv, w_kvp):
    item_count = embedded.shape[0]
    key_values = jnp.dot(embedded, w_kv, preferred_element_type=jnp.float32).astype(jnp.bfloat16)
    points = jnp.dot(embedded, w_kvp, preferred_element_type=jnp.float32).reshape(item_count, 3, -1)
    return (key_values, to_global(rotation, shift_vec, points))


def node_finish(
    denominator,
    values_out,
    points_out,
    pair_sums,
    embedded,
    rotation,
    shift_vec,
    mask_rows,
    w_out,
    w_mlp_in,
    w_mlp_out,
    w_edge_in,
):
    item_count = embedded.shape[0]
    scale_back = denominator[:, :, None]
    attended = values_out.reshape(item_count, HEADS, CH) / scale_back
    points = points_out.reshape(item_count, 3, HEADS, VP) / denominator[:, None, :, None]
    relative = points - jnp.transpose(shift_vec)[:, :, None, None]
    framed = jnp.einsum("abi,iahv->ibhv", rotation, relative, precision=highest)
    length = jnp.sqrt(jnp.maximum(jnp.sum(framed * framed, 1), 1.0))
    paired = pair_sums.reshape(item_count, HEADS, CZ) / scale_back
    features = jnp.concatenate(
        [
            attended.reshape(item_count, -1),
            framed.reshape(item_count, -1),
            length.reshape(item_count, -1),
            paired.reshape(item_count, -1),
        ],
        -1,
    ).astype(jnp.bfloat16)
    update = jnp.dot(features, w_out, preferred_element_type=jnp.float32)
    normed = layer_norm(embedded.astype(jnp.float32) + update).astype(jnp.bfloat16)
    normed = lax.optimization_barrier(normed)
    middle = jax.nn.relu(jnp.dot(normed, w_mlp_in, preferred_element_type=jnp.float32)).astype(
        jnp.bfloat16
    )
    node_new = layer_norm(
        normed.astype(jnp.float32) + jnp.dot(middle, w_mlp_out, preferred_element_type=jnp.float32)
    )
    node_new = (node_new * mask_rows.astype(jnp.float32)[:, None]).astype(jnp.bfloat16)
    edge_side = jnp.dot(node_new, w_edge_in, preferred_element_type=jnp.float32).astype(
        jnp.bfloat16
    )
    return (node_new, edge_side)


def body(
    node_embed,
    rotation,
    translation,
    pair_embed,
    chain_index,
    residue_mask,
    step_index,
    w_time,
    w_query,
    w_query_points,
    w_kv,
    w_kvp,
    w_bias,
    head_weights,
    chain_bias,
    w_out,
    w_mlp_in,
    w_mlp_out,
    w_edge_in,
    w_trunk_in,
    w_trunk_mid,
    w_final,
):
    row_count = node_embed.shape[0]
    key_count = pair_embed.shape[1]
    row_start = lax.axis_index("row") * row_count
    key_start = lax.axis_index("col") * key_count
    embedded = (
        node_embed.astype(jnp.float32)
        + jnp.dot(time_embedding(step_index, CS), w_time, preferred_element_type=jnp.float32)
    ).astype(jnp.bfloat16)
    embedded = lax.optimization_barrier(embedded)
    rot_rows = lax.dynamic_slice_in_dim(rotation, row_start, row_count, 2)
    shift_rows = lax.dynamic_slice_in_dim(translation, row_start, row_count, 1)
    mask_rows = lax.dynamic_slice_in_dim(residue_mask, row_start, row_count, 0)
    mask_keys = lax.dynamic_slice_in_dim(residue_mask, key_start, key_count, 0)
    chain_rows = lax.dynamic_slice_in_dim(chain_index, row_start, row_count, 0)
    chain_keys = lax.dynamic_slice_in_dim(chain_index, key_start, key_count, 0)
    query_feat = (
        jnp.dot(embedded, w_query, preferred_element_type=jnp.float32)
        .astype(jnp.bfloat16)
        .reshape(row_count, HEADS, CH)
    )
    query_pts = to_global(
        rot_rows,
        shift_rows,
        jnp.dot(embedded, w_query_points, preferred_element_type=jnp.float32).reshape(
            row_count, 3, HEADS * QP
        ),
    ).reshape(row_count, 3, HEADS, QP)
    all_nodes = lax.all_gather(embedded, "row", axis=0, tiled=True)
    key_nodes = lax.dynamic_slice_in_dim(all_nodes, key_start, key_count, 0)
    rot_keys = lax.dynamic_slice_in_dim(rotation, key_start, key_count, 2)
    shift_keys = lax.dynamic_slice_in_dim(translation, key_start, key_count, 1)
    key_values, key_points = project_keys(key_nodes, rot_keys, shift_keys, w_kv, w_kvp)
    key_feat = key_values[:, : HEADS * CH].reshape(key_count, HEADS, CH)
    value_feat = key_values[:, HEADS * CH :].reshape(key_count, HEADS, CH)
    key_points = key_points.reshape(key_count, 3, HEADS, QP + VP)
    key_pts = key_points[..., :QP]
    value_pts = key_points[..., QP:]
    scaled = math.sqrt(1.0 / 3.0)
    point_weight = math.sqrt(2.0 / (9.0 * QP))
    point_gain = jax.nn.softplus(head_weights)
    feature_dots = jnp.einsum(
        "ihc,jhc->hij", query_feat, key_feat, preferred_element_type=jnp.float32
    ) / math.sqrt(CH)
    pair_bias = jnp.einsum("ijc,ch->hij", pair_embed, w_bias, preferred_element_type=jnp.float32)
    same_chain = (chain_rows[:, None] == chain_keys[None, :]).astype(jnp.float32)
    query_square = jnp.einsum("iahp,iahp->hi", query_pts, query_pts, precision=highest)
    key_square = jnp.einsum("jahp,jahp->hj", key_pts, key_pts, precision=highest)
    cross_term = jnp.einsum("iahp,jahp->hij", query_pts, key_pts, precision=highest)
    distance = query_square[:, :, None] + key_square[:, None, :] - 2.0 * cross_term
    mask_term = (mask_keys.astype(jnp.float32) - 1.0) * masked_score
    scores = (
        scaled * (feature_dots + pair_bias + chain_bias[:, None, None] * same_chain[None])
        - scaled * point_weight * 0.5 * point_gain[:, None, None] * distance
        + mask_term[None, None, :]
    )
    row_peak = lax.pmax(jnp.max(scores, -1), "col")
    weights = jnp.exp(scores - row_peak[:, :, None])
    denominator = jnp.transpose(jnp.sum(weights, -1))
    rounded = weights.astype(jnp.bfloat16)
    values_out = jnp.einsum(
        "hij,jhc->ihc", rounded, value_feat, preferred_element_type=jnp.float32
    ).reshape(row_count, -1)
    points_out = jnp.einsum("hij,jahv->iahv", weights, value_pts, precision=highest).reshape(
        row_count, -1
    )
    pair_sums = jnp.einsum(
        "hij,ijc->ihc", rounded, pair_embed, preferred_element_type=jnp.float32
    ).reshape(row_count, -1)
    summed = lax.psum((denominator, values_out, points_out, pair_sums), "col")
    node_out, edge_side = node_finish(
        summed[0],
        summed[1],
        summed[2],
        summed[3],
        embedded,
        rot_rows,
        shift_rows,
        mask_rows,
        w_out,
        w_mlp_in,
        w_mlp_out,
        w_edge_in,
    )
    side_all = lax.all_gather(edge_side, "row", axis=0, tiled=True)
    side_rows = lax.dynamic_slice_in_dim(side_all, row_start, row_count, 0)
    side_keys = lax.dynamic_slice_in_dim(side_all, key_start, key_count, 0)
    pre_rows = jnp.dot(side_rows, w_trunk_in[CZ : CZ + NH], preferred_element_type=jnp.float32)
    pre_keys = jnp.dot(side_keys, w_trunk_in[CZ + NH :], preferred_element_type=jnp.float32)
    mask_key_f = mask_keys.astype(jnp.float32)
    block_rows = math.gcd(row_count, 8)
    block_count = row_count // block_rows

    def edge_block(inputs):
        pair_block, pre_block, side_block, keep_block = inputs
        lifted = (
            jnp.einsum(
                "ijc,cd->ijd", pair_block, w_trunk_in[:CZ], preferred_element_type=jnp.float32
            )
            + pre_block[:, None, :]
            + pre_keys[None, :, :]
        )
        hidden_one = jax.nn.relu(lifted).astype(jnp.bfloat16)
        hidden_two = jax.nn.relu(
            jnp.einsum("ijd,de->ije", hidden_one, w_trunk_mid, preferred_element_type=jnp.float32)
        )
        stacked = jnp.concatenate(
            [
                pair_block,
                jnp.broadcast_to(side_block[:, None, :], (block_rows, key_count, NH)),
                jnp.broadcast_to(side_keys[None, :, :], (block_rows, key_count, NH)),
            ],
            -1,
        )
        joined = (hidden_two + stacked.astype(jnp.float32)).astype(jnp.bfloat16)
        edge_out = jnp.einsum("ijd,dc->ijc", joined, w_final, preferred_element_type=jnp.float32)
        pair_keep = keep_block.astype(jnp.float32)[:, None] * mask_key_f[None, :]
        return (layer_norm(edge_out) * pair_keep[:, :, None]).astype(jnp.bfloat16)

    pair_out = lax.map(
        edge_block,
        (
            pair_embed.reshape(block_count, block_rows, key_count, CZ),
            pre_rows.reshape(block_count, block_rows, HID),
            side_rows.reshape(block_count, block_rows, NH),
            mask_rows.reshape(block_count, block_rows),
        ),
    )
    return (node_out, pair_out.reshape(row_count, key_count, CZ))


PAD = 64
GAIN = math.sqrt(1.0 / 3.0)
POINT = math.sqrt(2.0 / (9.0 * QP))
f32 = jnp.float32
bf16 = jnp.bfloat16


def dot(a, b, dims=((1,), (0,)), precision=None):
    return lax.dot_general(a, b, (dims, ((), ())), precision=precision, preferred_element_type=f32)


NT = ((1,), (1,))
TN = ((0,), (0,))


def params(mib):
    return pltpu.CompilerParams(vmem_limit_bytes=mib * 1024 * 1024)


def vmem(count):
    return [pl.BlockSpec(memory_space=pltpu.VMEM)] * count


def stay(*arrays):
    return [pltpu.with_memory_space_constraint(array, pltpu.HBM) for array in arrays]


def bias_kernel(pair_hbm, w_hbm, out_ref, pair_ref, w_ref, sems):
    copies = [pltpu.make_async_copy(pair_hbm, pair_ref, sems.at[0]), pltpu.make_async_copy(w_hbm, w_ref, sems.at[1])]
    for copy in copies:
        copy.start()
    for copy in copies:
        copy.wait()
    half = pair_ref.shape[0] // 2
    keys = pair_ref.shape[1]
    weight = w_ref[...]
    gap = jnp.zeros((PAD - keys, CZ), bf16)
    for i in range(half):
        both = jnp.concatenate([pair_ref[i], gap, pair_ref[i + half], gap], 0)
        out_ref[pl.ds(i, HEADS, stride=half), :] = dot(weight, both, NT) * GAIN


def one_hot(shape, source_dim, offset_of):
    src = lax.broadcasted_iota(jnp.int32, shape, source_dim)
    dst = lax.broadcasted_iota(jnp.int32, shape, 1 - source_dim)
    return (src == offset_of(dst)).astype(f32)


def prepare_kernel(
    step_ref, hw_hbm, rotation_hbm, shift_hbm, mask_hbm, chain_hbm, node_hbm, w_time_hbm, w_query_hbm, w_qp_hbm, w_kv_hbm,
    w_kvp_hbm, w_out_hbm,
    time_ref, own_ref, qk_ref, qpts_ref, w_mix_ref, w_pts_ref, kfeat_ref, rows_ref, keys_ref,
    hw_ref, rotation_ref, shift_ref, mask_ref, chain_ref, node_ref, w_time_ref, w_query_ref, w_qp_ref, w_kv_ref,
    w_kvp_ref, w_head_ref, feats_ref, sems,
):
    pairs = (
        (rotation_hbm, rotation_ref), (shift_hbm, shift_ref), (mask_hbm, mask_ref),
        (chain_hbm, chain_ref), (node_hbm, node_ref), (w_time_hbm, w_time_ref), (hw_hbm, hw_ref), (w_qp_hbm, w_qp_ref),
        (w_kvp_hbm, w_kvp_ref), (w_query_hbm, w_query_ref), (w_kv_hbm, w_kv_ref),
        (w_out_hbm.at[pl.ds(0, HEADS * CH)], w_head_ref),
    )
    copies = [pltpu.make_async_copy(src, dst, sems.at[n]) for n, (src, dst) in enumerate(pairs)]
    for copy in copies:
        copy.start()
    for copy in copies[:9]:
        copy.wait()
    rows = node_ref.shape[0]
    half = CS // 2
    row = lax.axis_index("row")
    col = lax.axis_index("col")
    feats_ref[...] = jnp.zeros(feats_ref.shape, f32)
    for a in range(3):
        feats_ref[3 * a : 3 * a + 3, :] = rotation_ref[a]
    feats_ref[9:12, :] = shift_ref[...]
    feats_ref[12:13, :] = mask_ref[...].astype(f32)
    feats_ref[13:14, :] = chain_ref[...].astype(f32)
    total = feats_ref.shape[1]
    lane = lax.broadcasted_iota(jnp.int32, (8, half), 1).astype(f32)
    frequency = jnp.exp(-math.log(10000.0) * lane / half)
    angles = step_ref[0].astype(f32) * frequency
    temb = jnp.concatenate([jnp.sin(angles), jnp.cos(angles)], 1).astype(bf16)
    time = dot(temb, w_time_ref[...])
    time_ref[...] = time
    own = (node_ref[...].astype(f32) + time[0:1]).astype(bf16)
    own_ref[...] = own
    feats = feats_ref[...]

    def key_of(dst):
        part = dst // PAD
        inside = dst - part * PAD
        return jnp.where(inside < rows, (part ^ col) * rows + inside, -1)

    kfeat_ref[...] = dot(feats, one_hot((total, 4 * PAD), 0, key_of), precision=highest)
    own_cols = dot(one_hot((rows, total), 1, lambda d: d + row * rows), feats, NT, precision=highest)
    rows_ref[...] = own_cols
    keys_ref[...] = dot(one_hot((rows, total), 1, lambda d: d + col * rows), feats, NT, precision=highest)
    for copy in copies[9:]:
        copy.wait()
    query = dot(own, w_query_ref[...]).astype(bf16)
    for h in range(HEADS):
        taken = dot(query[:, h * CH : (h + 1) * CH], w_kv_ref[:, h * CH : (h + 1) * CH], NT)
        qk_ref[h * rows : (h + 1) * rows, :] = (taken * (GAIN / math.sqrt(CH))).astype(bf16)
        w_mix_ref[h * CH : (h + 1) * CH, :] = dot(
            w_kv_ref[:, (HEADS + h) * CH : (HEADS + h + 1) * CH], w_head_ref[h * CH : (h + 1) * CH, :]
        ).astype(bf16)
    wide = HEADS * QP
    local = dot(own, w_qp_ref[...], NT)
    parts = [local[:, b * wide : (b + 1) * wide] for b in range(3)]
    points = []
    for a in range(3):
        turned = own_cols[:, 9 + a : 10 + a]
        for b in range(3):
            turned = turned + own_cols[:, 3 * a + b : 3 * a + b + 1] * parts[b]
        points.append(turned)
    points = jnp.concatenate(points + [jnp.zeros((rows, wide), f32)], 1)
    lanes = lax.broadcasted_iota(jnp.int32, (1, 4 * wide), 1)
    head_lane = lax.broadcasted_iota(jnp.int32, (1, 128), 1)
    hw = jnp.zeros((1, 128), f32)
    for h in range(HEADS):
        hw = jnp.where(head_lane == h, hw_ref[h], hw)
    gains = GAIN * POINT * 0.5 * (jnp.maximum(hw, 0.0) + jnp.log1p(jnp.exp(-jnp.abs(hw))))
    rows_ref[...] = own_cols
    for h in range(HEADS):
        gain = gains[:, h : h + 1]
        mine = jnp.where((lanes % wide) // QP == h, points, 0.0)
        square = jnp.sum(mine * mine, 1, keepdims=True)
        qpts_ref[h * rows : (h + 1) * rows, :] = jnp.where(lanes == 3 * wide, -square, 2.0 * mine) * gain
    width = w_kvp_ref.shape[0]
    group = HEADS * (QP + VP)
    dst = lax.broadcasted_iota(jnp.int32, (width, width), 0)
    src = lax.broadcasted_iota(jnp.int32, (width, width), 1)
    comp = dst // group
    inside = dst - comp * group
    value = inside - HEADS * QP
    from_key = (inside // QP) * (QP + VP) + inside % QP
    from_value = (value // VP) * (QP + VP) + QP + value % VP
    wanted = comp * group + jnp.where(inside < HEADS * QP, from_key, from_value)
    order = (src == wanted).astype(f32).astype(bf16)
    w_pts_ref[...] = dot(order, w_kvp_ref[...]).astype(bf16)


def attention_kernel(
    hw_ref, cb_ref, own_ref, n1_ref, n2_ref, n3_ref, time_ref, qk_ref, qpts_ref, w_mix_ref, w_pts_ref, kfeat_ref,
    rows_ref, b0_ref, b1_ref, b2_ref, b3_ref, pair_ref, w_out_ref,
    out_ref, x_ref, prob_ref, near_ref, opair_ref,
):
    rows = own_ref.shape[0]
    half = rows // 2
    row = lax.axis_index("row")
    col = lax.axis_index("col")
    tail = HEADS * CH
    time = time_ref[0:1]
    x_ref[...] = jnp.zeros(x_ref.shape, bf16)
    x_ref[pl.ds(pl.multiple_of((col ^ row) * PAD, PAD), rows), :] = own_ref[...]
    for k, ref in ((1, n1_ref), (2, n2_ref), (3, n3_ref)):
        place = col ^ ((row + 4 - k) % 4)
        x_ref[pl.ds(pl.multiple_of(place * PAD, PAD), rows), :] = (ref[...].astype(f32) + time).astype(bf16)
    x = x_ref[...]
    keys = x.shape[0]
    kfeat = kfeat_ref[...]
    group = HEADS * (QP + VP)
    wide = HEADS * QP
    local = dot(w_pts_ref[...], x, NT)
    points = []
    for a in range(3):
        turned = kfeat[9 + a : 10 + a]
        for b in range(3):
            turned = turned + kfeat[3 * a + b : 3 * a + b + 1] * local[b * group : (b + 1) * group]
        points.append(turned)
    key_points = [p[:wide] for p in points]
    cross = dot(qpts_ref[...], jnp.concatenate(key_points + [jnp.ones((wide, keys), f32)], 0), precision=highest)
    key_square = key_points[0] * key_points[0] + key_points[1] * key_points[1] + key_points[2] * key_points[2]
    feature = dot(qk_ref[...], x, NT)
    lane = lax.broadcasted_iota(jnp.int32, (1, 128), 1)
    low = lane < PAD
    bias_low, bias_high = [], []
    for left, right in ((b0_ref, b1_ref), (b2_ref, b3_ref)):
        left, right = left[...], right[...]
        bias_low.append(jnp.where(low, left, pltpu.roll(right, PAD, 1)))
        bias_high.append(jnp.where(low, pltpu.roll(left, PAD, 1), right))
    bias_low = jnp.concatenate(bias_low, 1)
    bias_high = jnp.concatenate(bias_high, 1)
    key_lane = lax.broadcasted_iota(jnp.int32, (1, keys), 1)
    blocked = jnp.where(key_lane % PAD < rows, (kfeat[12:13] - 1.0) * masked_score, -1e30)
    own_cols = rows_ref[...]
    same = (own_cols[:, 13:14] == kfeat[13:14]).astype(f32)
    hw = jnp.zeros((1, 128), f32)
    for h in range(HEADS):
        hw = jnp.where(lane == h, hw_ref[h], hw)
    gains = GAIN * POINT * 0.5 * (jnp.maximum(hw, 0.0) + jnp.log1p(jnp.exp(-jnp.abs(hw))))
    for h in range(HEADS):
        at = slice(h * rows, (h + 1) * rows)
        square = jnp.sum(key_square[h * QP : (h + 1) * QP], 0, keepdims=True)
        bias = jnp.concatenate([bias_low[h * half : (h + 1) * half], bias_high[h * half : (h + 1) * half]], 0)
        score = (
            feature[at] + bias + (GAIN * cb_ref[h]) * same + cross[at] + (blocked - gains[:, h : h + 1] * square)
        )
        peak = jnp.max(score, 1, keepdims=True)
        weight = jnp.exp(score - peak)
        weight = weight / jnp.sum(weight, 1, keepdims=True)
        prob_ref[at, :] = weight
        near_ref[at, :] = weight[:, :128]
    prob = prob_ref[...]
    prob_low = prob.astype(bf16)
    mixed = dot(prob_low, x).astype(bf16)
    mixed = jnp.concatenate([mixed[h * rows : (h + 1) * rows] for h in range(HEADS)], 1)
    update = dot(mixed, w_mix_ref[...])
    empty = jnp.zeros((128 - HEADS * VP, keys), f32)
    value_points = jnp.concatenate([x for p in points for x in (p[wide:], empty)], 0)
    gathered = dot(prob, value_points, NT, precision=highest)
    spread = lax.broadcasted_iota(jnp.int32, (1, 3 * 128), 1) % 128 // VP
    kept = jnp.zeros((rows, 3 * 128), f32)
    for h in range(HEADS):
        kept = jnp.where(spread == h, gathered[h * rows : (h + 1) * rows], kept)
    relative = [kept[:, a * 128 : (a + 1) * 128] - own_cols[:, 9 + a : 10 + a] for a in range(3)]
    framed = []
    for b in range(3):
        framed.append(
            own_cols[:, b : b + 1] * relative[0]
            + own_cols[:, 3 + b : 4 + b] * relative[1]
            + own_cols[:, 6 + b : 7 + b] * relative[2]
        )
    length = jnp.sqrt(jnp.maximum(framed[0] * framed[0] + framed[1] * framed[1] + framed[2] * framed[2], 1.0))
    own_keys = pair_ref.shape[1]
    for i in range(rows):
        weight = near_ref[pl.ds(i, HEADS, stride=rows), :][:, :own_keys].astype(bf16)
        opair_ref[pl.ds(i, HEADS, stride=rows), :] = dot(weight, pair_ref[i])
    span = HEADS * VP
    for n, part in enumerate(framed + [length]):
        update = update + dot(part[:, :span].astype(bf16), w_out_ref[tail + n * span : tail + (n + 1) * span])
    paired = jnp.concatenate([opair_ref[h * rows : (h + 1) * rows, :] for h in range(HEADS)], 1).astype(bf16)
    out_ref[...] = (0.25 * update + dot(paired, w_out_ref[tail + 4 * span :])).astype(out_ref.dtype)


def node_kernel(u0_ref, u1_ref, u2_ref, u3_ref, own_ref, rows_ref, w_in_ref, w_back_ref, w_edge_ref, node_ref, side_ref):
    update = (u0_ref[...].astype(f32) + u1_ref[...].astype(f32)) + (u2_ref[...].astype(f32) + u3_ref[...].astype(f32))
    normed = layer_norm(own_ref[...].astype(f32) + update).astype(bf16)
    middle = jnp.maximum(dot(normed, w_in_ref[...]), 0.0).astype(bf16)
    node = layer_norm(normed.astype(f32) + dot(middle, w_back_ref[...]))
    node = (node * rows_ref[:, 12:13]).astype(bf16)
    node_ref[...] = node
    side_ref[...] = dot(node, w_edge_ref[...]).astype(bf16)


def edge_kernel(side_ref, other_ref, rows_ref, keys_ref, pair_ref, w_in_ref, w_mid_ref, w_final_ref, out_ref):
    rows, keys = pair_ref.shape[:2]
    step = 8
    w_in = w_in_ref[...]
    side = side_ref[...]
    other = other_ref[...]
    pre_rows = dot(side, w_in[CZ : CZ + NH])
    pre_keys = dot(other, w_in[CZ + NH :])
    side = side.astype(f32)
    other = other.astype(f32)
    keep_rows = rows_ref[:, 12:13]
    keep_keys = keys_ref[:, 12:13]
    for begin in range(0, rows, step):
        pair = pair_ref[begin : begin + step].reshape(step * keys, CZ)
        lifted = dot(pair, w_in[:CZ])
        first = jnp.concatenate(
            [
                jnp.maximum(lifted[n * keys : (n + 1) * keys] + (pre_keys + pre_rows[begin + n : begin + n + 1]), 0.0).astype(bf16)
                for n in range(step)
            ],
            0,
        )
        second = jnp.maximum(dot(first, w_mid_ref[...]), 0.0)
        stacked = jnp.concatenate(
            [
                pair.astype(f32),
                jnp.concatenate([jnp.broadcast_to(side[begin + n : begin + n + 1], (keys, NH)) for n in range(step)], 0),
                jnp.concatenate([other] * step, 0),
            ],
            1,
        )
        edge = layer_norm(dot((second + stacked).astype(bf16), w_final_ref[...]))
        for n in range(step):
            keep = keep_keys * keep_rows[begin + n : begin + n + 1]
            out_ref[begin + n] = (edge[n * keys : (n + 1) * keys] * keep).astype(bf16)


def tile_body(
    node_embed, rotation, translation, pair_embed, chain_index, residue_mask, step_index, w_time, w_query,
    w_query_points, w_kv, w_kvp, w_bias, head_weights, chain_bias, w_out, w_mlp_in, w_mlp_out, w_edge_in,
    w_trunk_in, w_trunk_mid, w_final,
):
    rows = node_embed.shape[0]
    total = residue_mask.shape[0]
    smem = pl.BlockSpec(memory_space=pltpu.SMEM)
    hbm = pl.BlockSpec(memory_space=pltpu.HBM)
    others = [lax.ppermute(node_embed, "row", [(i, (i + k) % 4) for i in range(4)]) for k in (1, 2, 3)]
    bias = pl.pallas_call(
        bias_kernel,
        out_shape=jax.ShapeDtypeStruct((HEADS * rows // 2, 2 * PAD), f32),
        in_specs=[hbm, hbm],
        out_specs=pl.BlockSpec(memory_space=pltpu.VMEM),
        scratch_shapes=[
            pltpu.VMEM(pair_embed.shape, bf16),
            pltpu.VMEM((HEADS, CZ), bf16),
            pltpu.SemaphoreType.DMA((2,)),
        ],
        compiler_params=params(16),
    )(*stay(pair_embed, w_bias.T))
    biases = [lax.ppermute(bias, "col", [(i, i ^ k) for i in range(4)]) for k in (1, 2, 3)]
    prepared = pl.pallas_call(
        prepare_kernel,
        out_shape=(
            jax.ShapeDtypeStruct((8, CS), f32),
            jax.ShapeDtypeStruct((rows, CS), bf16),
            jax.ShapeDtypeStruct((HEADS * rows, CS), bf16),
            jax.ShapeDtypeStruct((HEADS * rows, 4 * HEADS * QP), f32),
            jax.ShapeDtypeStruct((HEADS * CH, CS), bf16),
            jax.ShapeDtypeStruct((w_kvp.shape[1], CS), bf16),
            jax.ShapeDtypeStruct((16, 4 * PAD), f32),
            jax.ShapeDtypeStruct((rows, 16), f32),
            jax.ShapeDtypeStruct((rows, 16), f32),
        ),
        in_specs=[smem] + [hbm] * 12,
        out_specs=tuple(vmem(9)),
        scratch_shapes=[
            pltpu.SMEM((HEADS,), f32),
            pltpu.VMEM(rotation.shape, f32),
            pltpu.VMEM(translation.shape, f32),
            pltpu.VMEM((1, total), jnp.int32),
            pltpu.VMEM((1, total), jnp.int32),
            pltpu.VMEM(node_embed.shape, bf16),
            pltpu.VMEM(w_time.shape, bf16),
            pltpu.VMEM(w_query.shape, bf16),
            pltpu.VMEM(w_query_points.shape[::-1], bf16),
            pltpu.VMEM(w_kv.shape, bf16),
            pltpu.VMEM(w_kvp.shape[::-1], bf16),
            pltpu.VMEM((HEADS * CH, CS), bf16),
            pltpu.VMEM((16, total), f32),
            pltpu.SemaphoreType.DMA((12,)),
        ],
        compiler_params=params(24),
        cost_estimate=pl.CostEstimate(flops=2 * 10**9, bytes_accessed=8 * 10**6, transcendentals=0),
    )(
        step_index,
        *stay(
            head_weights, rotation, translation, residue_mask[None], chain_index[None], node_embed, w_time,
            w_query, w_query_points.T, w_kv, w_kvp.T, w_out,
        )
    )
    time, own, qk, qpts, w_mix, w_pts, kfeat, row_cols, key_cols = prepared
    partial = pl.pallas_call(
        attention_kernel,
        out_shape=jax.ShapeDtypeStruct((rows, CS), f32),
        in_specs=[smem, smem] + vmem(17),
        out_specs=pl.BlockSpec(memory_space=pltpu.VMEM),
        scratch_shapes=[
            pltpu.VMEM((4 * PAD, CS), bf16),
            pltpu.VMEM((HEADS * rows, 4 * PAD), f32),
            pltpu.VMEM((HEADS * rows, 2 * PAD), f32),
            pltpu.VMEM((HEADS * rows, CZ), f32),
        ],
        compiler_params=params(24),
    )(head_weights, chain_bias, own, *others, time, qk, qpts, w_mix, w_pts, kfeat, row_cols, bias, *biases, pair_embed, w_out)
    partials = [lax.ppermute(partial, "col", [(i, i ^ k) for i in range(4)]) for k in (1, 2, 3)]
    node_out, side = pl.pallas_call(
        node_kernel,
        out_shape=(jax.ShapeDtypeStruct((rows, CS), bf16), jax.ShapeDtypeStruct((rows, NH), bf16)),
        in_specs=vmem(9),
        out_specs=tuple(vmem(2)),
        compiler_params=params(16),
    )(partial, *partials, own, row_cols, w_mlp_in, w_mlp_out, w_edge_in)
    turned = [(c * 4 + r, r * 4 + c) for r in range(4) for c in range(4)]
    other = lax.ppermute(side, ("row", "col"), turned)
    pair_out = pl.pallas_call(
        edge_kernel,
        out_shape=jax.ShapeDtypeStruct(pair_embed.shape, bf16),
        in_specs=vmem(8),
        out_specs=pl.BlockSpec(memory_space=pltpu.VMEM),
        compiler_params=params(24),
    )(side, other, row_cols, key_cols, pair_embed, w_trunk_in, w_trunk_mid, w_final)
    return node_out, pair_out


def dispatch(sizes, *arrays):
    rows, keys = arrays[3].shape[:2]
    square = sizes["row"] == 4 and sizes["col"] == 4 and rows == keys and rows == 48
    return tile_body(*arrays) if square else body(*arrays)


def solution(mesh):
    return jax.shard_map(
        functools.partial(dispatch, dict(mesh.shape)),
        mesh=mesh,
        in_specs=(
            P(("groups", "row"), None),
            P(None, None, "groups"),
            P(None, "groups"),
            P(("groups", "row"), "col", None),
            P("groups"),
            P("groups"),
            P("groups"),
            P(),
            P(),
            P(),
            P(),
            P(),
            P(),
            P(),
            P(),
            P(),
            P(),
            P(),
            P(),
            P(),
            P(),
            P(),
        ),
        out_specs=(P(("groups", "row"), None), P(("groups", "row"), "col", None)),
        check_vma=False,
    )
```

```python
import functools
import math

import jax
import jax.numpy as jnp
import numpy as np
from jax import lax
from jax.experimental import pallas as pl
from jax.experimental.pallas import tpu as pltpu
from jax.sharding import PartitionSpec as P

CS = 256
CZ = 128
HEADS = 8
CH = 256
QP = 8
VP = 12
NH = 128
HID = 384


norm_epsilon = 1e-05
masked_score = 100000.0
highest = lax.Precision.HIGHEST


def layer_norm(values):
    average = jnp.mean(values, -1, keepdims=True)
    centred = values - average
    spread = jnp.mean(centred * centred, -1, keepdims=True)
    return centred * lax.rsqrt(spread + norm_epsilon)


def time_embedding(step_index, embed_width):
    half_width = embed_width // 2
    frequency = jnp.exp(-math.log(10000.0) * jnp.arange(half_width, dtype=jnp.float32) / half_width)
    angles = step_index.astype(jnp.float32)[0] * frequency
    return jnp.concatenate([jnp.sin(angles), jnp.cos(angles)])[None, :].astype(jnp.bfloat16)


def to_global(rotation, shift_vec, points):
    turned = jnp.einsum("abn,nbm->nam", rotation, points, precision=highest)
    return turned + jnp.transpose(shift_vec)[:, :, None]


def project_keys(embedded, rotation, shift_vec, w_kv, w_kvp):
    item_count = embedded.shape[0]
    key_values = jnp.dot(embedded, w_kv, preferred_element_type=jnp.float32).astype(jnp.bfloat16)
    points = jnp.dot(embedded, w_kvp, preferred_element_type=jnp.float32).reshape(item_count, 3, -1)
    return (key_values, to_global(rotation, shift_vec, points))


def node_finish(
    denominator,
    values_out,
    points_out,
    pair_sums,
    embedded,
    rotation,
    shift_vec,
    mask_rows,
    w_out,
    w_mlp_in,
    w_mlp_out,
    w_edge_in,
):
    item_count = embedded.shape[0]
    scale_back = denominator[:, :, None]
    attended = values_out.reshape(item_count, HEADS, CH) / scale_back
    points = points_out.reshape(item_count, 3, HEADS, VP) / denominator[:, None, :, None]
    relative = points - jnp.transpose(shift_vec)[:, :, None, None]
    framed = jnp.einsum("abi,iahv->ibhv", rotation, relative, precision=highest)
    length = jnp.sqrt(jnp.maximum(jnp.sum(framed * framed, 1), 1.0))
    paired = pair_sums.reshape(item_count, HEADS, CZ) / scale_back
    features = jnp.concatenate(
        [
            attended.reshape(item_count, -1),
            framed.reshape(item_count, -1),
            length.reshape(item_count, -1),
            paired.reshape(item_count, -1),
        ],
        -1,
    ).astype(jnp.bfloat16)
    update = jnp.dot(features, w_out, preferred_element_type=jnp.float32)
    normed = layer_norm(embedded.astype(jnp.float32) + update).astype(jnp.bfloat16)
    normed = lax.optimization_barrier(normed)
    middle = jax.nn.relu(jnp.dot(normed, w_mlp_in, preferred_element_type=jnp.float32)).astype(
        jnp.bfloat16
    )
    node_new = layer_norm(
        normed.astype(jnp.float32) + jnp.dot(middle, w_mlp_out, preferred_element_type=jnp.float32)
    )
    node_new = (node_new * mask_rows.astype(jnp.float32)[:, None]).astype(jnp.bfloat16)
    edge_side = jnp.dot(node_new, w_edge_in, preferred_element_type=jnp.float32).astype(
        jnp.bfloat16
    )
    return (node_new, edge_side)


def body(
    node_embed,
    rotation,
    translation,
    pair_embed,
    chain_index,
    residue_mask,
    step_index,
    w_time,
    w_query,
    w_query_points,
    w_kv,
    w_kvp,
    w_bias,
    head_weights,
    chain_bias,
    w_out,
    w_mlp_in,
    w_mlp_out,
    w_edge_in,
    w_trunk_in,
    w_trunk_mid,
    w_final,
):
    row_count = node_embed.shape[0]
    key_count = pair_embed.shape[1]
    row_start = lax.axis_index("row") * row_count
    key_start = lax.axis_index("col") * key_count
    embedded = (
        node_embed.astype(jnp.float32)
        + jnp.dot(time_embedding(step_index, CS), w_time, preferred_element_type=jnp.float32)
    ).astype(jnp.bfloat16)
    embedded = lax.optimization_barrier(embedded)
    rot_rows = lax.dynamic_slice_in_dim(rotation, row_start, row_count, 2)
    shift_rows = lax.dynamic_slice_in_dim(translation, row_start, row_count, 1)
    mask_rows = lax.dynamic_slice_in_dim(residue_mask, row_start, row_count, 0)
    mask_keys = lax.dynamic_slice_in_dim(residue_mask, key_start, key_count, 0)
    chain_rows = lax.dynamic_slice_in_dim(chain_index, row_start, row_count, 0)
    chain_keys = lax.dynamic_slice_in_dim(chain_index, key_start, key_count, 0)
    query_feat = (
        jnp.dot(embedded, w_query, preferred_element_type=jnp.float32)
        .astype(jnp.bfloat16)
        .reshape(row_count, HEADS, CH)
    )
    query_pts = to_global(
        rot_rows,
        shift_rows,
        jnp.dot(embedded, w_query_points, preferred_element_type=jnp.float32).reshape(
            row_count, 3, HEADS * QP
        ),
    ).reshape(row_count, 3, HEADS, QP)
    all_nodes = lax.all_gather(embedded, "row", axis=0, tiled=True)
    key_nodes = lax.dynamic_slice_in_dim(all_nodes, key_start, key_count, 0)
    rot_keys = lax.dynamic_slice_in_dim(rotation, key_start, key_count, 2)
    shift_keys = lax.dynamic_slice_in_dim(translation, key_start, key_count, 1)
    key_values, key_points = project_keys(key_nodes, rot_keys, shift_keys, w_kv, w_kvp)
    key_feat = key_values[:, : HEADS * CH].reshape(key_count, HEADS, CH)
    value_feat = key_values[:, HEADS * CH :].reshape(key_count, HEADS, CH)
    key_points = key_points.reshape(key_count, 3, HEADS, QP + VP)
    key_pts = key_points[..., :QP]
    value_pts = key_points[..., QP:]
    scaled = math.sqrt(1.0 / 3.0)
    point_weight = math.sqrt(2.0 / (9.0 * QP))
    point_gain = jax.nn.softplus(head_weights)
    feature_dots = jnp.einsum(
        "ihc,jhc->hij", query_feat, key_feat, preferred_element_type=jnp.float32
    ) / math.sqrt(CH)
    pair_bias = jnp.einsum("ijc,ch->hij", pair_embed, w_bias, preferred_element_type=jnp.float32)
    same_chain = (chain_rows[:, None] == chain_keys[None, :]).astype(jnp.float32)
    query_square = jnp.einsum("iahp,iahp->hi", query_pts, query_pts, precision=highest)
    key_square = jnp.einsum("jahp,jahp->hj", key_pts, key_pts, precision=highest)
    cross_term = jnp.einsum("iahp,jahp->hij", query_pts, key_pts, precision=highest)
    distance = query_square[:, :, None] + key_square[:, None, :] - 2.0 * cross_term
    mask_term = (mask_keys.astype(jnp.float32) - 1.0) * masked_score
    scores = (
        scaled * (feature_dots + pair_bias + chain_bias[:, None, None] * same_chain[None])
        - scaled * point_weight * 0.5 * point_gain[:, None, None] * distance
        + mask_term[None, None, :]
    )
    row_peak = lax.pmax(jnp.max(scores, -1), "col")
    weights = jnp.exp(scores - row_peak[:, :, None])
    denominator = jnp.transpose(jnp.sum(weights, -1))
    rounded = weights.astype(jnp.bfloat16)
    values_out = jnp.einsum(
        "hij,jhc->ihc", rounded, value_feat, preferred_element_type=jnp.float32
    ).reshape(row_count, -1)
    points_out = jnp.einsum("hij,jahv->iahv", weights, value_pts, precision=highest).reshape(
        row_count, -1
    )
    pair_sums = jnp.einsum(
        "hij,ijc->ihc", rounded, pair_embed, preferred_element_type=jnp.float32
    ).reshape(row_count, -1)
    summed = lax.psum((denominator, values_out, points_out, pair_sums), "col")
    node_out, edge_side = node_finish(
        summed[0],
        summed[1],
        summed[2],
        summed[3],
        embedded,
        rot_rows,
        shift_rows,
        mask_rows,
        w_out,
        w_mlp_in,
        w_mlp_out,
        w_edge_in,
    )
    side_all = lax.all_gather(edge_side, "row", axis=0, tiled=True)
    side_rows = lax.dynamic_slice_in_dim(side_all, row_start, row_count, 0)
    side_keys = lax.dynamic_slice_in_dim(side_all, key_start, key_count, 0)
    pre_rows = jnp.dot(side_rows, w_trunk_in[CZ : CZ + NH], preferred_element_type=jnp.float32)
    pre_keys = jnp.dot(side_keys, w_trunk_in[CZ + NH :], preferred_element_type=jnp.float32)
    mask_key_f = mask_keys.astype(jnp.float32)
    block_rows = math.gcd(row_count, 8)
    block_count = row_count // block_rows

    def edge_block(inputs):
        pair_block, pre_block, side_block, keep_block = inputs
        lifted = (
            jnp.einsum(
                "ijc,cd->ijd", pair_block, w_trunk_in[:CZ], preferred_element_type=jnp.float32
            )
            + pre_block[:, None, :]
            + pre_keys[None, :, :]
        )
        hidden_one = jax.nn.relu(lifted).astype(jnp.bfloat16)
        hidden_two = jax.nn.relu(
            jnp.einsum("ijd,de->ije", hidden_one, w_trunk_mid, preferred_element_type=jnp.float32)
        )
        stacked = jnp.concatenate(
            [
                pair_block,
                jnp.broadcast_to(side_block[:, None, :], (block_rows, key_count, NH)),
                jnp.broadcast_to(side_keys[None, :, :], (block_rows, key_count, NH)),
            ],
            -1,
        )
        joined = (hidden_two + stacked.astype(jnp.float32)).astype(jnp.bfloat16)
        edge_out = jnp.einsum("ijd,dc->ijc", joined, w_final, preferred_element_type=jnp.float32)
        pair_keep = keep_block.astype(jnp.float32)[:, None] * mask_key_f[None, :]
        return (layer_norm(edge_out) * pair_keep[:, :, None]).astype(jnp.bfloat16)

    pair_out = lax.map(
        edge_block,
        (
            pair_embed.reshape(block_count, block_rows, key_count, CZ),
            pre_rows.reshape(block_count, block_rows, HID),
            side_rows.reshape(block_count, block_rows, NH),
            mask_rows.reshape(block_count, block_rows),
        ),
    )
    return (node_out, pair_out.reshape(row_count, key_count, CZ))


PAD = 64
GAIN = math.sqrt(1.0 / 3.0)
POINT = math.sqrt(2.0 / (9.0 * QP))
f32 = jnp.float32
bf16 = jnp.bfloat16


def dot(a, b, dims=((1,), (0,)), precision=None):
    return lax.dot_general(a, b, (dims, ((), ())), precision=precision, preferred_element_type=f32)


NT = ((1,), (1,))
TN = ((0,), (0,))


def params(mib):
    return pltpu.CompilerParams(vmem_limit_bytes=mib * 1024 * 1024)


def vmem(count):
    return [pl.BlockSpec(memory_space=pltpu.VMEM)] * count


def stay(*arrays):
    return [pltpu.with_memory_space_constraint(array, pltpu.HBM) for array in arrays]


def bias_kernel(pair_hbm, w_hbm, out_ref, pair_ref, w_ref, sems):
    half = pair_ref.shape[0] // 2
    part = half // 3
    copies = [pltpu.make_async_copy(w_hbm, w_ref, sems.at[6])]
    for n in range(3):
        for m in range(2):
            at = pl.ds(m * half + n * part, part)
            copies.append(pltpu.make_async_copy(pair_hbm.at[at], pair_ref.at[at], sems.at[2 * n + m]))
    for copy in copies:
        copy.start()
    copies[0].wait()
    keys = pair_ref.shape[1]
    weight = w_ref[...]
    gap = jnp.zeros((PAD - keys, CZ), bf16)
    for i in range(half):
        if i % part == 0:
            copies[1 + 2 * (i // part)].wait()
            copies[2 + 2 * (i // part)].wait()
        both = jnp.concatenate([pair_ref[i], gap, pair_ref[i + half], gap], 0)
        out_ref[pl.ds(i, HEADS, stride=half), :] = dot(weight, both, NT) * GAIN


def one_hot(shape, source_dim, offset_of):
    src = lax.broadcasted_iota(jnp.int32, shape, source_dim)
    dst = lax.broadcasted_iota(jnp.int32, shape, 1 - source_dim)
    return (src == offset_of(dst)).astype(f32)


def prepare_kernel(
    step_ref, hw_hbm, rotation_hbm, shift_hbm, mask_hbm, chain_hbm, node_hbm, w_time_hbm, w_query_hbm, w_qp_hbm, w_kv_hbm,
    w_kvp_hbm, order_hbm,
    time_ref, own_ref, qk_ref, qpts_ref, w_pts_ref, kfeat_ref, rows_ref, keys_ref,
    hw_ref, rotation_ref, shift_ref, mask_ref, chain_ref, node_ref, w_time_ref, w_query_ref, w_qp_ref, w_kv_ref,
    w_kvp_ref, order_ref, feats_ref, sems,
):
    pairs = (
        (rotation_hbm, rotation_ref), (shift_hbm, shift_ref), (mask_hbm, mask_ref),
        (chain_hbm, chain_ref), (node_hbm, node_ref), (w_time_hbm, w_time_ref), (hw_hbm, hw_ref), (w_qp_hbm, w_qp_ref),
        (w_kvp_hbm, w_kvp_ref), (order_hbm, order_ref), (w_query_hbm, w_query_ref), (w_kv_hbm.at[:, pl.ds(0, HEADS * CH)], w_kv_ref),
    )
    copies = [pltpu.make_async_copy(src, dst, sems.at[n]) for n, (src, dst) in enumerate(pairs)]
    for copy in copies:
        copy.start()
    for copy in copies[:10]:
        copy.wait()
    rows = node_ref.shape[0]
    half = CS // 2
    row = lax.axis_index("row")
    col = lax.axis_index("col")
    feats_ref[...] = jnp.zeros(feats_ref.shape, f32)
    for a in range(3):
        feats_ref[3 * a : 3 * a + 3, :] = rotation_ref[a]
    feats_ref[9:12, :] = shift_ref[...]
    feats_ref[12:13, :] = mask_ref[...].astype(f32)
    feats_ref[13:14, :] = chain_ref[...].astype(f32)
    total = feats_ref.shape[1]
    lane = lax.broadcasted_iota(jnp.int32, (8, half), 1).astype(f32)
    frequency = jnp.exp(-math.log(10000.0) * lane / half)
    angles = step_ref[0].astype(f32) * frequency
    temb = jnp.concatenate([jnp.sin(angles), jnp.cos(angles)], 1).astype(bf16)
    time = dot(temb, w_time_ref[...])
    time_ref[...] = time
    own = (node_ref[...].astype(f32) + time[0:1]).astype(bf16)
    own_ref[...] = own
    feats = feats_ref[...]

    def key_of(dst):
        part = dst // PAD
        inside = dst - part * PAD
        return jnp.where(inside < rows, part * rows + inside, -1)

    kfeat_ref[...] = dot(feats, one_hot((total, 4 * PAD), 0, key_of), precision=highest)
    own_cols = dot(one_hot((rows, total), 1, lambda d: d + row * rows), feats, NT, precision=highest)
    rows_ref[...] = own_cols
    keys_ref[...] = dot(one_hot((rows, total), 1, lambda d: d + col * rows), feats, NT, precision=highest)
    wide = HEADS * QP
    local = dot(own, w_qp_ref[...], NT)
    parts = [local[:, b * wide : (b + 1) * wide] for b in range(3)]
    points = []
    for a in range(3):
        turned = own_cols[:, 9 + a : 10 + a]
        for b in range(3):
            turned = turned + own_cols[:, 3 * a + b : 3 * a + b + 1] * parts[b]
        points.append(turned)
    points = jnp.concatenate(points + [jnp.zeros((rows, wide), f32)], 1)
    lanes = lax.broadcasted_iota(jnp.int32, (1, 4 * wide), 1)
    head_lane = lax.broadcasted_iota(jnp.int32, (1, 128), 1)
    hw = jnp.zeros((1, 128), f32)
    for h in range(HEADS):
        hw = jnp.where(head_lane == h, hw_ref[h], hw)
    gains = GAIN * POINT * 0.5 * (jnp.maximum(hw, 0.0) + jnp.log1p(jnp.exp(-jnp.abs(hw))))
    rows_ref[...] = own_cols
    for h in range(HEADS):
        gain = gains[:, h : h + 1]
        mine = jnp.where((lanes % wide) // QP == h, points, 0.0)
        square = jnp.sum(mine * mine, 1, keepdims=True)
        qpts_ref[h * rows : (h + 1) * rows, :] = jnp.where(lanes == 3 * wide, -square, 2.0 * mine) * gain
    group = HEADS * (QP + VP)
    for a in range(3):
        at = slice(a * group, (a + 1) * group)
        w_pts_ref[at, :] = dot(order_ref[...], w_kvp_ref[at, :]).astype(bf16)
    for copy in copies[10:]:
        copy.wait()
    query = dot(own, w_query_ref[...]).astype(bf16)
    for h in range(HEADS):
        taken = dot(query[:, h * CH : (h + 1) * CH], w_kv_ref[:, h * CH : (h + 1) * CH], NT)
        qk_ref[h * rows : (h + 1) * rows, :] = (taken * (GAIN / math.sqrt(CH))).astype(bf16)


def score_kernel(
    hw_ref, cb_ref, own_ref, n1_ref, n2_ref, n3_ref, time_ref, qk_ref, qpts_ref, w_pts_ref, kfeat_ref, rows_ref,
    b0_ref, b1_ref, b2_ref, b3_ref, pair_ref, w_out_ref,
    out_ref, x_ref, prob_ref, vpts_ref, near_ref, opair_ref, bias_ref,
):
    rows = own_ref.shape[0]
    half = rows // 2
    row = lax.axis_index("row")
    col = lax.axis_index("col")
    time = time_ref[0:1]
    x_ref[...] = jnp.zeros(x_ref.shape, bf16)
    x_ref[pl.ds(pl.multiple_of(row * PAD, PAD), rows), :] = own_ref[...]
    for k, ref in ((1, n1_ref), (2, n2_ref), (3, n3_ref)):
        place = (row + 4 - k) % 4
        x_ref[pl.ds(pl.multiple_of(place * PAD, PAD), rows), :] = (ref[...].astype(f32) + time).astype(bf16)
    for k, ref in enumerate((b0_ref, b1_ref, b2_ref, b3_ref)):
        bias_ref[col ^ k] = ref[...]
    x = x_ref[...]
    keys = x.shape[0]
    kfeat = kfeat_ref[...]
    group = HEADS * (QP + VP)
    wide = HEADS * QP
    local = dot(w_pts_ref[...], x, NT)
    points = []
    for a in range(3):
        turned = kfeat[9 + a : 10 + a]
        for b in range(3):
            turned = turned + kfeat[3 * a + b : 3 * a + b + 1] * local[b * group : (b + 1) * group]
        points.append(turned)
    empty = jnp.zeros((128 - HEADS * VP, keys), f32)
    vpts_ref[...] = jnp.concatenate([part for p in points for part in (p[wide:], empty)], 0)
    key_points = [p[:wide] for p in points]
    cross = dot(qpts_ref[...], jnp.concatenate(key_points + [jnp.ones((wide, keys), f32)], 0), precision=highest)
    key_square = key_points[0] * key_points[0] + key_points[1] * key_points[1] + key_points[2] * key_points[2]
    feature = dot(qk_ref[...], x, NT)
    lane = lax.broadcasted_iota(jnp.int32, (1, 128), 1)
    low = lane < PAD
    bias_low, bias_high = [], []
    for n in (0, 2):
        left, right = bias_ref[n], bias_ref[n + 1]
        bias_low.append(jnp.where(low, left, pltpu.roll(right, PAD, 1)))
        bias_high.append(jnp.where(low, pltpu.roll(left, PAD, 1), right))
    bias_low = jnp.concatenate(bias_low, 1)
    bias_high = jnp.concatenate(bias_high, 1)
    key_lane = lax.broadcasted_iota(jnp.int32, (1, keys), 1)
    blocked = jnp.where(key_lane % PAD < rows, (kfeat[12:13] - 1.0) * masked_score, -1e30)
    same = (rows_ref[:, 13:14] == kfeat[13:14]).astype(f32)
    hw = jnp.zeros((1, 128), f32)
    for h in range(HEADS):
        hw = jnp.where(lane == h, hw_ref[h], hw)
    gains = GAIN * POINT * 0.5 * (jnp.maximum(hw, 0.0) + jnp.log1p(jnp.exp(-jnp.abs(hw))))
    for h in range(HEADS):
        at = slice(h * rows, (h + 1) * rows)
        square = jnp.sum(key_square[h * QP : (h + 1) * QP], 0, keepdims=True)
        bias = jnp.concatenate([bias_low[h * half : (h + 1) * half], bias_high[h * half : (h + 1) * half]], 0)
        score = (
            feature[at] + bias + (GAIN * cb_ref[h]) * same + cross[at] + (blocked - gains[:, h : h + 1] * square)
        )
        peak = jnp.max(score, 1, keepdims=True)
        weight = jnp.exp(score - peak)
        weight = weight / jnp.sum(weight, 1, keepdims=True)
        prob_ref[at, :] = weight
        side = jnp.where(col >= 2, weight[:, 128:], weight[:, :128])
        near_ref[at, :] = pltpu.roll(side, (col % 2) * PAD, 1)
    own_keys = pair_ref.shape[1]
    for i in range(rows):
        weight = near_ref[pl.ds(i, HEADS, stride=rows), :][:, :own_keys].astype(bf16)
        opair_ref[pl.ds(i, HEADS, stride=rows), :] = dot(weight, pair_ref[i])
    tail = HEADS * CH + 4 * HEADS * VP
    paired = jnp.concatenate([opair_ref[h * rows : (h + 1) * rows, :] for h in range(HEADS)], 1).astype(bf16)
    out_ref[...] = dot(paired, w_out_ref[tail:]).astype(out_ref.dtype)


def value_kernel(x_ref, prob_ref, vpts_ref, own_ref, rows_ref, w_kv_ref, w_out_ref, out_ref):
    rows = own_ref.shape[0]
    tail = HEADS * CH
    own_cols = rows_ref[...]
    prob = prob_ref[...]
    mixed = dot(prob.astype(bf16), x_ref[...]).astype(bf16)
    attended = jnp.concatenate(
        [
            dot(mixed[h * rows : (h + 1) * rows], w_kv_ref[:, tail + h * CH : tail + (h + 1) * CH]).astype(bf16)
            for h in range(HEADS)
        ],
        1,
    )
    update = own_ref[...].astype(f32) + dot(attended, w_out_ref[:tail])
    gathered = dot(prob, vpts_ref[...], NT, precision=highest)
    spread = lax.broadcasted_iota(jnp.int32, (1, 3 * 128), 1) % 128 // VP
    kept = jnp.zeros((rows, 3 * 128), f32)
    for h in range(HEADS):
        kept = jnp.where(spread == h, gathered[h * rows : (h + 1) * rows], kept)
    relative = [kept[:, a * 128 : (a + 1) * 128] - own_cols[:, 9 + a : 10 + a] for a in range(3)]
    framed = []
    for b in range(3):
        framed.append(
            own_cols[:, b : b + 1] * relative[0]
            + own_cols[:, 3 + b : 4 + b] * relative[1]
            + own_cols[:, 6 + b : 7 + b] * relative[2]
        )
    length = jnp.sqrt(jnp.maximum(framed[0] * framed[0] + framed[1] * framed[1] + framed[2] * framed[2], 1.0))
    span = HEADS * VP
    for n, part in enumerate(framed + [length]):
        update = update + dot(part[:, :span].astype(bf16), w_out_ref[tail + n * span : tail + (n + 1) * span])
    out_ref[...] = update


def node_kernel(u0_ref, u1_ref, u2_ref, u3_ref, base_ref, rows_ref, w_in_ref, w_back_ref, w_edge_ref, node_ref, side_ref):
    update = (u0_ref[...].astype(f32) + u1_ref[...].astype(f32)) + (u2_ref[...].astype(f32) + u3_ref[...].astype(f32))
    normed = layer_norm(base_ref[...] + update).astype(bf16)
    middle = jnp.maximum(dot(normed, w_in_ref[...]), 0.0).astype(bf16)
    node = layer_norm(normed.astype(f32) + dot(middle, w_back_ref[...]))
    node = (node * rows_ref[:, 12:13]).astype(bf16)
    node_ref[...] = node
    side_ref[...] = dot(node, w_edge_ref[...]).astype(bf16)


def edge_kernel(side_ref, other_ref, rows_ref, keys_ref, pair_ref, w_in_ref, w_mid_ref, w_final_ref, out_ref):
    rows, keys = pair_ref.shape[:2]
    step = 8
    w_in = w_in_ref[...]
    side = side_ref[...]
    other = other_ref[...]
    pre_rows = dot(side, w_in[CZ : CZ + NH])
    pre_keys = dot(other, w_in[CZ + NH :])
    side = side.astype(f32)
    other = other.astype(f32)
    keep_rows = rows_ref[:, 12:13]
    keep_keys = keys_ref[:, 12:13]
    for begin in range(0, rows, step):
        pair = pair_ref[begin : begin + step].reshape(step * keys, CZ)
        lifted = dot(pair, w_in[:CZ])
        first = jnp.concatenate(
            [
                jnp.maximum(lifted[n * keys : (n + 1) * keys] + (pre_keys + pre_rows[begin + n : begin + n + 1]), 0.0).astype(bf16)
                for n in range(step)
            ],
            0,
        )
        second = jnp.maximum(dot(first, w_mid_ref[...]), 0.0)
        stacked = jnp.concatenate(
            [
                pair.astype(f32),
                jnp.concatenate([jnp.broadcast_to(side[begin + n : begin + n + 1], (keys, NH)) for n in range(step)], 0),
                jnp.concatenate([other] * step, 0),
            ],
            1,
        )
        edge = layer_norm(dot((second + stacked).astype(bf16), w_final_ref[...]))
        for n in range(step):
            keep = keep_keys * keep_rows[begin + n : begin + n + 1]
            out_ref[begin + n] = (edge[n * keys : (n + 1) * keys] * keep).astype(bf16)


def tile_body(
    node_embed, rotation, translation, pair_embed, chain_index, residue_mask, step_index, w_time, w_query,
    w_query_points, w_kv, w_kvp, w_bias, head_weights, chain_bias, w_out, w_mlp_in, w_mlp_out, w_edge_in,
    w_trunk_in, w_trunk_mid, w_final,
):
    rows = node_embed.shape[0]
    total = residue_mask.shape[0]
    smem = pl.BlockSpec(memory_space=pltpu.SMEM)
    hbm = pl.BlockSpec(memory_space=pltpu.HBM)
    bias = pl.pallas_call(
        bias_kernel,
        out_shape=jax.ShapeDtypeStruct((HEADS * rows // 2, 2 * PAD), f32),
        in_specs=[hbm, hbm],
        out_specs=pl.BlockSpec(memory_space=pltpu.VMEM),
        scratch_shapes=[
            pltpu.VMEM(pair_embed.shape, bf16),
            pltpu.VMEM((HEADS, CZ), bf16),
            pltpu.SemaphoreType.DMA((7,)),
        ],
        compiler_params=params(16),
    )(*stay(pair_embed, w_bias.T))
    near, far = [lax.ppermute(bias, "col", [(i, i ^ k) for i in range(4)]) for k in (1, 2)]
    others = [lax.ppermute(node_embed, "row", [(i, (i + k) % 4) for i in range(4)]) for k in (1, 2, 3)]
    biases = [near, far, lax.ppermute(far, "col", [(i, i ^ 1) for i in range(4)])]
    order = [h * (QP + VP) + n for h in range(HEADS) for n in range(QP)]
    order += [h * (QP + VP) + QP + n for h in range(HEADS) for n in range(VP)]
    order = jnp.asarray(np.eye(len(order), dtype=np.float32)[order], bf16)
    prepared = pl.pallas_call(
        prepare_kernel,
        out_shape=(
            jax.ShapeDtypeStruct((8, CS), f32),
            jax.ShapeDtypeStruct((rows, CS), bf16),
            jax.ShapeDtypeStruct((HEADS * rows, CS), bf16),
            jax.ShapeDtypeStruct((HEADS * rows, 4 * HEADS * QP), f32),
            jax.ShapeDtypeStruct((w_kvp.shape[1], CS), bf16),
            jax.ShapeDtypeStruct((16, 4 * PAD), f32),
            jax.ShapeDtypeStruct((rows, 16), f32),
            jax.ShapeDtypeStruct((rows, 16), f32),
        ),
        in_specs=[smem] + [hbm] * 12,
        out_specs=tuple(vmem(8)),
        scratch_shapes=[
            pltpu.SMEM((HEADS,), f32),
            pltpu.VMEM(rotation.shape, f32),
            pltpu.VMEM(translation.shape, f32),
            pltpu.VMEM((1, total), jnp.int32),
            pltpu.VMEM((1, total), jnp.int32),
            pltpu.VMEM(node_embed.shape, bf16),
            pltpu.VMEM(w_time.shape, bf16),
            pltpu.VMEM(w_query.shape, bf16),
            pltpu.VMEM(w_query_points.shape[::-1], bf16),
            pltpu.VMEM((CS, HEADS * CH), bf16),
            pltpu.VMEM(w_kvp.shape[::-1], bf16),
            pltpu.VMEM(order.shape, bf16),
            pltpu.VMEM((16, total), f32),
            pltpu.SemaphoreType.DMA((12,)),
        ],
        compiler_params=params(24),
        cost_estimate=pl.CostEstimate(flops=2 * 10**9, bytes_accessed=8 * 10**6, transcendentals=0),
    )(
        step_index,
        *stay(
            head_weights, rotation, translation, residue_mask[None], chain_index[None], node_embed, w_time,
            w_query, w_query_points.T, w_kv, w_kvp.T, order,
        )
    )
    time, own, qk, qpts, w_pts, kfeat, row_cols, key_cols = prepared
    partial, x, prob, vpts = pl.pallas_call(
        score_kernel,
        out_shape=(
            jax.ShapeDtypeStruct((rows, CS), bf16),
            jax.ShapeDtypeStruct((4 * PAD, CS), bf16),
            jax.ShapeDtypeStruct((HEADS * rows, 4 * PAD), f32),
            jax.ShapeDtypeStruct((3 * 128, 4 * PAD), f32),
        ),
        in_specs=[smem, smem] + vmem(16),
        out_specs=tuple(vmem(4)),
        scratch_shapes=[
            pltpu.VMEM((HEADS * rows, 2 * PAD), f32),
            pltpu.VMEM((HEADS * rows, CZ), f32),
            pltpu.VMEM((4,) + bias.shape, f32),
        ],
        compiler_params=params(24),
    )(head_weights, chain_bias, own, *others, time, qk, qpts, w_pts, kfeat, row_cols, bias, *biases, pair_embed, w_out)
    base = pl.pallas_call(
        value_kernel,
        out_shape=jax.ShapeDtypeStruct((rows, CS), f32),
        in_specs=vmem(7),
        out_specs=pl.BlockSpec(memory_space=pltpu.VMEM),
        compiler_params=params(24),
        cost_estimate=pl.CostEstimate(flops=10**9, bytes_accessed=4 * 10**6, transcendentals=0),
    )(x, prob, vpts, own, row_cols, w_kv, w_out)
    partials = [lax.ppermute(partial, "col", [(i, i ^ k) for i in range(4)]) for k in (1, 2, 3)]
    node_out, side = pl.pallas_call(
        node_kernel,
        out_shape=(jax.ShapeDtypeStruct((rows, CS), bf16), jax.ShapeDtypeStruct((rows, NH), bf16)),
        in_specs=vmem(9),
        out_specs=tuple(vmem(2)),
        compiler_params=params(16),
    )(partial, *partials, base, row_cols, w_mlp_in, w_mlp_out, w_edge_in)
    turned = []
    for c in range(4):
        far = sorted((r for r in range(4) if r != c), key=lambda r: -abs(r - c))
        turned += [(4 * c + source, 4 * r + c) for r, source in zip([c] + far, (c, c ^ 1, c ^ 2, c ^ 3))]
    other = lax.ppermute(side, ("row", "col"), turned)
    pair_out = pl.pallas_call(
        edge_kernel,
        out_shape=jax.ShapeDtypeStruct(pair_embed.shape, bf16),
        in_specs=vmem(8),
        out_specs=pl.BlockSpec(memory_space=pltpu.VMEM),
        compiler_params=params(24),
    )(side, other, row_cols, key_cols, pair_embed, w_trunk_in, w_trunk_mid, w_final)
    return node_out, pair_out


def dispatch(sizes, *arrays):
    rows, keys = arrays[3].shape[:2]
    square = sizes["row"] == 4 and sizes["col"] == 4 and rows == keys and rows == 48
    return tile_body(*arrays) if square else body(*arrays)


def solution(mesh):
    return jax.shard_map(
        functools.partial(dispatch, dict(mesh.shape)),
        mesh=mesh,
        in_specs=(
            P(("groups", "row"), None),
            P(None, None, "groups"),
            P(None, "groups"),
            P(("groups", "row"), "col", None),
            P("groups"),
            P("groups"),
            P("groups"),
            P(),
            P(),
            P(),
            P(),
            P(),
            P(),
            P(),
            P(),
            P(),
            P(),
            P(),
            P(),
            P(),
            P(),
            P(),
        ),
        out_specs=(P(("groups", "row"), None), P(("groups", "row"), "col", None)),
        check_vma=False,
    )
```

```python
import functools
import math

import jax
import jax.numpy as jnp
import numpy as np
from jax import lax
from jax.experimental import pallas as pl
from jax.experimental.pallas import tpu as pltpu
from jax.sharding import PartitionSpec as P

CS = 256
CZ = 128
HEADS = 8
CH = 256
QP = 8
VP = 12
NH = 128
HID = 384


norm_epsilon = 1e-05
masked_score = 100000.0
highest = lax.Precision.HIGHEST


def layer_norm(values):
    average = jnp.mean(values, -1, keepdims=True)
    centred = values - average
    spread = jnp.mean(centred * centred, -1, keepdims=True)
    return centred * lax.rsqrt(spread + norm_epsilon)


def time_embedding(step_index, embed_width):
    half_width = embed_width // 2
    frequency = jnp.exp(-math.log(10000.0) * jnp.arange(half_width, dtype=jnp.float32) / half_width)
    angles = step_index.astype(jnp.float32)[0] * frequency
    return jnp.concatenate([jnp.sin(angles), jnp.cos(angles)])[None, :].astype(jnp.bfloat16)


def to_global(rotation, shift_vec, points):
    turned = jnp.einsum("abn,nbm->nam", rotation, points, precision=highest)
    return turned + jnp.transpose(shift_vec)[:, :, None]


def project_keys(embedded, rotation, shift_vec, w_kv, w_kvp):
    item_count = embedded.shape[0]
    key_values = jnp.dot(embedded, w_kv, preferred_element_type=jnp.float32).astype(jnp.bfloat16)
    points = jnp.dot(embedded, w_kvp, preferred_element_type=jnp.float32).reshape(item_count, 3, -1)
    return (key_values, to_global(rotation, shift_vec, points))


def node_finish(
    denominator,
    values_out,
    points_out,
    pair_sums,
    embedded,
    rotation,
    shift_vec,
    mask_rows,
    w_out,
    w_mlp_in,
    w_mlp_out,
    w_edge_in,
):
    item_count = embedded.shape[0]
    scale_back = denominator[:, :, None]
    attended = values_out.reshape(item_count, HEADS, CH) / scale_back
    points = points_out.reshape(item_count, 3, HEADS, VP) / denominator[:, None, :, None]
    relative = points - jnp.transpose(shift_vec)[:, :, None, None]
    framed = jnp.einsum("abi,iahv->ibhv", rotation, relative, precision=highest)
    length = jnp.sqrt(jnp.maximum(jnp.sum(framed * framed, 1), 1.0))
    paired = pair_sums.reshape(item_count, HEADS, CZ) / scale_back
    features = jnp.concatenate(
        [
            attended.reshape(item_count, -1),
            framed.reshape(item_count, -1),
            length.reshape(item_count, -1),
            paired.reshape(item_count, -1),
        ],
        -1,
    ).astype(jnp.bfloat16)
    update = jnp.dot(features, w_out, preferred_element_type=jnp.float32)
    normed = layer_norm(embedded.astype(jnp.float32) + update).astype(jnp.bfloat16)
    normed = lax.optimization_barrier(normed)
    middle = jax.nn.relu(jnp.dot(normed, w_mlp_in, preferred_element_type=jnp.float32)).astype(
        jnp.bfloat16
    )
    node_new = layer_norm(
        normed.astype(jnp.float32) + jnp.dot(middle, w_mlp_out, preferred_element_type=jnp.float32)
    )
    node_new = (node_new * mask_rows.astype(jnp.float32)[:, None]).astype(jnp.bfloat16)
    edge_side = jnp.dot(node_new, w_edge_in, preferred_element_type=jnp.float32).astype(
        jnp.bfloat16
    )
    return (node_new, edge_side)


def body(
    node_embed,
    rotation,
    translation,
    pair_embed,
    chain_index,
    residue_mask,
    step_index,
    w_time,
    w_query,
    w_query_points,
    w_kv,
    w_kvp,
    w_bias,
    head_weights,
    chain_bias,
    w_out,
    w_mlp_in,
    w_mlp_out,
    w_edge_in,
    w_trunk_in,
    w_trunk_mid,
    w_final,
):
    row_count = node_embed.shape[0]
    key_count = pair_embed.shape[1]
    row_start = lax.axis_index("row") * row_count
    key_start = lax.axis_index("col") * key_count
    embedded = (
        node_embed.astype(jnp.float32)
        + jnp.dot(time_embedding(step_index, CS), w_time, preferred_element_type=jnp.float32)
    ).astype(jnp.bfloat16)
    embedded = lax.optimization_barrier(embedded)
    rot_rows = lax.dynamic_slice_in_dim(rotation, row_start, row_count, 2)
    shift_rows = lax.dynamic_slice_in_dim(translation, row_start, row_count, 1)
    mask_rows = lax.dynamic_slice_in_dim(residue_mask, row_start, row_count, 0)
    mask_keys = lax.dynamic_slice_in_dim(residue_mask, key_start, key_count, 0)
    chain_rows = lax.dynamic_slice_in_dim(chain_index, row_start, row_count, 0)
    chain_keys = lax.dynamic_slice_in_dim(chain_index, key_start, key_count, 0)
    query_feat = (
        jnp.dot(embedded, w_query, preferred_element_type=jnp.float32)
        .astype(jnp.bfloat16)
        .reshape(row_count, HEADS, CH)
    )
    query_pts = to_global(
        rot_rows,
        shift_rows,
        jnp.dot(embedded, w_query_points, preferred_element_type=jnp.float32).reshape(
            row_count, 3, HEADS * QP
        ),
    ).reshape(row_count, 3, HEADS, QP)
    all_nodes = lax.all_gather(embedded, "row", axis=0, tiled=True)
    key_nodes = lax.dynamic_slice_in_dim(all_nodes, key_start, key_count, 0)
    rot_keys = lax.dynamic_slice_in_dim(rotation, key_start, key_count, 2)
    shift_keys = lax.dynamic_slice_in_dim(translation, key_start, key_count, 1)
    key_values, key_points = project_keys(key_nodes, rot_keys, shift_keys, w_kv, w_kvp)
    key_feat = key_values[:, : HEADS * CH].reshape(key_count, HEADS, CH)
    value_feat = key_values[:, HEADS * CH :].reshape(key_count, HEADS, CH)
    key_points = key_points.reshape(key_count, 3, HEADS, QP + VP)
    key_pts = key_points[..., :QP]
    value_pts = key_points[..., QP:]
    scaled = math.sqrt(1.0 / 3.0)
    point_weight = math.sqrt(2.0 / (9.0 * QP))
    point_gain = jax.nn.softplus(head_weights)
    feature_dots = jnp.einsum(
        "ihc,jhc->hij", query_feat, key_feat, preferred_element_type=jnp.float32
    ) / math.sqrt(CH)
    pair_bias = jnp.einsum("ijc,ch->hij", pair_embed, w_bias, preferred_element_type=jnp.float32)
    same_chain = (chain_rows[:, None] == chain_keys[None, :]).astype(jnp.float32)
    query_square = jnp.einsum("iahp,iahp->hi", query_pts, query_pts, precision=highest)
    key_square = jnp.einsum("jahp,jahp->hj", key_pts, key_pts, precision=highest)
    cross_term = jnp.einsum("iahp,jahp->hij", query_pts, key_pts, precision=highest)
    distance = query_square[:, :, None] + key_square[:, None, :] - 2.0 * cross_term
    mask_term = (mask_keys.astype(jnp.float32) - 1.0) * masked_score
    scores = (
        scaled * (feature_dots + pair_bias + chain_bias[:, None, None] * same_chain[None])
        - scaled * point_weight * 0.5 * point_gain[:, None, None] * distance
        + mask_term[None, None, :]
    )
    row_peak = lax.pmax(jnp.max(scores, -1), "col")
    weights = jnp.exp(scores - row_peak[:, :, None])
    denominator = jnp.transpose(jnp.sum(weights, -1))
    rounded = weights.astype(jnp.bfloat16)
    values_out = jnp.einsum(
        "hij,jhc->ihc", rounded, value_feat, preferred_element_type=jnp.float32
    ).reshape(row_count, -1)
    points_out = jnp.einsum("hij,jahv->iahv", weights, value_pts, precision=highest).reshape(
        row_count, -1
    )
    pair_sums = jnp.einsum(
        "hij,ijc->ihc", rounded, pair_embed, preferred_element_type=jnp.float32
    ).reshape(row_count, -1)
    summed = lax.psum((denominator, values_out, points_out, pair_sums), "col")
    node_out, edge_side = node_finish(
        summed[0],
        summed[1],
        summed[2],
        summed[3],
        embedded,
        rot_rows,
        shift_rows,
        mask_rows,
        w_out,
        w_mlp_in,
        w_mlp_out,
        w_edge_in,
    )
    side_all = lax.all_gather(edge_side, "row", axis=0, tiled=True)
    side_rows = lax.dynamic_slice_in_dim(side_all, row_start, row_count, 0)
    side_keys = lax.dynamic_slice_in_dim(side_all, key_start, key_count, 0)
    pre_rows = jnp.dot(side_rows, w_trunk_in[CZ : CZ + NH], preferred_element_type=jnp.float32)
    pre_keys = jnp.dot(side_keys, w_trunk_in[CZ + NH :], preferred_element_type=jnp.float32)
    mask_key_f = mask_keys.astype(jnp.float32)
    block_rows = math.gcd(row_count, 8)
    block_count = row_count // block_rows

    def edge_block(inputs):
        pair_block, pre_block, side_block, keep_block = inputs
        lifted = (
            jnp.einsum(
                "ijc,cd->ijd", pair_block, w_trunk_in[:CZ], preferred_element_type=jnp.float32
            )
            + pre_block[:, None, :]
            + pre_keys[None, :, :]
        )
        hidden_one = jax.nn.relu(lifted).astype(jnp.bfloat16)
        hidden_two = jax.nn.relu(
            jnp.einsum("ijd,de->ije", hidden_one, w_trunk_mid, preferred_element_type=jnp.float32)
        )
        stacked = jnp.concatenate(
            [
                pair_block,
                jnp.broadcast_to(side_block[:, None, :], (block_rows, key_count, NH)),
                jnp.broadcast_to(side_keys[None, :, :], (block_rows, key_count, NH)),
            ],
            -1,
        )
        joined = (hidden_two + stacked.astype(jnp.float32)).astype(jnp.bfloat16)
        edge_out = jnp.einsum("ijd,dc->ijc", joined, w_final, preferred_element_type=jnp.float32)
        pair_keep = keep_block.astype(jnp.float32)[:, None] * mask_key_f[None, :]
        return (layer_norm(edge_out) * pair_keep[:, :, None]).astype(jnp.bfloat16)

    pair_out = lax.map(
        edge_block,
        (
            pair_embed.reshape(block_count, block_rows, key_count, CZ),
            pre_rows.reshape(block_count, block_rows, HID),
            side_rows.reshape(block_count, block_rows, NH),
            mask_rows.reshape(block_count, block_rows),
        ),
    )
    return (node_out, pair_out.reshape(row_count, key_count, CZ))


PAD = 64
GAIN = math.sqrt(1.0 / 3.0)
POINT = math.sqrt(2.0 / (9.0 * QP))
f32 = jnp.float32
bf16 = jnp.bfloat16


def dot(a, b, dims=((1,), (0,)), precision=None):
    return lax.dot_general(a, b, (dims, ((), ())), precision=precision, preferred_element_type=f32)


NT = ((1,), (1,))
TN = ((0,), (0,))


def params(mib):
    return pltpu.CompilerParams(vmem_limit_bytes=mib * 1024 * 1024)


def vmem(count):
    return [pl.BlockSpec(memory_space=pltpu.VMEM)] * count


def stay(*arrays):
    return [pltpu.with_memory_space_constraint(array, pltpu.HBM) for array in arrays]


def bias_kernel(*refs):
    count = (len(refs) - 6) // 2
    pair_hbm, w_hbm, *held_hbm = refs[: 2 + count]
    out_ref, *held_refs, pair_ref, w_ref, sems = refs[2 + count :]
    half = pair_ref.shape[0] // 2
    copies = [pltpu.make_async_copy(w_hbm, w_ref, sems.at[2])]
    for m in range(2):
        at = pl.ds(m * half, half)
        copies.append(pltpu.make_async_copy(pair_hbm.at[at], pair_ref.at[at], sems.at[m]))
    for n, (src, dst) in enumerate(zip(held_hbm, held_refs)):
        if src.shape != dst.shape:
            src = src.at[:, pl.ds(0, dst.shape[1])]
        copies.append(pltpu.make_async_copy(src, dst, sems.at[3 + n]))
    for copy in copies:
        copy.start()
    for copy in copies[:3]:
        copy.wait()
    keys = pair_ref.shape[1]
    weight = w_ref[...]
    gap = jnp.zeros((PAD - keys, CZ), bf16)
    for i in range(half):
        both = jnp.concatenate([pair_ref[i], gap, pair_ref[i + half], gap], 0)
        out_ref[pl.ds(i, HEADS, stride=half), :] = dot(weight, both, NT) * GAIN
    for copy in copies[3:]:
        copy.wait()


def one_hot(shape, source_dim, offset_of):
    src = lax.broadcasted_iota(jnp.int32, shape, source_dim)
    dst = lax.broadcasted_iota(jnp.int32, shape, 1 - source_dim)
    return (src == offset_of(dst)).astype(f32)


def prepare_kernel(
    step_ref, hw_ref, rotation_ref, shift_ref, mask_ref, chain_ref, node_ref, w_time_ref, w_qp_ref, w_kvp_ref, order_ref,
    w_query_ref, w_kv_ref,
    time_ref, own_ref, qk_ref, qpts_ref, w_pts_ref, kfeat_ref, rows_ref, keys_ref, feats_ref,
):
    rows = node_ref.shape[0]
    half = CS // 2
    row = lax.axis_index("row")
    col = lax.axis_index("col")
    feats_ref[...] = jnp.zeros(feats_ref.shape, f32)
    for a in range(3):
        feats_ref[3 * a : 3 * a + 3, :] = rotation_ref[a]
    feats_ref[9:12, :] = shift_ref[...]
    feats_ref[12:13, :] = mask_ref[...].astype(f32)
    feats_ref[13:14, :] = chain_ref[...].astype(f32)
    total = feats_ref.shape[1]
    lane = lax.broadcasted_iota(jnp.int32, (8, half), 1).astype(f32)
    frequency = jnp.exp(-math.log(10000.0) * lane / half)
    angles = step_ref[0].astype(f32) * frequency
    temb = jnp.concatenate([jnp.sin(angles), jnp.cos(angles)], 1).astype(bf16)
    time = dot(temb, w_time_ref[...])
    time_ref[...] = time
    own = (node_ref[...].astype(f32) + time[0:1]).astype(bf16)
    own_ref[...] = own
    feats = feats_ref[...]

    def key_of(dst):
        part = dst // PAD
        inside = dst - part * PAD
        return jnp.where(inside < rows, part * rows + inside, -1)

    kfeat_ref[...] = dot(feats, one_hot((total, 4 * PAD), 0, key_of), precision=highest)
    own_cols = dot(one_hot((rows, total), 1, lambda d: d + row * rows), feats, NT, precision=highest)
    rows_ref[...] = own_cols
    keys_ref[...] = dot(one_hot((rows, total), 1, lambda d: d + col * rows), feats, NT, precision=highest)
    wide = HEADS * QP
    local = dot(own, w_qp_ref[...], NT)
    parts = [local[:, b * wide : (b + 1) * wide] for b in range(3)]
    points = []
    for a in range(3):
        turned = own_cols[:, 9 + a : 10 + a]
        for b in range(3):
            turned = turned + own_cols[:, 3 * a + b : 3 * a + b + 1] * parts[b]
        points.append(turned)
    points = jnp.concatenate(points + [jnp.zeros((rows, wide), f32)], 1)
    lanes = lax.broadcasted_iota(jnp.int32, (1, 4 * wide), 1)
    hw = hw_ref[...]
    gains = GAIN * POINT * 0.5 * (jnp.maximum(hw, 0.0) + jnp.log1p(jnp.exp(-jnp.abs(hw))))
    rows_ref[...] = own_cols
    for h in range(HEADS):
        gain = gains[:, h : h + 1]
        mine = jnp.where((lanes % wide) // QP == h, points, 0.0)
        square = jnp.sum(mine * mine, 1, keepdims=True)
        qpts_ref[h * rows : (h + 1) * rows, :] = jnp.where(lanes == 3 * wide, -square, 2.0 * mine) * gain
    group = HEADS * (QP + VP)
    for a in range(3):
        at = slice(a * group, (a + 1) * group)
        w_pts_ref[at, :] = dot(order_ref[...], w_kvp_ref[at, :]).astype(bf16)
    query = dot(own, w_query_ref[...]).astype(bf16)
    for h in range(HEADS):
        taken = dot(query[:, h * CH : (h + 1) * CH], w_kv_ref[:, h * CH : (h + 1) * CH], NT)
        qk_ref[h * rows : (h + 1) * rows, :] = (taken * (GAIN / math.sqrt(CH))).astype(bf16)


def score_kernel(
    hw_ref, cb_ref, own_ref, n1_ref, n2_ref, n3_ref, time_ref, qk_ref, qpts_ref, w_pts_ref, kfeat_ref, rows_ref,
    b0_ref, b1_ref, b2_ref, b3_ref, pair_ref, w_out_ref,
    out_ref, x_ref, prob_ref, vpts_ref, near_ref, opair_ref, bias_ref,
):
    rows = own_ref.shape[0]
    half = rows // 2
    row = lax.axis_index("row")
    col = lax.axis_index("col")
    time = time_ref[0:1]
    x_ref[...] = jnp.zeros(x_ref.shape, bf16)
    x_ref[pl.ds(pl.multiple_of(row * PAD, PAD), rows), :] = own_ref[...]
    for k, ref in ((2 + col % 2, n1_ref), (3 - col % 2, n2_ref), (1, n3_ref)):
        place = row ^ k
        x_ref[pl.ds(pl.multiple_of(place * PAD, PAD), rows), :] = (ref[...].astype(f32) + time).astype(bf16)
    for k, ref in enumerate((b0_ref, b1_ref, b2_ref, b3_ref)):
        bias_ref[col ^ k] = ref[...]
    x = x_ref[...]
    keys = x.shape[0]
    kfeat = kfeat_ref[...]
    group = HEADS * (QP + VP)
    wide = HEADS * QP
    local = dot(w_pts_ref[...], x, NT)
    points = []
    for a in range(3):
        turned = kfeat[9 + a : 10 + a]
        for b in range(3):
            turned = turned + kfeat[3 * a + b : 3 * a + b + 1] * local[b * group : (b + 1) * group]
        points.append(turned)
    empty = jnp.zeros((128 - HEADS * VP, keys), f32)
    vpts_ref[...] = jnp.concatenate([part for p in points for part in (p[wide:], empty)], 0)
    key_points = [p[:wide] for p in points]
    cross = dot(qpts_ref[...], jnp.concatenate(key_points + [jnp.ones((wide, keys), f32)], 0), precision=highest)
    key_square = key_points[0] * key_points[0] + key_points[1] * key_points[1] + key_points[2] * key_points[2]
    feature = dot(qk_ref[...], x, NT)
    lane = lax.broadcasted_iota(jnp.int32, (1, 128), 1)
    low = lane < PAD
    bias_low, bias_high = [], []
    for n in (0, 2):
        left, right = bias_ref[n], bias_ref[n + 1]
        bias_low.append(jnp.where(low, left, pltpu.roll(right, PAD, 1)))
        bias_high.append(jnp.where(low, pltpu.roll(left, PAD, 1), right))
    bias_low = jnp.concatenate(bias_low, 1)
    bias_high = jnp.concatenate(bias_high, 1)
    key_lane = lax.broadcasted_iota(jnp.int32, (1, keys), 1)
    blocked = jnp.where(key_lane % PAD < rows, (kfeat[12:13] - 1.0) * masked_score, -1e30)
    same = (rows_ref[:, 13:14] == kfeat[13:14]).astype(f32)
    hw = jnp.zeros((1, 128), f32)
    for h in range(HEADS):
        hw = jnp.where(lane == h, hw_ref[h], hw)
    gains = GAIN * POINT * 0.5 * (jnp.maximum(hw, 0.0) + jnp.log1p(jnp.exp(-jnp.abs(hw))))
    for h in range(HEADS):
        at = slice(h * rows, (h + 1) * rows)
        square = jnp.sum(key_square[h * QP : (h + 1) * QP], 0, keepdims=True)
        bias = jnp.concatenate([bias_low[h * half : (h + 1) * half], bias_high[h * half : (h + 1) * half]], 0)
        score = (
            feature[at] + bias + (GAIN * cb_ref[h]) * same + cross[at] + (blocked - gains[:, h : h + 1] * square)
        )
        peak = jnp.max(score, 1, keepdims=True)
        weight = jnp.exp(score - peak)
        weight = weight / jnp.sum(weight, 1, keepdims=True)
        prob_ref[at, :] = weight
        side = jnp.where(col >= 2, weight[:, 128:], weight[:, :128])
        near_ref[at, :] = pltpu.roll(side, (col % 2) * PAD, 1)
    own_keys = pair_ref.shape[1]
    for i in range(rows):
        weight = near_ref[pl.ds(i, HEADS, stride=rows), :][:, :own_keys].astype(bf16)
        opair_ref[pl.ds(i, HEADS, stride=rows), :] = dot(weight, pair_ref[i])
    tail = HEADS * CH + 4 * HEADS * VP
    paired = jnp.concatenate([opair_ref[h * rows : (h + 1) * rows, :] for h in range(HEADS)], 1).astype(bf16)
    out_ref[...] = dot(paired, w_out_ref[tail:]).astype(out_ref.dtype)


def value_kernel(x_ref, prob_ref, vpts_ref, own_ref, rows_ref, w_kv_ref, w_out_ref, out_ref):
    rows = own_ref.shape[0]
    tail = HEADS * CH
    own_cols = rows_ref[...]
    prob = prob_ref[...]
    mixed = dot(prob.astype(bf16), x_ref[...]).astype(bf16)
    attended = jnp.concatenate(
        [
            dot(mixed[h * rows : (h + 1) * rows], w_kv_ref[:, tail + h * CH : tail + (h + 1) * CH]).astype(bf16)
            for h in range(HEADS)
        ],
        1,
    )
    update = own_ref[...].astype(f32) + dot(attended, w_out_ref[:tail])
    gathered = dot(prob, vpts_ref[...], NT, precision=highest)
    spread = lax.broadcasted_iota(jnp.int32, (1, 3 * 128), 1) % 128 // VP
    kept = jnp.zeros((rows, 3 * 128), f32)
    for h in range(HEADS):
        kept = jnp.where(spread == h, gathered[h * rows : (h + 1) * rows], kept)
    relative = [kept[:, a * 128 : (a + 1) * 128] - own_cols[:, 9 + a : 10 + a] for a in range(3)]
    framed = []
    for b in range(3):
        framed.append(
            own_cols[:, b : b + 1] * relative[0]
            + own_cols[:, 3 + b : 4 + b] * relative[1]
            + own_cols[:, 6 + b : 7 + b] * relative[2]
        )
    length = jnp.sqrt(jnp.maximum(framed[0] * framed[0] + framed[1] * framed[1] + framed[2] * framed[2], 1.0))
    span = HEADS * VP
    for n, part in enumerate(framed + [length]):
        update = update + dot(part[:, :span].astype(bf16), w_out_ref[tail + n * span : tail + (n + 1) * span])
    out_ref[...] = update


def node_kernel(u0_ref, u1_ref, u2_ref, u3_ref, base_ref, rows_ref, w_in_ref, w_back_ref, w_edge_ref, node_ref, side_ref):
    update = (u0_ref[...].astype(f32) + u1_ref[...].astype(f32)) + (u2_ref[...].astype(f32) + u3_ref[...].astype(f32))
    normed = layer_norm(base_ref[...] + update).astype(bf16)
    middle = jnp.maximum(dot(normed, w_in_ref[...]), 0.0).astype(bf16)
    node = layer_norm(normed.astype(f32) + dot(middle, w_back_ref[...]))
    node = (node * rows_ref[:, 12:13]).astype(bf16)
    node_ref[...] = node
    side_ref[...] = dot(node, w_edge_ref[...]).astype(bf16)


def edge_kernel(
    side_ref, other_ref, rows_ref, keys_ref, pair_ref, w_in_ref, w_mid_ref, w_final_ref, out_hbm, out_ref, sems
):
    rows, keys = pair_ref.shape[:2]
    step = math.gcd(rows, 16)
    pre_rows = dot(side_ref[...], w_in_ref[CZ : CZ + NH])
    pre_keys = dot(other_ref[...], w_in_ref[CZ + NH :])
    side = side_ref[...].astype(f32)
    other = other_ref[...].astype(f32)
    keep_rows = rows_ref[:, 12:13]
    keep_keys = keys_ref[:, 12:13]
    copies = []
    for begin in range(0, rows, step):
        parts = [(begin + n, slice(n * keys, (n + 1) * keys)) for n in range(step)]
        pair = pair_ref[begin : begin + step].reshape(step * keys, CZ)
        lifted = dot(pair, w_in_ref[:CZ])
        first = jnp.concatenate(
            [jnp.maximum(lifted[at] + (pre_keys + pre_rows[i : i + 1]), 0.0).astype(bf16) for i, at in parts], 0
        )
        second = jnp.maximum(dot(first, w_mid_ref[...]), 0.0)
        joined = jnp.concatenate(
            [
                (second[:, :CZ] + pair.astype(f32)).astype(bf16),
                jnp.concatenate([(second[at, CZ : CZ + NH] + side[i : i + 1]).astype(bf16) for i, at in parts], 0),
                jnp.concatenate([(second[at, CZ + NH :] + other).astype(bf16) for i, at in parts], 0),
            ],
            1,
        )
        edge = layer_norm(dot(joined, w_final_ref[...]))
        for i, at in parts:
            out_ref[i] = (edge[at] * (keep_keys * keep_rows[i : i + 1])).astype(bf16)
        done = pl.ds(begin, step)
        copies.append(pltpu.make_async_copy(out_ref.at[done], out_hbm.at[done], sems.at[begin // step]))
        copies[-1].start()
    for copy in copies:
        copy.wait()


def tile_body(
    node_embed, rotation, translation, pair_embed, chain_index, residue_mask, step_index, w_time, w_query,
    w_query_points, w_kv, w_kvp, w_bias, head_weights, chain_bias, w_out, w_mlp_in, w_mlp_out, w_edge_in,
    w_trunk_in, w_trunk_mid, w_final,
):
    rows = node_embed.shape[0]
    total = residue_mask.shape[0]
    smem = pl.BlockSpec(memory_space=pltpu.SMEM)
    hbm = pl.BlockSpec(memory_space=pltpu.HBM)
    order = [h * (QP + VP) + n for h in range(HEADS) for n in range(QP)]
    order += [h * (QP + VP) + QP + n for h in range(HEADS) for n in range(VP)]
    order = jnp.asarray(np.eye(len(order), dtype=np.float32)[order], bf16)
    held = (
        head_weights[None], rotation, translation, residue_mask[None], chain_index[None], node_embed, w_time,
        w_query_points.T, w_kvp.T, order, w_query, w_kv,
    )
    shapes = [jax.ShapeDtypeStruct(array.shape, array.dtype) for array in held]
    shapes[-1] = jax.ShapeDtypeStruct((CS, HEADS * CH), bf16)
    bias, *held = pl.pallas_call(
        bias_kernel,
        out_shape=[jax.ShapeDtypeStruct((HEADS * rows // 2, 2 * PAD), f32)] + shapes,
        in_specs=[hbm] * (2 + len(held)),
        out_specs=vmem(1 + len(held)),
        scratch_shapes=[
            pltpu.VMEM(pair_embed.shape, bf16),
            pltpu.VMEM((HEADS, CZ), bf16),
            pltpu.SemaphoreType.DMA((3 + len(held),)),
        ],
        compiler_params=params(16),
    )(*stay(pair_embed, w_bias.T, *held))
    near, far = [lax.ppermute(bias, "col", [(i, i ^ k) for i in range(4)]) for k in (1, 2)]
    apart = [(4 * r + c, 4 * (r ^ (2 + c % 2)) + c) for r in range(4) for c in range(4)]
    fetched = lax.ppermute(node_embed, ("row", "col"), apart)
    beside = lax.ppermute(node_embed, "row", [(i, i ^ 1) for i in range(4)])
    others = [fetched, lax.ppermute(fetched, "col", [(i, i ^ 1) for i in range(4)]), beside]
    biases = [near, far, lax.ppermute(far, "col", [(i, i ^ 1) for i in range(4)])]
    prepared = pl.pallas_call(
        prepare_kernel,
        out_shape=(
            jax.ShapeDtypeStruct((8, CS), f32),
            jax.ShapeDtypeStruct((rows, CS), bf16),
            jax.ShapeDtypeStruct((HEADS * rows, CS), bf16),
            jax.ShapeDtypeStruct((HEADS * rows, 4 * HEADS * QP), f32),
            jax.ShapeDtypeStruct((w_kvp.shape[1], CS), bf16),
            jax.ShapeDtypeStruct((16, 4 * PAD), f32),
            jax.ShapeDtypeStruct((rows, 16), f32),
            jax.ShapeDtypeStruct((rows, 16), f32),
        ),
        in_specs=[smem] + vmem(12),
        out_specs=tuple(vmem(8)),
        scratch_shapes=[pltpu.VMEM((16, total), f32)],
        compiler_params=params(16),
        cost_estimate=pl.CostEstimate(flops=2 * 10**9, bytes_accessed=8 * 10**6, transcendentals=0),
    )(step_index, *held)
    time, own, qk, qpts, w_pts, kfeat, row_cols, key_cols = prepared
    partial, x, prob, vpts = pl.pallas_call(
        score_kernel,
        out_shape=(
            jax.ShapeDtypeStruct((rows, CS), bf16),
            jax.ShapeDtypeStruct((4 * PAD, CS), bf16),
            jax.ShapeDtypeStruct((HEADS * rows, 4 * PAD), f32),
            jax.ShapeDtypeStruct((3 * 128, 4 * PAD), f32),
        ),
        in_specs=[smem, smem] + vmem(16),
        out_specs=tuple(vmem(4)),
        scratch_shapes=[
            pltpu.VMEM((HEADS * rows, 2 * PAD), f32),
            pltpu.VMEM((HEADS * rows, CZ), f32),
            pltpu.VMEM((4,) + bias.shape, f32),
        ],
        compiler_params=params(24),
    )(head_weights, chain_bias, own, *others, time, qk, qpts, w_pts, kfeat, row_cols, bias, *biases, pair_embed, w_out)
    base = pl.pallas_call(
        value_kernel,
        out_shape=jax.ShapeDtypeStruct((rows, CS), f32),
        in_specs=vmem(7),
        out_specs=pl.BlockSpec(memory_space=pltpu.VMEM),
        compiler_params=params(24),
        cost_estimate=pl.CostEstimate(flops=10**9, bytes_accessed=4 * 10**6, transcendentals=0),
    )(x, prob, vpts, own, row_cols, w_kv, w_out)
    partials = [lax.ppermute(partial, "col", [(i, i ^ k) for i in range(4)]) for k in (1, 2, 3)]
    node_out, side = pl.pallas_call(
        node_kernel,
        out_shape=(jax.ShapeDtypeStruct((rows, CS), bf16), jax.ShapeDtypeStruct((rows, NH), bf16)),
        in_specs=vmem(9),
        out_specs=tuple(vmem(2)),
        compiler_params=params(16),
    )(partial, *partials, base, row_cols, w_mlp_in, w_mlp_out, w_edge_in)
    turned = []
    for c in range(4):
        far = sorted((r for r in range(4) if r != c), key=lambda r: -abs(r - c))
        turned += [(4 * c + source, 4 * r + c) for r, source in zip([c] + far, (c, c ^ 1, c ^ 2, c ^ 3))]
    other = lax.ppermute(side, ("row", "col"), turned)
    pair_out = pl.pallas_call(
        edge_kernel,
        out_shape=jax.ShapeDtypeStruct(pair_embed.shape, bf16),
        in_specs=vmem(8),
        out_specs=hbm,
        scratch_shapes=[pltpu.VMEM(pair_embed.shape, bf16), pltpu.SemaphoreType.DMA((rows // math.gcd(rows, 16),))],
        compiler_params=params(24),
    )(side, other, row_cols, key_cols, pair_embed, w_trunk_in, w_trunk_mid, w_final)
    return node_out, pair_out


def dispatch(sizes, *arrays):
    rows, keys = arrays[3].shape[:2]
    square = sizes["row"] == 4 and sizes["col"] == 4 and rows == keys and rows == 48
    return tile_body(*arrays) if square else body(*arrays)


def solution(mesh):
    return jax.shard_map(
        functools.partial(dispatch, dict(mesh.shape)),
        mesh=mesh,
        in_specs=(
            P(("groups", "row"), None),
            P(None, None, "groups"),
            P(None, "groups"),
            P(("groups", "row"), "col", None),
            P("groups"),
            P("groups"),
            P("groups"),
            P(),
            P(),
            P(),
            P(),
            P(),
            P(),
            P(),
            P(),
            P(),
            P(),
            P(),
            P(),
            P(),
            P(),
            P(),
        ),
        out_specs=(P(("groups", "row"), None), P(("groups", "row"), "col", None)),
        check_vma=False,
    )
```

```python
import functools
import math

import jax
import jax.numpy as jnp
import numpy as np
from jax import lax
from jax.experimental import pallas as pl
from jax.experimental.pallas import tpu as pltpu
from jax.sharding import PartitionSpec as P

CS = 256
CZ = 128
HEADS = 8
CH = 256
QP = 8
VP = 12
NH = 128
HID = 384


norm_epsilon = 1e-05
masked_score = 100000.0
highest = lax.Precision.HIGHEST


def layer_norm(values):
    average = jnp.mean(values, -1, keepdims=True)
    centred = values - average
    spread = jnp.mean(centred * centred, -1, keepdims=True)
    return centred * lax.rsqrt(spread + norm_epsilon)


def time_embedding(step_index, embed_width):
    half_width = embed_width // 2
    frequency = jnp.exp(-math.log(10000.0) * jnp.arange(half_width, dtype=jnp.float32) / half_width)
    angles = step_index.astype(jnp.float32)[0] * frequency
    return jnp.concatenate([jnp.sin(angles), jnp.cos(angles)])[None, :].astype(jnp.bfloat16)


def to_global(rotation, shift_vec, points):
    turned = jnp.einsum("abn,nbm->nam", rotation, points, precision=highest)
    return turned + jnp.transpose(shift_vec)[:, :, None]


def project_keys(embedded, rotation, shift_vec, w_kv, w_kvp):
    item_count = embedded.shape[0]
    key_values = jnp.dot(embedded, w_kv, preferred_element_type=jnp.float32).astype(jnp.bfloat16)
    points = jnp.dot(embedded, w_kvp, preferred_element_type=jnp.float32).reshape(item_count, 3, -1)
    return (key_values, to_global(rotation, shift_vec, points))


def node_finish(
    denominator,
    values_out,
    points_out,
    pair_sums,
    embedded,
    rotation,
    shift_vec,
    mask_rows,
    w_out,
    w_mlp_in,
    w_mlp_out,
    w_edge_in,
):
    item_count = embedded.shape[0]
    scale_back = denominator[:, :, None]
    attended = values_out.reshape(item_count, HEADS, CH) / scale_back
    points = points_out.reshape(item_count, 3, HEADS, VP) / denominator[:, None, :, None]
    relative = points - jnp.transpose(shift_vec)[:, :, None, None]
    framed = jnp.einsum("abi,iahv->ibhv", rotation, relative, precision=highest)
    length = jnp.sqrt(jnp.maximum(jnp.sum(framed * framed, 1), 1.0))
    paired = pair_sums.reshape(item_count, HEADS, CZ) / scale_back
    features = jnp.concatenate(
        [
            attended.reshape(item_count, -1),
            framed.reshape(item_count, -1),
            length.reshape(item_count, -1),
            paired.reshape(item_count, -1),
        ],
        -1,
    ).astype(jnp.bfloat16)
    update = jnp.dot(features, w_out, preferred_element_type=jnp.float32)
    normed = layer_norm(embedded.astype(jnp.float32) + update).astype(jnp.bfloat16)
    normed = lax.optimization_barrier(normed)
    middle = jax.nn.relu(jnp.dot(normed, w_mlp_in, preferred_element_type=jnp.float32)).astype(
        jnp.bfloat16
    )
    node_new = layer_norm(
        normed.astype(jnp.float32) + jnp.dot(middle, w_mlp_out, preferred_element_type=jnp.float32)
    )
    node_new = (node_new * mask_rows.astype(jnp.float32)[:, None]).astype(jnp.bfloat16)
    edge_side = jnp.dot(node_new, w_edge_in, preferred_element_type=jnp.float32).astype(
        jnp.bfloat16
    )
    return (node_new, edge_side)


def body(
    node_embed,
    rotation,
    translation,
    pair_embed,
    chain_index,
    residue_mask,
    step_index,
    w_time,
    w_query,
    w_query_points,
    w_kv,
    w_kvp,
    w_bias,
    head_weights,
    chain_bias,
    w_out,
    w_mlp_in,
    w_mlp_out,
    w_edge_in,
    w_trunk_in,
    w_trunk_mid,
    w_final,
):
    row_count = node_embed.shape[0]
    key_count = pair_embed.shape[1]
    row_start = lax.axis_index("row") * row_count
    key_start = lax.axis_index("col") * key_count
    embedded = (
        node_embed.astype(jnp.float32)
        + jnp.dot(time_embedding(step_index, CS), w_time, preferred_element_type=jnp.float32)
    ).astype(jnp.bfloat16)
    embedded = lax.optimization_barrier(embedded)
    rot_rows = lax.dynamic_slice_in_dim(rotation, row_start, row_count, 2)
    shift_rows = lax.dynamic_slice_in_dim(translation, row_start, row_count, 1)
    mask_rows = lax.dynamic_slice_in_dim(residue_mask, row_start, row_count, 0)
    mask_keys = lax.dynamic_slice_in_dim(residue_mask, key_start, key_count, 0)
    chain_rows = lax.dynamic_slice_in_dim(chain_index, row_start, row_count, 0)
    chain_keys = lax.dynamic_slice_in_dim(chain_index, key_start, key_count, 0)
    query_feat = (
        jnp.dot(embedded, w_query, preferred_element_type=jnp.float32)
        .astype(jnp.bfloat16)
        .reshape(row_count, HEADS, CH)
    )
    query_pts = to_global(
        rot_rows,
        shift_rows,
        jnp.dot(embedded, w_query_points, preferred_element_type=jnp.float32).reshape(
            row_count, 3, HEADS * QP
        ),
    ).reshape(row_count, 3, HEADS, QP)
    all_nodes = lax.all_gather(embedded, "row", axis=0, tiled=True)
    key_nodes = lax.dynamic_slice_in_dim(all_nodes, key_start, key_count, 0)
    rot_keys = lax.dynamic_slice_in_dim(rotation, key_start, key_count, 2)
    shift_keys = lax.dynamic_slice_in_dim(translation, key_start, key_count, 1)
    key_values, key_points = project_keys(key_nodes, rot_keys, shift_keys, w_kv, w_kvp)
    key_feat = key_values[:, : HEADS * CH].reshape(key_count, HEADS, CH)
    value_feat = key_values[:, HEADS * CH :].reshape(key_count, HEADS, CH)
    key_points = key_points.reshape(key_count, 3, HEADS, QP + VP)
    key_pts = key_points[..., :QP]
    value_pts = key_points[..., QP:]
    scaled = math.sqrt(1.0 / 3.0)
    point_weight = math.sqrt(2.0 / (9.0 * QP))
    point_gain = jax.nn.softplus(head_weights)
    feature_dots = jnp.einsum(
        "ihc,jhc->hij", query_feat, key_feat, preferred_element_type=jnp.float32
    ) / math.sqrt(CH)
    pair_bias = jnp.einsum("ijc,ch->hij", pair_embed, w_bias, preferred_element_type=jnp.float32)
    same_chain = (chain_rows[:, None] == chain_keys[None, :]).astype(jnp.float32)
    query_square = jnp.einsum("iahp,iahp->hi", query_pts, query_pts, precision=highest)
    key_square = jnp.einsum("jahp,jahp->hj", key_pts, key_pts, precision=highest)
    cross_term = jnp.einsum("iahp,jahp->hij", query_pts, key_pts, precision=highest)
    distance = query_square[:, :, None] + key_square[:, None, :] - 2.0 * cross_term
    mask_term = (mask_keys.astype(jnp.float32) - 1.0) * masked_score
    scores = (
        scaled * (feature_dots + pair_bias + chain_bias[:, None, None] * same_chain[None])
        - scaled * point_weight * 0.5 * point_gain[:, None, None] * distance
        + mask_term[None, None, :]
    )
    row_peak = lax.pmax(jnp.max(scores, -1), "col")
    weights = jnp.exp(scores - row_peak[:, :, None])
    denominator = jnp.transpose(jnp.sum(weights, -1))
    rounded = weights.astype(jnp.bfloat16)
    values_out = jnp.einsum(
        "hij,jhc->ihc", rounded, value_feat, preferred_element_type=jnp.float32
    ).reshape(row_count, -1)
    points_out = jnp.einsum("hij,jahv->iahv", weights, value_pts, precision=highest).reshape(
        row_count, -1
    )
    pair_sums = jnp.einsum(
        "hij,ijc->ihc", rounded, pair_embed, preferred_element_type=jnp.float32
    ).reshape(row_count, -1)
    summed = lax.psum((denominator, values_out, points_out, pair_sums), "col")
    node_out, edge_side = node_finish(
        summed[0],
        summed[1],
        summed[2],
        summed[3],
        embedded,
        rot_rows,
        shift_rows,
        mask_rows,
        w_out,
        w_mlp_in,
        w_mlp_out,
        w_edge_in,
    )
    side_all = lax.all_gather(edge_side, "row", axis=0, tiled=True)
    side_rows = lax.dynamic_slice_in_dim(side_all, row_start, row_count, 0)
    side_keys = lax.dynamic_slice_in_dim(side_all, key_start, key_count, 0)
    pre_rows = jnp.dot(side_rows, w_trunk_in[CZ : CZ + NH], preferred_element_type=jnp.float32)
    pre_keys = jnp.dot(side_keys, w_trunk_in[CZ + NH :], preferred_element_type=jnp.float32)
    mask_key_f = mask_keys.astype(jnp.float32)
    block_rows = math.gcd(row_count, 8)
    block_count = row_count // block_rows

    def edge_block(inputs):
        pair_block, pre_block, side_block, keep_block = inputs
        lifted = (
            jnp.einsum(
                "ijc,cd->ijd", pair_block, w_trunk_in[:CZ], preferred_element_type=jnp.float32
            )
            + pre_block[:, None, :]
            + pre_keys[None, :, :]
        )
        hidden_one = jax.nn.relu(lifted).astype(jnp.bfloat16)
        hidden_two = jax.nn.relu(
            jnp.einsum("ijd,de->ije", hidden_one, w_trunk_mid, preferred_element_type=jnp.float32)
        )
        stacked = jnp.concatenate(
            [
                pair_block,
                jnp.broadcast_to(side_block[:, None, :], (block_rows, key_count, NH)),
                jnp.broadcast_to(side_keys[None, :, :], (block_rows, key_count, NH)),
            ],
            -1,
        )
        joined = (hidden_two + stacked.astype(jnp.float32)).astype(jnp.bfloat16)
        edge_out = jnp.einsum("ijd,dc->ijc", joined, w_final, preferred_element_type=jnp.float32)
        pair_keep = keep_block.astype(jnp.float32)[:, None] * mask_key_f[None, :]
        return (layer_norm(edge_out) * pair_keep[:, :, None]).astype(jnp.bfloat16)

    pair_out = lax.map(
        edge_block,
        (
            pair_embed.reshape(block_count, block_rows, key_count, CZ),
            pre_rows.reshape(block_count, block_rows, HID),
            side_rows.reshape(block_count, block_rows, NH),
            mask_rows.reshape(block_count, block_rows),
        ),
    )
    return (node_out, pair_out.reshape(row_count, key_count, CZ))


PAD = 64
GAIN = math.sqrt(1.0 / 3.0)
POINT = math.sqrt(2.0 / (9.0 * QP))
f32 = jnp.float32
bf16 = jnp.bfloat16


def dot(a, b, dims=((1,), (0,)), precision=None):
    return lax.dot_general(a, b, (dims, ((), ())), precision=precision, preferred_element_type=f32)


NT = ((1,), (1,))
TN = ((0,), (0,))


def params(mib):
    return pltpu.CompilerParams(vmem_limit_bytes=mib * 1024 * 1024)


def vmem(count):
    return [pl.BlockSpec(memory_space=pltpu.VMEM)] * count


def stay(*arrays):
    return [pltpu.with_memory_space_constraint(array, pltpu.HBM) for array in arrays]


def bias_kernel(*refs):
    count = (len(refs) - 6) // 2
    pair_hbm, w_hbm, *held_hbm = refs[: 2 + count]
    out_ref, *held_refs, pair_ref, w_ref, sems = refs[2 + count :]
    half = pair_ref.shape[0] // 2
    copies = [pltpu.make_async_copy(w_hbm, w_ref, sems.at[2])]
    for m in range(2):
        at = pl.ds(m * half, half)
        copies.append(pltpu.make_async_copy(pair_hbm.at[at], pair_ref.at[at], sems.at[m]))
    for n, (src, dst) in enumerate(zip(held_hbm, held_refs)):
        if src.shape != dst.shape:
            src = src.at[:, pl.ds(0, dst.shape[1])]
        copies.append(pltpu.make_async_copy(src, dst, sems.at[3 + n]))
    for copy in copies:
        copy.start()
    for copy in copies[:3]:
        copy.wait()
    keys = pair_ref.shape[1]
    weight = w_ref[...]
    gap = jnp.zeros((PAD - keys, CZ), bf16)
    for i in range(half):
        both = jnp.concatenate([pair_ref[i], gap, pair_ref[i + half], gap], 0)
        out_ref[pl.ds(i, HEADS, stride=half), :] = dot(weight, both, NT) * GAIN
    for copy in copies[3:]:
        copy.wait()


def one_hot(shape, source_dim, offset_of):
    src = lax.broadcasted_iota(jnp.int32, shape, source_dim)
    dst = lax.broadcasted_iota(jnp.int32, shape, 1 - source_dim)
    return (src == offset_of(dst)).astype(f32)


def prepare_kernel(
    step_ref, hw_ref, cb_ref, rotation_ref, shift_ref, mask_ref, chain_ref, node_ref, w_time_ref, w_qp_ref, w_kvp_ref, order_ref,
    w_query_ref, w_kv_ref,
    time_ref, own_ref, qk_ref, qpts_ref, w_pts_ref, kfeat_ref, rows_ref, keys_ref, heads_ref, feats_ref,
):
    rows = node_ref.shape[0]
    half = CS // 2
    row = lax.axis_index("row")
    col = lax.axis_index("col")
    feats_ref[...] = jnp.zeros(feats_ref.shape, f32)
    for a in range(3):
        feats_ref[3 * a : 3 * a + 3, :] = rotation_ref[a]
    feats_ref[9:12, :] = shift_ref[...]
    feats_ref[12:13, :] = mask_ref[...].astype(f32)
    feats_ref[13:14, :] = chain_ref[...].astype(f32)
    total = feats_ref.shape[1]
    lane = lax.broadcasted_iota(jnp.int32, (8, half), 1).astype(f32)
    frequency = jnp.exp(-math.log(10000.0) * lane / half)
    angles = step_ref[0].astype(f32) * frequency
    temb = jnp.concatenate([jnp.sin(angles), jnp.cos(angles)], 1).astype(bf16)
    time = dot(temb, w_time_ref[...])
    time_ref[...] = time
    own = (node_ref[...].astype(f32) + time[0:1]).astype(bf16)
    own_ref[...] = own
    feats = feats_ref[...]

    def key_of(dst):
        part = dst // PAD
        inside = dst - part * PAD
        return jnp.where(inside < rows, part * rows + inside, -1)

    kfeat_ref[...] = dot(feats, one_hot((total, 4 * PAD), 0, key_of), precision=highest)
    own_cols = dot(one_hot((rows, total), 1, lambda d: d + row * rows), feats, NT, precision=highest)
    rows_ref[...] = own_cols
    keys_ref[...] = dot(one_hot((rows, total), 1, lambda d: d + col * rows), feats, NT, precision=highest)
    wide = HEADS * QP
    local = dot(own, w_qp_ref[...], NT)
    parts = [local[:, b * wide : (b + 1) * wide] for b in range(3)]
    points = []
    for a in range(3):
        turned = own_cols[:, 9 + a : 10 + a]
        for b in range(3):
            turned = turned + own_cols[:, 3 * a + b : 3 * a + b + 1] * parts[b]
        points.append(turned)
    points = jnp.concatenate(points + [jnp.zeros((rows, wide), f32)], 1)
    lanes = lax.broadcasted_iota(jnp.int32, (1, 4 * wide), 1)
    hw = hw_ref[...]
    gains = GAIN * POINT * 0.5 * (jnp.maximum(hw, 0.0) + jnp.log1p(jnp.exp(-jnp.abs(hw))))
    heads_ref[0:1, :] = gains
    heads_ref[1:2, :] = GAIN * cb_ref[...]
    for h in range(HEADS):
        gain = gains[:, h : h + 1]
        mine = jnp.where((lanes % wide) // QP == h, points, 0.0)
        square = jnp.sum(mine * mine, 1, keepdims=True)
        mine = jnp.where(lanes == 3 * wide, -square, 2.0 * mine) * gain
        high = mine.astype(bf16)
        qpts_ref[0, h * rows : (h + 1) * rows, :] = high
        qpts_ref[1, h * rows : (h + 1) * rows, :] = (mine - high.astype(f32)).astype(bf16)
    group = HEADS * (QP + VP)
    for a in range(3):
        at = slice(a * group, (a + 1) * group)
        w_pts_ref[at, :] = dot(order_ref[...], w_kvp_ref[at, :]).astype(bf16)
    query = dot(own, w_query_ref[...]).astype(bf16)
    for h in range(HEADS):
        taken = dot(query[:, h * CH : (h + 1) * CH], w_kv_ref[:, h * CH : (h + 1) * CH], NT)
        qk_ref[h * rows : (h + 1) * rows, :] = (taken * (GAIN / math.sqrt(CH))).astype(bf16)


def score_kernel(
    heads_ref, own_ref, n1_ref, n2_ref, n3_ref, time_ref, qk_ref, qpts_ref, w_pts_ref, kfeat_ref, rows_ref,
    b0_ref, b1_ref, b2_ref, b3_ref, pair_ref, w_out_ref,
    out_ref, x_ref, prob_ref, vpts_ref, near_ref, opair_ref, bias_ref, w_tail_ref, sem,
):
    tail = HEADS * CH + 4 * HEADS * VP
    copy = pltpu.make_async_copy(w_out_ref.at[pl.ds(tail, HEADS * CZ)], w_tail_ref, sem)
    copy.start()
    rows = own_ref.shape[0]
    half = rows // 2
    row = lax.axis_index("row")
    col = lax.axis_index("col")
    time = time_ref[0:1]
    x_ref[...] = jnp.zeros(x_ref.shape, bf16)
    x_ref[pl.ds(pl.multiple_of(row * PAD, PAD), rows), :] = own_ref[...]
    for k, ref in ((2 + col % 2, n1_ref), (3 - col % 2, n2_ref), (1, n3_ref)):
        place = row ^ k
        x_ref[pl.ds(pl.multiple_of(place * PAD, PAD), rows), :] = (ref[...].astype(f32) + time).astype(bf16)
    for k, ref in enumerate((b0_ref, b1_ref, b2_ref, b3_ref)):
        bias_ref[col ^ k] = ref[...]
    x = x_ref[...]
    keys = x.shape[0]
    kfeat = kfeat_ref[...]
    group = HEADS * (QP + VP)
    wide = HEADS * QP
    local = dot(w_pts_ref[...], x, NT)
    points = []
    for a in range(3):
        turned = kfeat[9 + a : 10 + a]
        for b in range(3):
            turned = turned + kfeat[3 * a + b : 3 * a + b + 1] * local[b * group : (b + 1) * group]
        points.append(turned)
    empty = jnp.zeros((128 - HEADS * VP, keys), f32)
    vpts_ref[...] = jnp.concatenate([part for p in points for part in (p[wide:], empty)], 0)
    key_points = [p[:wide] for p in points]
    exact = jnp.concatenate(key_points + [jnp.ones((wide, keys), f32)], 0)
    high = exact.astype(bf16)
    cross = dot(qpts_ref[0], high) + (dot(qpts_ref[0], (exact - high.astype(f32)).astype(bf16)) + dot(qpts_ref[1], high))
    key_square = key_points[0] * key_points[0] + key_points[1] * key_points[1] + key_points[2] * key_points[2]
    feature = dot(qk_ref[...], x, NT)
    lane = lax.broadcasted_iota(jnp.int32, (1, 128), 1)
    low = lane < PAD
    bias_low, bias_high = [], []
    for n in (0, 2):
        left, right = bias_ref[n], bias_ref[n + 1]
        bias_low.append(jnp.where(low, left, pltpu.roll(right, PAD, 1)))
        bias_high.append(jnp.where(low, pltpu.roll(left, PAD, 1), right))
    bias_low = jnp.concatenate(bias_low, 1)
    bias_high = jnp.concatenate(bias_high, 1)
    key_lane = lax.broadcasted_iota(jnp.int32, (1, keys), 1)
    blocked = jnp.where(key_lane % PAD < rows, (kfeat[12:13] - 1.0) * masked_score, -1e30)
    same = (rows_ref[:, 13:14] == kfeat[13:14]).astype(f32)
    gains = heads_ref[0:1]
    together = heads_ref[1:2]
    for h in range(HEADS):
        at = slice(h * rows, (h + 1) * rows)
        square = jnp.sum(key_square[h * QP : (h + 1) * QP], 0, keepdims=True)
        bias = jnp.concatenate([bias_low[h * half : (h + 1) * half], bias_high[h * half : (h + 1) * half]], 0)
        score = (
            feature[at] + bias + together[:, h : h + 1] * same + cross[at] + (blocked - gains[:, h : h + 1] * square)
        )
        peak = jnp.max(score, 1, keepdims=True)
        weight = jnp.exp(score - peak)
        weight = weight / jnp.sum(weight, 1, keepdims=True)
        prob_ref[at, :] = weight
        side = jnp.where(col >= 2, weight[:, 128:], weight[:, :128])
        near_ref[0, at, :] = jnp.where(low, pltpu.roll(side, (col % 2) * PAD, 1), 0.0)
        near_ref[1, at, :] = jnp.where(low, 0.0, pltpu.roll(side, (1 - col % 2) * PAD, 1))
    gap = jnp.zeros((PAD - pair_ref.shape[1], CZ), bf16)
    blank = jnp.zeros((2 * HEADS, 2 * PAD), f32)
    for i in range(0, rows, 4):
        weight = []
        for n in (i, i + 2):
            weight.append(
                jnp.concatenate([near_ref[m, pl.ds(n + m, HEADS, stride=rows), :] for m in (0, 1)], 0)
            )
        weight = jnp.concatenate(
            [jnp.concatenate([weight[0], blank], 1), jnp.concatenate([blank, weight[1]], 1)], 0
        ).astype(bf16)
        summed = dot(weight, jnp.concatenate([part for n in range(4) for part in (pair_ref[i + n], gap)], 0))
        for n in range(4):
            opair_ref[pl.ds(i + n, HEADS, stride=rows), :] = summed[n * HEADS : (n + 1) * HEADS]
    copy.wait()
    paired = jnp.concatenate([opair_ref[h * rows : (h + 1) * rows, :] for h in range(HEADS)], 1).astype(bf16)
    out_ref[...] = dot(paired, w_tail_ref[...]).astype(out_ref.dtype)


def value_kernel(x_ref, prob_ref, vpts_ref, own_ref, rows_ref, w_kv_ref, w_out_ref, out_ref):
    rows = own_ref.shape[0]
    tail = HEADS * CH
    own_cols = rows_ref[...]
    prob = prob_ref[...]
    mixed = dot(prob.astype(bf16), x_ref[...]).astype(bf16)
    attended = jnp.concatenate(
        [
            dot(mixed[h * rows : (h + 1) * rows], w_kv_ref[:, tail + h * CH : tail + (h + 1) * CH]).astype(bf16)
            for h in range(HEADS)
        ],
        1,
    )
    update = own_ref[...].astype(f32) + dot(attended, w_out_ref[:tail])
    gathered = dot(prob, vpts_ref[...], NT, precision=highest)
    spread = lax.broadcasted_iota(jnp.int32, (1, 3 * 128), 1) % 128 // VP
    kept = jnp.zeros((rows, 3 * 128), f32)
    for h in range(HEADS):
        kept = jnp.where(spread == h, gathered[h * rows : (h + 1) * rows], kept)
    relative = [kept[:, a * 128 : (a + 1) * 128] - own_cols[:, 9 + a : 10 + a] for a in range(3)]
    framed = []
    for b in range(3):
        framed.append(
            own_cols[:, b : b + 1] * relative[0]
            + own_cols[:, 3 + b : 4 + b] * relative[1]
            + own_cols[:, 6 + b : 7 + b] * relative[2]
        )
    length = jnp.sqrt(jnp.maximum(framed[0] * framed[0] + framed[1] * framed[1] + framed[2] * framed[2], 1.0))
    span = HEADS * VP
    for n, part in enumerate(framed + [length]):
        update = update + dot(part[:, :span].astype(bf16), w_out_ref[tail + n * span : tail + (n + 1) * span])
    out_ref[...] = update


def node_kernel(u0_ref, u1_ref, u2_ref, u3_ref, base_ref, rows_ref, w_in_ref, w_back_ref, w_edge_ref, node_ref, side_ref):
    update = (u0_ref[...].astype(f32) + u1_ref[...].astype(f32)) + (u2_ref[...].astype(f32) + u3_ref[...].astype(f32))
    normed = layer_norm(base_ref[...] + update).astype(bf16)
    middle = jnp.maximum(dot(normed, w_in_ref[...]), 0.0).astype(bf16)
    node = layer_norm(normed.astype(f32) + dot(middle, w_back_ref[...]))
    node = (node * rows_ref[:, 12:13]).astype(bf16)
    node_ref[...] = node
    side_ref[...] = dot(node, w_edge_ref[...]).astype(bf16)


def edge_kernel(
    side_ref, other_ref, rows_ref, keys_ref, pair_ref, w_in_ref, w_mid_ref, w_final_ref, out_hbm, out_ref, sems
):
    rows, keys = pair_ref.shape[:2]
    step = math.gcd(rows, 16)
    pre_rows = dot(side_ref[...], w_in_ref[CZ : CZ + NH])
    pre_keys = dot(other_ref[...], w_in_ref[CZ + NH :])
    side = side_ref[...].astype(f32)
    other = other_ref[...].astype(f32)
    keep_rows = rows_ref[:, 12:13]
    keep_keys = keys_ref[:, 12:13]
    copies = []
    for begin in range(0, rows, step):
        parts = [(begin + n, slice(n * keys, (n + 1) * keys)) for n in range(step)]
        pair = pair_ref[begin : begin + step].reshape(step * keys, CZ)
        lifted = dot(pair, w_in_ref[:CZ])
        first = jnp.concatenate(
            [jnp.maximum(lifted[at] + (pre_keys + pre_rows[i : i + 1]), 0.0).astype(bf16) for i, at in parts], 0
        )
        second = jnp.maximum(dot(first, w_mid_ref[...]), 0.0)
        joined = jnp.concatenate(
            [
                (second[:, :CZ] + pair.astype(f32)).astype(bf16),
                jnp.concatenate([(second[at, CZ : CZ + NH] + side[i : i + 1]).astype(bf16) for i, at in parts], 0),
                jnp.concatenate([(second[at, CZ + NH :] + other).astype(bf16) for i, at in parts], 0),
            ],
            1,
        )
        edge = layer_norm(dot(joined, w_final_ref[...]))
        for i, at in parts:
            out_ref[i] = (edge[at] * (keep_keys * keep_rows[i : i + 1])).astype(bf16)
        done = pl.ds(begin, step)
        copies.append(pltpu.make_async_copy(out_ref.at[done], out_hbm.at[done], sems.at[begin // step]))
        copies[-1].start()
    for copy in copies:
        copy.wait()


def tile_body(
    node_embed, rotation, translation, pair_embed, chain_index, residue_mask, step_index, w_time, w_query,
    w_query_points, w_kv, w_kvp, w_bias, head_weights, chain_bias, w_out, w_mlp_in, w_mlp_out, w_edge_in,
    w_trunk_in, w_trunk_mid, w_final,
):
    rows = node_embed.shape[0]
    total = residue_mask.shape[0]
    smem = pl.BlockSpec(memory_space=pltpu.SMEM)
    hbm = pl.BlockSpec(memory_space=pltpu.HBM)
    order = [h * (QP + VP) + n for h in range(HEADS) for n in range(QP)]
    order += [h * (QP + VP) + QP + n for h in range(HEADS) for n in range(VP)]
    order = jnp.asarray(np.eye(len(order), dtype=np.float32)[order], bf16)
    held = (
        head_weights[None], chain_bias[None], rotation, translation, residue_mask[None], chain_index[None], node_embed, w_time,
        w_query_points.T, w_kvp.T, order, w_query, w_kv,
    )
    shapes = [jax.ShapeDtypeStruct(array.shape, array.dtype) for array in held]
    shapes[-1] = jax.ShapeDtypeStruct((CS, HEADS * CH), bf16)
    bias, *held, pair = pl.pallas_call(
        bias_kernel,
        out_shape=[jax.ShapeDtypeStruct((HEADS * rows // 2, 2 * PAD), f32)] + shapes
        + [jax.ShapeDtypeStruct(pair_embed.shape, bf16)],
        in_specs=[hbm] * (2 + len(held)),
        out_specs=vmem(2 + len(held)),
        scratch_shapes=[
            pltpu.VMEM((HEADS, CZ), bf16),
            pltpu.SemaphoreType.DMA((3 + len(held),)),
        ],
        compiler_params=params(16),
    )(*stay(pair_embed, w_bias.T, *held))
    near, far = [lax.ppermute(bias, "col", [(i, i ^ k) for i in range(4)]) for k in (1, 2)]
    apart = [(4 * r + c, 4 * (r ^ (2 + c % 2)) + c) for r in range(4) for c in range(4)]
    fetched = lax.ppermute(node_embed, ("row", "col"), apart)
    beside = lax.ppermute(node_embed, "row", [(i, i ^ 1) for i in range(4)])
    others = [fetched, lax.ppermute(fetched, "col", [(i, i ^ 1) for i in range(4)]), beside]
    biases = [near, far, lax.ppermute(far, "col", [(i, i ^ 1) for i in range(4)])]
    prepared = pl.pallas_call(
        prepare_kernel,
        out_shape=(
            jax.ShapeDtypeStruct((8, CS), f32),
            jax.ShapeDtypeStruct((rows, CS), bf16),
            jax.ShapeDtypeStruct((HEADS * rows, CS), bf16),
            jax.ShapeDtypeStruct((2, HEADS * rows, 4 * HEADS * QP), bf16),
            jax.ShapeDtypeStruct((w_kvp.shape[1], CS), bf16),
            jax.ShapeDtypeStruct((16, 4 * PAD), f32),
            jax.ShapeDtypeStruct((rows, 16), f32),
            jax.ShapeDtypeStruct((rows, 16), f32),
            jax.ShapeDtypeStruct((2, HEADS), f32),
        ),
        in_specs=[smem] + vmem(13),
        out_specs=tuple(vmem(9)),
        scratch_shapes=[pltpu.VMEM((16, total), f32)],
        compiler_params=params(16),
        cost_estimate=pl.CostEstimate(flops=2 * 10**9, bytes_accessed=8 * 10**6, transcendentals=0),
    )(step_index, *held)
    time, own, qk, qpts, w_pts, kfeat, row_cols, key_cols, heads = prepared
    partial, x, prob, vpts = pl.pallas_call(
        score_kernel,
        out_shape=(
            jax.ShapeDtypeStruct((rows, CS), bf16),
            jax.ShapeDtypeStruct((4 * PAD, CS), bf16),
            jax.ShapeDtypeStruct((HEADS * rows, 4 * PAD), f32),
            jax.ShapeDtypeStruct((3 * 128, 4 * PAD), f32),
        ),
        in_specs=vmem(16) + [hbm],
        out_specs=tuple(vmem(4)),
        scratch_shapes=[
            pltpu.VMEM((2, HEADS * rows, 2 * PAD), f32),
            pltpu.VMEM((HEADS * rows, CZ), f32),
            pltpu.VMEM((4,) + bias.shape, f32),
            pltpu.VMEM((HEADS * CZ, CS), bf16),
            pltpu.SemaphoreType.DMA,
        ],
        compiler_params=params(24),
    )(heads, own, *others, time, qk, qpts, w_pts, kfeat, row_cols, bias, *biases, pair, *stay(w_out))
    base = pl.pallas_call(
        value_kernel,
        out_shape=jax.ShapeDtypeStruct((rows, CS), f32),
        in_specs=vmem(7),
        out_specs=pl.BlockSpec(memory_space=pltpu.VMEM),
        compiler_params=params(24),
        cost_estimate=pl.CostEstimate(flops=10**9, bytes_accessed=4 * 10**6, transcendentals=0),
    )(x, prob, vpts, own, row_cols, w_kv, w_out)
    partials = [lax.ppermute(partial, "col", [(i, i ^ k) for i in range(4)]) for k in (1, 2, 3)]
    node_out, side = pl.pallas_call(
        node_kernel,
        out_shape=(jax.ShapeDtypeStruct((rows, CS), bf16), jax.ShapeDtypeStruct((rows, NH), bf16)),
        in_specs=vmem(9),
        out_specs=tuple(vmem(2)),
        compiler_params=params(16),
    )(partial, *partials, base, row_cols, w_mlp_in, w_mlp_out, w_edge_in)
    turned = []
    for c in range(4):
        far = sorted((r for r in range(4) if r != c), key=lambda r: -abs(r - c))
        turned += [(4 * c + source, 4 * r + c) for r, source in zip([c] + far, (c, c ^ 1, c ^ 2, c ^ 3))]
    other = lax.ppermute(side, ("row", "col"), turned)
    pair_out = pl.pallas_call(
        edge_kernel,
        out_shape=jax.ShapeDtypeStruct(pair_embed.shape, bf16),
        in_specs=vmem(8),
        out_specs=hbm,
        scratch_shapes=[pltpu.VMEM(pair_embed.shape, bf16), pltpu.SemaphoreType.DMA((rows // math.gcd(rows, 16),))],
        compiler_params=params(24),
    )(side, other, row_cols, key_cols, pair, w_trunk_in, w_trunk_mid, w_final)
    return node_out, pair_out


def dispatch(sizes, *arrays):
    rows, keys = arrays[3].shape[:2]
    square = sizes["row"] == 4 and sizes["col"] == 4 and rows == keys and rows == 48
    return tile_body(*arrays) if square else body(*arrays)


def solution(mesh):
    return jax.shard_map(
        functools.partial(dispatch, dict(mesh.shape)),
        mesh=mesh,
        in_specs=(
            P(("groups", "row"), None),
            P(None, None, "groups"),
            P(None, "groups"),
            P(("groups", "row"), "col", None),
            P("groups"),
            P("groups"),
            P("groups"),
            P(),
            P(),
            P(),
            P(),
            P(),
            P(),
            P(),
            P(),
            P(),
            P(),
            P(),
            P(),
            P(),
            P(),
            P(),
        ),
        out_specs=(P(("groups", "row"), None), P(("groups", "row"), "col", None)),
        check_vma=False,
    )
```

```python
import functools
import math

import jax
import jax.numpy as jnp
import numpy as np
from jax import lax
from jax.experimental import pallas as pl
from jax.experimental.pallas import tpu as pltpu
from jax.sharding import PartitionSpec as P

CS = 256
CZ = 128
HEADS = 8
CH = 256
QP = 8
VP = 12
NH = 128
HID = 384


norm_epsilon = 1e-05
masked_score = 100000.0
highest = lax.Precision.HIGHEST


def layer_norm(values):
    average = jnp.mean(values, -1, keepdims=True)
    centred = values - average
    spread = jnp.mean(centred * centred, -1, keepdims=True)
    return centred * lax.rsqrt(spread + norm_epsilon)


def time_embedding(step_index, embed_width):
    half_width = embed_width // 2
    frequency = jnp.exp(-math.log(10000.0) * jnp.arange(half_width, dtype=jnp.float32) / half_width)
    angles = step_index.astype(jnp.float32)[0] * frequency
    return jnp.concatenate([jnp.sin(angles), jnp.cos(angles)])[None, :].astype(jnp.bfloat16)


def to_global(rotation, shift_vec, points):
    turned = jnp.einsum("abn,nbm->nam", rotation, points, precision=highest)
    return turned + jnp.transpose(shift_vec)[:, :, None]


def project_keys(embedded, rotation, shift_vec, w_kv, w_kvp):
    item_count = embedded.shape[0]
    key_values = jnp.dot(embedded, w_kv, preferred_element_type=jnp.float32).astype(jnp.bfloat16)
    points = jnp.dot(embedded, w_kvp, preferred_element_type=jnp.float32).reshape(item_count, 3, -1)
    return (key_values, to_global(rotation, shift_vec, points))


def node_finish(
    denominator,
    values_out,
    points_out,
    pair_sums,
    embedded,
    rotation,
    shift_vec,
    mask_rows,
    w_out,
    w_mlp_in,
    w_mlp_out,
    w_edge_in,
):
    item_count = embedded.shape[0]
    scale_back = denominator[:, :, None]
    attended = values_out.reshape(item_count, HEADS, CH) / scale_back
    points = points_out.reshape(item_count, 3, HEADS, VP) / denominator[:, None, :, None]
    relative = points - jnp.transpose(shift_vec)[:, :, None, None]
    framed = jnp.einsum("abi,iahv->ibhv", rotation, relative, precision=highest)
    length = jnp.sqrt(jnp.maximum(jnp.sum(framed * framed, 1), 1.0))
    paired = pair_sums.reshape(item_count, HEADS, CZ) / scale_back
    features = jnp.concatenate(
        [
            attended.reshape(item_count, -1),
            framed.reshape(item_count, -1),
            length.reshape(item_count, -1),
            paired.reshape(item_count, -1),
        ],
        -1,
    ).astype(jnp.bfloat16)
    update = jnp.dot(features, w_out, preferred_element_type=jnp.float32)
    normed = layer_norm(embedded.astype(jnp.float32) + update).astype(jnp.bfloat16)
    normed = lax.optimization_barrier(normed)
    middle = jax.nn.relu(jnp.dot(normed, w_mlp_in, preferred_element_type=jnp.float32)).astype(
        jnp.bfloat16
    )
    node_new = layer_norm(
        normed.astype(jnp.float32) + jnp.dot(middle, w_mlp_out, preferred_element_type=jnp.float32)
    )
    node_new = (node_new * mask_rows.astype(jnp.float32)[:, None]).astype(jnp.bfloat16)
    edge_side = jnp.dot(node_new, w_edge_in, preferred_element_type=jnp.float32).astype(
        jnp.bfloat16
    )
    return (node_new, edge_side)


def body(
    node_embed,
    rotation,
    translation,
    pair_embed,
    chain_index,
    residue_mask,
    step_index,
    w_time,
    w_query,
    w_query_points,
    w_kv,
    w_kvp,
    w_bias,
    head_weights,
    chain_bias,
    w_out,
    w_mlp_in,
    w_mlp_out,
    w_edge_in,
    w_trunk_in,
    w_trunk_mid,
    w_final,
):
    row_count = node_embed.shape[0]
    key_count = pair_embed.shape[1]
    row_start = lax.axis_index("row") * row_count
    key_start = lax.axis_index("col") * key_count
    embedded = (
        node_embed.astype(jnp.float32)
        + jnp.dot(time_embedding(step_index, CS), w_time, preferred_element_type=jnp.float32)
    ).astype(jnp.bfloat16)
    embedded = lax.optimization_barrier(embedded)
    rot_rows = lax.dynamic_slice_in_dim(rotation, row_start, row_count, 2)
    shift_rows = lax.dynamic_slice_in_dim(translation, row_start, row_count, 1)
    mask_rows = lax.dynamic_slice_in_dim(residue_mask, row_start, row_count, 0)
    mask_keys = lax.dynamic_slice_in_dim(residue_mask, key_start, key_count, 0)
    chain_rows = lax.dynamic_slice_in_dim(chain_index, row_start, row_count, 0)
    chain_keys = lax.dynamic_slice_in_dim(chain_index, key_start, key_count, 0)
    query_feat = (
        jnp.dot(embedded, w_query, preferred_element_type=jnp.float32)
        .astype(jnp.bfloat16)
        .reshape(row_count, HEADS, CH)
    )
    query_pts = to_global(
        rot_rows,
        shift_rows,
        jnp.dot(embedded, w_query_points, preferred_element_type=jnp.float32).reshape(
            row_count, 3, HEADS * QP
        ),
    ).reshape(row_count, 3, HEADS, QP)
    all_nodes = lax.all_gather(embedded, "row", axis=0, tiled=True)
    key_nodes = lax.dynamic_slice_in_dim(all_nodes, key_start, key_count, 0)
    rot_keys = lax.dynamic_slice_in_dim(rotation, key_start, key_count, 2)
    shift_keys = lax.dynamic_slice_in_dim(translation, key_start, key_count, 1)
    key_values, key_points = project_keys(key_nodes, rot_keys, shift_keys, w_kv, w_kvp)
    key_feat = key_values[:, : HEADS * CH].reshape(key_count, HEADS, CH)
    value_feat = key_values[:, HEADS * CH :].reshape(key_count, HEADS, CH)
    key_points = key_points.reshape(key_count, 3, HEADS, QP + VP)
    key_pts = key_points[..., :QP]
    value_pts = key_points[..., QP:]
    scaled = math.sqrt(1.0 / 3.0)
    point_weight = math.sqrt(2.0 / (9.0 * QP))
    point_gain = jax.nn.softplus(head_weights)
    feature_dots = jnp.einsum(
        "ihc,jhc->hij", query_feat, key_feat, preferred_element_type=jnp.float32
    ) / math.sqrt(CH)
    pair_bias = jnp.einsum("ijc,ch->hij", pair_embed, w_bias, preferred_element_type=jnp.float32)
    same_chain = (chain_rows[:, None] == chain_keys[None, :]).astype(jnp.float32)
    query_square = jnp.einsum("iahp,iahp->hi", query_pts, query_pts, precision=highest)
    key_square = jnp.einsum("jahp,jahp->hj", key_pts, key_pts, precision=highest)
    cross_term = jnp.einsum("iahp,jahp->hij", query_pts, key_pts, precision=highest)
    distance = query_square[:, :, None] + key_square[:, None, :] - 2.0 * cross_term
    mask_term = (mask_keys.astype(jnp.float32) - 1.0) * masked_score
    scores = (
        scaled * (feature_dots + pair_bias + chain_bias[:, None, None] * same_chain[None])
        - scaled * point_weight * 0.5 * point_gain[:, None, None] * distance
        + mask_term[None, None, :]
    )
    row_peak = lax.pmax(jnp.max(scores, -1), "col")
    weights = jnp.exp(scores - row_peak[:, :, None])
    denominator = jnp.transpose(jnp.sum(weights, -1))
    rounded = weights.astype(jnp.bfloat16)
    values_out = jnp.einsum(
        "hij,jhc->ihc", rounded, value_feat, preferred_element_type=jnp.float32
    ).reshape(row_count, -1)
    points_out = jnp.einsum("hij,jahv->iahv", weights, value_pts, precision=highest).reshape(
        row_count, -1
    )
    pair_sums = jnp.einsum(
        "hij,ijc->ihc", rounded, pair_embed, preferred_element_type=jnp.float32
    ).reshape(row_count, -1)
    summed = lax.psum((denominator, values_out, points_out, pair_sums), "col")
    node_out, edge_side = node_finish(
        summed[0],
        summed[1],
        summed[2],
        summed[3],
        embedded,
        rot_rows,
        shift_rows,
        mask_rows,
        w_out,
        w_mlp_in,
        w_mlp_out,
        w_edge_in,
    )
    side_all = lax.all_gather(edge_side, "row", axis=0, tiled=True)
    side_rows = lax.dynamic_slice_in_dim(side_all, row_start, row_count, 0)
    side_keys = lax.dynamic_slice_in_dim(side_all, key_start, key_count, 0)
    pre_rows = jnp.dot(side_rows, w_trunk_in[CZ : CZ + NH], preferred_element_type=jnp.float32)
    pre_keys = jnp.dot(side_keys, w_trunk_in[CZ + NH :], preferred_element_type=jnp.float32)
    mask_key_f = mask_keys.astype(jnp.float32)
    block_rows = math.gcd(row_count, 8)
    block_count = row_count // block_rows

    def edge_block(inputs):
        pair_block, pre_block, side_block, keep_block = inputs
        lifted = (
            jnp.einsum(
                "ijc,cd->ijd", pair_block, w_trunk_in[:CZ], preferred_element_type=jnp.float32
            )
            + pre_block[:, None, :]
            + pre_keys[None, :, :]
        )
        hidden_one = jax.nn.relu(lifted).astype(jnp.bfloat16)
        hidden_two = jax.nn.relu(
            jnp.einsum("ijd,de->ije", hidden_one, w_trunk_mid, preferred_element_type=jnp.float32)
        )
        stacked = jnp.concatenate(
            [
                pair_block,
                jnp.broadcast_to(side_block[:, None, :], (block_rows, key_count, NH)),
                jnp.broadcast_to(side_keys[None, :, :], (block_rows, key_count, NH)),
            ],
            -1,
        )
        joined = (hidden_two + stacked.astype(jnp.float32)).astype(jnp.bfloat16)
        edge_out = jnp.einsum("ijd,dc->ijc", joined, w_final, preferred_element_type=jnp.float32)
        pair_keep = keep_block.astype(jnp.float32)[:, None] * mask_key_f[None, :]
        return (layer_norm(edge_out) * pair_keep[:, :, None]).astype(jnp.bfloat16)

    pair_out = lax.map(
        edge_block,
        (
            pair_embed.reshape(block_count, block_rows, key_count, CZ),
            pre_rows.reshape(block_count, block_rows, HID),
            side_rows.reshape(block_count, block_rows, NH),
            mask_rows.reshape(block_count, block_rows),
        ),
    )
    return (node_out, pair_out.reshape(row_count, key_count, CZ))


PAD = 64
GAIN = math.sqrt(1.0 / 3.0)
POINT = math.sqrt(2.0 / (9.0 * QP))
f32 = jnp.float32
bf16 = jnp.bfloat16


def dot(a, b, dims=((1,), (0,)), precision=None):
    return lax.dot_general(a, b, (dims, ((), ())), precision=precision, preferred_element_type=f32)


NT = ((1,), (1,))
TN = ((0,), (0,))


def params(mib):
    return pltpu.CompilerParams(vmem_limit_bytes=mib * 1024 * 1024)


def vmem(count):
    return [pl.BlockSpec(memory_space=pltpu.VMEM)] * count


def stay(*arrays):
    return [pltpu.with_memory_space_constraint(array, pltpu.HBM) for array in arrays]


def bias_kernel(*refs):
    count = (len(refs) - 6) // 2
    pair_hbm, w_hbm, *held_hbm = refs[: 2 + count]
    out_ref, *held_refs, pair_ref, w_ref, sems = refs[2 + count :]
    half = pair_ref.shape[0] // 2
    copies = [pltpu.make_async_copy(w_hbm, w_ref, sems.at[2])]
    for m in range(2):
        at = pl.ds(m * half, half)
        copies.append(pltpu.make_async_copy(pair_hbm.at[at], pair_ref.at[at], sems.at[m]))
    for n, (src, dst) in enumerate(zip(held_hbm, held_refs)):
        if src.shape != dst.shape:
            src = src.at[:, pl.ds(0, dst.shape[1])]
        copies.append(pltpu.make_async_copy(src, dst, sems.at[3 + n]))
    for copy in copies:
        copy.start()
    for copy in copies[:3]:
        copy.wait()
    keys = pair_ref.shape[1]
    weight = w_ref[...]
    gap = jnp.zeros((PAD - keys, CZ), bf16)
    for i in range(half):
        both = jnp.concatenate([pair_ref[i], gap, pair_ref[i + half], gap], 0)
        out_ref[pl.ds(i, HEADS, stride=half), :] = dot(weight, both, NT) * GAIN
    for copy in copies[3:]:
        copy.wait()


def one_hot(shape, source_dim, offset_of):
    src = lax.broadcasted_iota(jnp.int32, shape, source_dim)
    dst = lax.broadcasted_iota(jnp.int32, shape, 1 - source_dim)
    return (src == offset_of(dst)).astype(f32)


def prepare_kernel(
    step_ref, hw_ref, cb_ref, rotation_ref, shift_ref, mask_ref, chain_ref, node_ref, w_time_ref, w_qp_ref, w_kvp_ref, order_ref,
    w_query_ref, w_kv_ref,
    time_ref, own_ref, qk_ref, qpts_ref, w_pts_ref, kfeat_ref, rows_ref, keys_ref, heads_ref, feats_ref,
):
    rows = node_ref.shape[0]
    half = CS // 2
    row = lax.axis_index("row")
    col = lax.axis_index("col")
    feats_ref[...] = jnp.zeros(feats_ref.shape, f32)
    for a in range(3):
        feats_ref[3 * a : 3 * a + 3, :] = rotation_ref[a]
    feats_ref[9:12, :] = shift_ref[...]
    feats_ref[12:13, :] = mask_ref[...].astype(f32)
    feats_ref[13:14, :] = chain_ref[...].astype(f32)
    total = feats_ref.shape[1]
    lane = lax.broadcasted_iota(jnp.int32, (8, half), 1).astype(f32)
    frequency = jnp.exp(-math.log(10000.0) * lane / half)
    angles = step_ref[0].astype(f32) * frequency
    temb = jnp.concatenate([jnp.sin(angles), jnp.cos(angles)], 1).astype(bf16)
    time = dot(temb, w_time_ref[...])
    time_ref[...] = time
    own = (node_ref[...].astype(f32) + time[0:1]).astype(bf16)
    own_ref[...] = own
    feats = feats_ref[...]

    def key_of(dst):
        part = dst // PAD
        inside = dst - part * PAD
        return jnp.where(inside < rows, part * rows + inside, -1)

    kfeat_ref[...] = dot(feats, one_hot((total, 4 * PAD), 0, key_of), precision=highest)
    own_cols = dot(one_hot((rows, total), 1, lambda d: d + row * rows), feats, NT, precision=highest)
    rows_ref[...] = own_cols
    keys_ref[...] = dot(one_hot((rows, total), 1, lambda d: d + col * rows), feats, NT, precision=highest)
    wide = HEADS * QP
    local = dot(own, w_qp_ref[...], NT)
    parts = [local[:, b * wide : (b + 1) * wide] for b in range(3)]
    points = []
    for a in range(3):
        turned = own_cols[:, 9 + a : 10 + a]
        for b in range(3):
            turned = turned + own_cols[:, 3 * a + b : 3 * a + b + 1] * parts[b]
        points.append(turned)
    points = jnp.concatenate(points + [jnp.zeros((rows, wide), f32)], 1)
    lanes = lax.broadcasted_iota(jnp.int32, (1, 4 * wide), 1)
    hw = hw_ref[...]
    gains = GAIN * POINT * 0.5 * (jnp.maximum(hw, 0.0) + jnp.log1p(jnp.exp(-jnp.abs(hw))))
    heads_ref[0:1, :] = gains
    heads_ref[1:2, :] = GAIN * cb_ref[...]
    for h in range(HEADS):
        gain = gains[:, h : h + 1]
        mine = jnp.where((lanes % wide) // QP == h, points, 0.0)
        square = jnp.sum(mine * mine, 1, keepdims=True)
        mine = jnp.where(lanes == 3 * wide, -square, 2.0 * mine) * gain
        high = mine.astype(bf16)
        qpts_ref[0, h * rows : (h + 1) * rows, :] = high
        qpts_ref[1, h * rows : (h + 1) * rows, :] = (mine - high.astype(f32)).astype(bf16)
    group = HEADS * (QP + VP)
    for a in range(3):
        at = slice(a * group, (a + 1) * group)
        w_pts_ref[at, :] = dot(order_ref[...], w_kvp_ref[at, :]).astype(bf16)
    query = dot(own, w_query_ref[...]).astype(bf16)
    for h in range(HEADS):
        taken = dot(query[:, h * CH : (h + 1) * CH], w_kv_ref[:, h * CH : (h + 1) * CH], NT)
        qk_ref[h * rows : (h + 1) * rows, :] = (taken * (GAIN / math.sqrt(CH))).astype(bf16)


def score_kernel(
    heads_ref, own_ref, n1_ref, n2_ref, n3_ref, time_ref, qk_ref, qpts_ref, w_pts_ref, kfeat_ref, rows_ref,
    b0_ref, b1_ref, b2_ref, b3_ref, pair_ref, w_out_ref,
    out_ref, x_ref, prob_ref, vpts_ref, near_ref, opair_ref, bias_ref, w_tail_ref, sem,
):
    tail = HEADS * CH + 4 * HEADS * VP
    copy = pltpu.make_async_copy(w_out_ref.at[pl.ds(tail, HEADS * CZ)], w_tail_ref, sem)
    copy.start()
    rows = own_ref.shape[0]
    half = rows // 2
    row = lax.axis_index("row")
    col = lax.axis_index("col")
    time = time_ref[0:1]
    x_ref[...] = jnp.zeros(x_ref.shape, bf16)
    x_ref[pl.ds(pl.multiple_of(row * PAD, PAD), rows), :] = own_ref[...]
    for k, ref in ((2 + col % 2, n1_ref), (3 - col % 2, n2_ref), (1, n3_ref)):
        place = row ^ k
        x_ref[pl.ds(pl.multiple_of(place * PAD, PAD), rows), :] = (ref[...].astype(f32) + time).astype(bf16)
    for k, ref in enumerate((b0_ref, b1_ref, b2_ref, b3_ref)):
        bias_ref[col ^ k] = ref[...]
    x = x_ref[...]
    keys = x.shape[0]
    kfeat = kfeat_ref[...]
    group = HEADS * (QP + VP)
    wide = HEADS * QP
    local = dot(w_pts_ref[...], x, NT)
    points = []
    for a in range(3):
        turned = kfeat[9 + a : 10 + a]
        for b in range(3):
            turned = turned + kfeat[3 * a + b : 3 * a + b + 1] * local[b * group : (b + 1) * group]
        points.append(turned)
    empty = jnp.zeros((128 - HEADS * VP, keys), f32)
    vpts_ref[...] = jnp.concatenate([part for p in points for part in (p[wide:], empty)], 0)
    key_points = [p[:wide] for p in points]
    exact = jnp.concatenate(key_points + [jnp.ones((wide, keys), f32)], 0)
    high = exact.astype(bf16)
    cross = dot(qpts_ref[0], high) + (dot(qpts_ref[0], (exact - high.astype(f32)).astype(bf16)) + dot(qpts_ref[1], high))
    key_square = key_points[0] * key_points[0] + key_points[1] * key_points[1] + key_points[2] * key_points[2]
    feature = dot(qk_ref[...], x, NT)
    lane = lax.broadcasted_iota(jnp.int32, (1, 128), 1)
    low = lane < PAD
    bias_low, bias_high = [], []
    for n in (0, 2):
        left, right = bias_ref[n], bias_ref[n + 1]
        bias_low.append(jnp.where(low, left, pltpu.roll(right, PAD, 1)))
        bias_high.append(jnp.where(low, pltpu.roll(left, PAD, 1), right))
    bias_low = jnp.concatenate(bias_low, 1)
    bias_high = jnp.concatenate(bias_high, 1)
    key_lane = lax.broadcasted_iota(jnp.int32, (1, keys), 1)
    blocked = jnp.where(key_lane % PAD < rows, (kfeat[12:13] - 1.0) * masked_score, -1e30)
    same = (rows_ref[:, 13:14] == kfeat[13:14]).astype(f32)
    gains = heads_ref[0:1]
    together = heads_ref[1:2]
    for h in range(HEADS):
        at = slice(h * rows, (h + 1) * rows)
        square = jnp.sum(key_square[h * QP : (h + 1) * QP], 0, keepdims=True)
        bias = jnp.concatenate([bias_low[h * half : (h + 1) * half], bias_high[h * half : (h + 1) * half]], 0)
        score = (
            feature[at] + bias + together[:, h : h + 1] * same + cross[at] + (blocked - gains[:, h : h + 1] * square)
        )
        peak = jnp.max(score, 1, keepdims=True)
        weight = jnp.exp(score - peak)
        weight = weight / jnp.sum(weight, 1, keepdims=True)
        prob_ref[at, :] = weight
        side = jnp.where(col >= 2, weight[:, 128:], weight[:, :128])
        near_ref[0, at, :] = jnp.where(low, pltpu.roll(side, (col % 2) * PAD, 1), 0.0)
        near_ref[1, at, :] = jnp.where(low, 0.0, pltpu.roll(side, (1 - col % 2) * PAD, 1))
    gap = jnp.zeros((PAD - pair_ref.shape[1], CZ), bf16)
    blank = jnp.zeros((2 * HEADS, 2 * PAD), f32)
    for i in range(0, rows, 4):
        weight = []
        for n in (i, i + 2):
            weight.append(
                jnp.concatenate([near_ref[m, pl.ds(n + m, HEADS, stride=rows), :] for m in (0, 1)], 0)
            )
        weight = jnp.concatenate(
            [jnp.concatenate([weight[0], blank], 1), jnp.concatenate([blank, weight[1]], 1)], 0
        ).astype(bf16)
        summed = dot(weight, jnp.concatenate([part for n in range(4) for part in (pair_ref[i + n], gap)], 0))
        for n in range(4):
            opair_ref[pl.ds(i + n, HEADS, stride=rows), :] = summed[n * HEADS : (n + 1) * HEADS]
    copy.wait()
    paired = jnp.concatenate([opair_ref[h * rows : (h + 1) * rows, :] for h in range(HEADS)], 1).astype(bf16)
    out_ref[...] = dot(paired, w_tail_ref[...]).astype(out_ref.dtype)


def value_kernel(x_ref, prob_ref, vpts_ref, own_ref, rows_ref, w_kv_ref, w_out_ref, out_ref):
    rows = own_ref.shape[0]
    tail = HEADS * CH
    own_cols = rows_ref[...]
    prob = prob_ref[...]
    mixed = dot(prob.astype(bf16), x_ref[...]).astype(bf16)
    attended = jnp.concatenate(
        [
            dot(mixed[h * rows : (h + 1) * rows], w_kv_ref[:, tail + h * CH : tail + (h + 1) * CH]).astype(bf16)
            for h in range(HEADS)
        ],
        1,
    )
    update = own_ref[...].astype(f32) + dot(attended, w_out_ref[:tail])
    gathered = dot(prob, vpts_ref[...], NT, precision=highest)
    spread = lax.broadcasted_iota(jnp.int32, (1, 3 * 128), 1) % 128 // VP
    kept = jnp.zeros((rows, 3 * 128), f32)
    for h in range(HEADS):
        kept = jnp.where(spread == h, gathered[h * rows : (h + 1) * rows], kept)
    relative = [kept[:, a * 128 : (a + 1) * 128] - own_cols[:, 9 + a : 10 + a] for a in range(3)]
    framed = []
    for b in range(3):
        framed.append(
            own_cols[:, b : b + 1] * relative[0]
            + own_cols[:, 3 + b : 4 + b] * relative[1]
            + own_cols[:, 6 + b : 7 + b] * relative[2]
        )
    length = jnp.sqrt(jnp.maximum(framed[0] * framed[0] + framed[1] * framed[1] + framed[2] * framed[2], 1.0))
    span = HEADS * VP
    for n, part in enumerate(framed + [length]):
        update = update + dot(part[:, :span].astype(bf16), w_out_ref[tail + n * span : tail + (n + 1) * span])
    out_ref[...] = update


def node_kernel(u0_ref, u1_ref, u2_ref, u3_ref, base_ref, rows_ref, w_in_ref, w_back_ref, w_edge_ref, node_ref, side_ref):
    update = (u0_ref[...].astype(f32) + u1_ref[...].astype(f32)) + (u2_ref[...].astype(f32) + u3_ref[...].astype(f32))
    normed = layer_norm(base_ref[...] + update).astype(bf16)
    middle = jnp.maximum(dot(normed, w_in_ref[...]), 0.0).astype(bf16)
    node = layer_norm(normed.astype(f32) + dot(middle, w_back_ref[...]))
    node = (node * rows_ref[:, 12:13]).astype(bf16)
    node_ref[...] = node
    side_ref[...] = dot(node, w_edge_ref[...]).astype(bf16)


def lift_kernel(node_ref, side_ref, pair_ref, w_in_ref, node_hbm, out_ref, sem):
    copy = pltpu.make_async_copy(node_ref, node_hbm, sem)
    copy.start()
    rows, keys = pair_ref.shape[:2]
    step = math.gcd(rows, 16)
    pre_rows = dot(side_ref[...], w_in_ref[CZ : CZ + NH])
    for begin in range(0, rows, step):
        lifted = dot(pair_ref[begin : begin + step].reshape(step * keys, CZ), w_in_ref[:CZ])
        for n in range(step):
            out_ref[begin + n] = lifted[n * keys : (n + 1) * keys] + pre_rows[begin + n : begin + n + 1]
    copy.wait()


def edge_kernel(
    lifted_ref, side_ref, other_ref, rows_ref, keys_ref, pair_ref, w_in_ref, w_mid_ref, w_final_ref, out_hbm, out_ref, sems
):
    rows, keys = pair_ref.shape[:2]
    step = math.gcd(rows, 16)
    pre_keys = dot(other_ref[...], w_in_ref[CZ + NH :])
    side = side_ref[...].astype(f32)
    other = other_ref[...].astype(f32)
    keep_rows = rows_ref[:, 12:13]
    keep_keys = keys_ref[:, 12:13]
    copies = []
    for begin in range(0, rows, step):
        parts = [(begin + n, slice(n * keys, (n + 1) * keys)) for n in range(step)]
        pair = pair_ref[begin : begin + step].reshape(step * keys, CZ)
        first = jnp.concatenate([jnp.maximum(lifted_ref[i] + pre_keys, 0.0).astype(bf16) for i, at in parts], 0)
        second = jnp.maximum(dot(first, w_mid_ref[...]), 0.0)
        joined = jnp.concatenate(
            [
                (second[:, :CZ] + pair.astype(f32)).astype(bf16),
                jnp.concatenate([(second[at, CZ : CZ + NH] + side[i : i + 1]).astype(bf16) for i, at in parts], 0),
                jnp.concatenate([(second[at, CZ + NH :] + other).astype(bf16) for i, at in parts], 0),
            ],
            1,
        )
        edge = layer_norm(dot(joined, w_final_ref[...]))
        for i, at in parts:
            out_ref[i] = (edge[at] * (keep_keys * keep_rows[i : i + 1])).astype(bf16)
        done = pl.ds(begin, step)
        copies.append(pltpu.make_async_copy(out_ref.at[done], out_hbm.at[done], sems.at[begin // step]))
        copies[-1].start()
    for copy in copies:
        copy.wait()


def tile_body(
    node_embed, rotation, translation, pair_embed, chain_index, residue_mask, step_index, w_time, w_query,
    w_query_points, w_kv, w_kvp, w_bias, head_weights, chain_bias, w_out, w_mlp_in, w_mlp_out, w_edge_in,
    w_trunk_in, w_trunk_mid, w_final,
):
    rows = node_embed.shape[0]
    total = residue_mask.shape[0]
    smem = pl.BlockSpec(memory_space=pltpu.SMEM)
    hbm = pl.BlockSpec(memory_space=pltpu.HBM)
    order = [h * (QP + VP) + n for h in range(HEADS) for n in range(QP)]
    order += [h * (QP + VP) + QP + n for h in range(HEADS) for n in range(VP)]
    order = jnp.asarray(np.eye(len(order), dtype=np.float32)[order], bf16)
    held = (
        head_weights[None], chain_bias[None], rotation, translation, residue_mask[None], chain_index[None], node_embed, w_time,
        w_query_points.T, w_kvp.T, order, w_query, w_kv,
    )
    shapes = [jax.ShapeDtypeStruct(array.shape, array.dtype) for array in held]
    shapes[-1] = jax.ShapeDtypeStruct((CS, HEADS * CH), bf16)
    bias, *held, pair = pl.pallas_call(
        bias_kernel,
        out_shape=[jax.ShapeDtypeStruct((HEADS * rows // 2, 2 * PAD), f32)] + shapes
        + [jax.ShapeDtypeStruct(pair_embed.shape, bf16)],
        in_specs=[hbm] * (2 + len(held)),
        out_specs=vmem(2 + len(held)),
        scratch_shapes=[
            pltpu.VMEM((HEADS, CZ), bf16),
            pltpu.SemaphoreType.DMA((3 + len(held),)),
        ],
        compiler_params=params(16),
    )(*stay(pair_embed, w_bias.T, *held))
    near, far = [lax.ppermute(bias, "col", [(i, i ^ k) for i in range(4)]) for k in (1, 2)]
    apart = [(4 * r + c, 4 * (r ^ (2 + c % 2)) + c) for r in range(4) for c in range(4)]
    fetched = lax.ppermute(node_embed, ("row", "col"), apart)
    beside = lax.ppermute(node_embed, "row", [(i, i ^ 1) for i in range(4)])
    others = [fetched, lax.ppermute(fetched, "col", [(i, i ^ 1) for i in range(4)]), beside]
    biases = [near, far, lax.ppermute(far, "col", [(i, i ^ 1) for i in range(4)])]
    prepared = pl.pallas_call(
        prepare_kernel,
        out_shape=(
            jax.ShapeDtypeStruct((8, CS), f32),
            jax.ShapeDtypeStruct((rows, CS), bf16),
            jax.ShapeDtypeStruct((HEADS * rows, CS), bf16),
            jax.ShapeDtypeStruct((2, HEADS * rows, 4 * HEADS * QP), bf16),
            jax.ShapeDtypeStruct((w_kvp.shape[1], CS), bf16),
            jax.ShapeDtypeStruct((16, 4 * PAD), f32),
            jax.ShapeDtypeStruct((rows, 16), f32),
            jax.ShapeDtypeStruct((rows, 16), f32),
            jax.ShapeDtypeStruct((2, HEADS), f32),
        ),
        in_specs=[smem] + vmem(13),
        out_specs=tuple(vmem(9)),
        scratch_shapes=[pltpu.VMEM((16, total), f32)],
        compiler_params=params(16),
        cost_estimate=pl.CostEstimate(flops=2 * 10**9, bytes_accessed=8 * 10**6, transcendentals=0),
    )(step_index, *held)
    time, own, qk, qpts, w_pts, kfeat, row_cols, key_cols, heads = prepared
    partial, x, prob, vpts = pl.pallas_call(
        score_kernel,
        out_shape=(
            jax.ShapeDtypeStruct((rows, CS), bf16),
            jax.ShapeDtypeStruct((4 * PAD, CS), bf16),
            jax.ShapeDtypeStruct((HEADS * rows, 4 * PAD), f32),
            jax.ShapeDtypeStruct((3 * 128, 4 * PAD), f32),
        ),
        in_specs=vmem(16) + [hbm],
        out_specs=tuple(vmem(4)),
        scratch_shapes=[
            pltpu.VMEM((2, HEADS * rows, 2 * PAD), f32),
            pltpu.VMEM((HEADS * rows, CZ), f32),
            pltpu.VMEM((4,) + bias.shape, f32),
            pltpu.VMEM((HEADS * CZ, CS), bf16),
            pltpu.SemaphoreType.DMA,
        ],
        compiler_params=params(24),
    )(heads, own, *others, time, qk, qpts, w_pts, kfeat, row_cols, bias, *biases, pair, *stay(w_out))
    base = pl.pallas_call(
        value_kernel,
        out_shape=jax.ShapeDtypeStruct((rows, CS), f32),
        in_specs=vmem(7),
        out_specs=pl.BlockSpec(memory_space=pltpu.VMEM),
        compiler_params=params(24),
        cost_estimate=pl.CostEstimate(flops=10**9, bytes_accessed=4 * 10**6, transcendentals=0),
    )(x, prob, vpts, own, row_cols, w_kv, w_out)
    partials = [lax.ppermute(partial, "col", [(i, i ^ k) for i in range(4)]) for k in (1, 2, 3)]
    node, side = pl.pallas_call(
        node_kernel,
        out_shape=(jax.ShapeDtypeStruct((rows, CS), bf16), jax.ShapeDtypeStruct((rows, NH), bf16)),
        in_specs=vmem(9),
        out_specs=tuple(vmem(2)),
        compiler_params=params(16),
    )(partial, *partials, base, row_cols, w_mlp_in, w_mlp_out, w_edge_in)
    turned = []
    for c in range(4):
        far = sorted((r for r in range(4) if r != c), key=lambda r: -abs(r - c))
        turned += [(4 * c + source, 4 * r + c) for r, source in zip(far + [c], (c, c ^ 1, c ^ 2, c ^ 3))]
    other = lax.ppermute(side, ("row", "col"), turned)
    node_out, lifted = pl.pallas_call(
        lift_kernel,
        out_shape=(
            jax.ShapeDtypeStruct(node.shape, bf16),
            jax.ShapeDtypeStruct(pair_embed.shape[:2] + (HID,), f32),
        ),
        in_specs=vmem(4),
        out_specs=(hbm, pl.BlockSpec(memory_space=pltpu.VMEM)),
        scratch_shapes=[pltpu.SemaphoreType.DMA],
        compiler_params=params(16),
        cost_estimate=pl.CostEstimate(flops=2 * rows * rows * CZ * HID, bytes_accessed=4 * 10**6, transcendentals=0),
    )(node, side, pair, w_trunk_in)
    pair_out = pl.pallas_call(
        edge_kernel,
        out_shape=jax.ShapeDtypeStruct(pair_embed.shape, bf16),
        in_specs=vmem(9),
        out_specs=hbm,
        scratch_shapes=[pltpu.VMEM(pair_embed.shape, bf16), pltpu.SemaphoreType.DMA((rows // math.gcd(rows, 16),))],
        compiler_params=params(24),
    )(lifted, side, other, row_cols, key_cols, pair, w_trunk_in, w_trunk_mid, w_final)
    return node_out, pair_out


def dispatch(sizes, *arrays):
    rows, keys = arrays[3].shape[:2]
    square = sizes["row"] == 4 and sizes["col"] == 4 and rows == keys and rows == 48
    return tile_body(*arrays) if square else body(*arrays)


def solution(mesh):
    return jax.shard_map(
        functools.partial(dispatch, dict(mesh.shape)),
        mesh=mesh,
        in_specs=(
            P(("groups", "row"), None),
            P(None, None, "groups"),
            P(None, "groups"),
            P(("groups", "row"), "col", None),
            P("groups"),
            P("groups"),
            P("groups"),
            P(),
            P(),
            P(),
            P(),
            P(),
            P(),
            P(),
            P(),
            P(),
            P(),
            P(),
            P(),
            P(),
            P(),
            P(),
        ),
        out_specs=(P(("groups", "row"), None), P(("groups", "row"), "col", None)),
        check_vma=False,
    )
```

```python
import functools
import math

import jax
import jax.numpy as jnp
import numpy as np
from jax import lax
from jax.experimental import pallas as pl
from jax.experimental.pallas import tpu as pltpu
from jax.sharding import PartitionSpec as P

CS = 256
CZ = 128
HEADS = 8
CH = 256
QP = 8
VP = 12
NH = 128
HID = 384


norm_epsilon = 1e-05
masked_score = 100000.0
highest = lax.Precision.HIGHEST


def layer_norm(values):
    average = jnp.mean(values, -1, keepdims=True)
    centred = values - average
    spread = jnp.mean(centred * centred, -1, keepdims=True)
    return centred * lax.rsqrt(spread + norm_epsilon)


def time_embedding(step_index, embed_width):
    half_width = embed_width // 2
    frequency = jnp.exp(-math.log(10000.0) * jnp.arange(half_width, dtype=jnp.float32) / half_width)
    angles = step_index.astype(jnp.float32)[0] * frequency
    return jnp.concatenate([jnp.sin(angles), jnp.cos(angles)])[None, :].astype(jnp.bfloat16)


def to_global(rotation, shift_vec, points):
    turned = jnp.einsum("abn,nbm->nam", rotation, points, precision=highest)
    return turned + jnp.transpose(shift_vec)[:, :, None]


def project_keys(embedded, rotation, shift_vec, w_kv, w_kvp):
    item_count = embedded.shape[0]
    key_values = jnp.dot(embedded, w_kv, preferred_element_type=jnp.float32).astype(jnp.bfloat16)
    points = jnp.dot(embedded, w_kvp, preferred_element_type=jnp.float32).reshape(item_count, 3, -1)
    return (key_values, to_global(rotation, shift_vec, points))


def node_finish(
    denominator,
    values_out,
    points_out,
    pair_sums,
    embedded,
    rotation,
    shift_vec,
    mask_rows,
    w_out,
    w_mlp_in,
    w_mlp_out,
    w_edge_in,
):
    item_count = embedded.shape[0]
    scale_back = denominator[:, :, None]
    attended = values_out.reshape(item_count, HEADS, CH) / scale_back
    points = points_out.reshape(item_count, 3, HEADS, VP) / denominator[:, None, :, None]
    relative = points - jnp.transpose(shift_vec)[:, :, None, None]
    framed = jnp.einsum("abi,iahv->ibhv", rotation, relative, precision=highest)
    length = jnp.sqrt(jnp.maximum(jnp.sum(framed * framed, 1), 1.0))
    paired = pair_sums.reshape(item_count, HEADS, CZ) / scale_back
    features = jnp.concatenate(
        [
            attended.reshape(item_count, -1),
            framed.reshape(item_count, -1),
            length.reshape(item_count, -1),
            paired.reshape(item_count, -1),
        ],
        -1,
    ).astype(jnp.bfloat16)
    update = jnp.dot(features, w_out, preferred_element_type=jnp.float32)
    normed = layer_norm(embedded.astype(jnp.float32) + update).astype(jnp.bfloat16)
    normed = lax.optimization_barrier(normed)
    middle = jax.nn.relu(jnp.dot(normed, w_mlp_in, preferred_element_type=jnp.float32)).astype(
        jnp.bfloat16
    )
    node_new = layer_norm(
        normed.astype(jnp.float32) + jnp.dot(middle, w_mlp_out, preferred_element_type=jnp.float32)
    )
    node_new = (node_new * mask_rows.astype(jnp.float32)[:, None]).astype(jnp.bfloat16)
    edge_side = jnp.dot(node_new, w_edge_in, preferred_element_type=jnp.float32).astype(
        jnp.bfloat16
    )
    return (node_new, edge_side)


def body(
    node_embed,
    rotation,
    translation,
    pair_embed,
    chain_index,
    residue_mask,
    step_index,
    w_time,
    w_query,
    w_query_points,
    w_kv,
    w_kvp,
    w_bias,
    head_weights,
    chain_bias,
    w_out,
    w_mlp_in,
    w_mlp_out,
    w_edge_in,
    w_trunk_in,
    w_trunk_mid,
    w_final,
):
    row_count = node_embed.shape[0]
    key_count = pair_embed.shape[1]
    row_start = lax.axis_index("row") * row_count
    key_start = lax.axis_index("col") * key_count
    embedded = (
        node_embed.astype(jnp.float32)
        + jnp.dot(time_embedding(step_index, CS), w_time, preferred_element_type=jnp.float32)
    ).astype(jnp.bfloat16)
    embedded = lax.optimization_barrier(embedded)
    rot_rows = lax.dynamic_slice_in_dim(rotation, row_start, row_count, 2)
    shift_rows = lax.dynamic_slice_in_dim(translation, row_start, row_count, 1)
    mask_rows = lax.dynamic_slice_in_dim(residue_mask, row_start, row_count, 0)
    mask_keys = lax.dynamic_slice_in_dim(residue_mask, key_start, key_count, 0)
    chain_rows = lax.dynamic_slice_in_dim(chain_index, row_start, row_count, 0)
    chain_keys = lax.dynamic_slice_in_dim(chain_index, key_start, key_count, 0)
    query_feat = (
        jnp.dot(embedded, w_query, preferred_element_type=jnp.float32)
        .astype(jnp.bfloat16)
        .reshape(row_count, HEADS, CH)
    )
    query_pts = to_global(
        rot_rows,
        shift_rows,
        jnp.dot(embedded, w_query_points, preferred_element_type=jnp.float32).reshape(
            row_count, 3, HEADS * QP
        ),
    ).reshape(row_count, 3, HEADS, QP)
    all_nodes = lax.all_gather(embedded, "row", axis=0, tiled=True)
    key_nodes = lax.dynamic_slice_in_dim(all_nodes, key_start, key_count, 0)
    rot_keys = lax.dynamic_slice_in_dim(rotation, key_start, key_count, 2)
    shift_keys = lax.dynamic_slice_in_dim(translation, key_start, key_count, 1)
    key_values, key_points = project_keys(key_nodes, rot_keys, shift_keys, w_kv, w_kvp)
    key_feat = key_values[:, : HEADS * CH].reshape(key_count, HEADS, CH)
    value_feat = key_values[:, HEADS * CH :].reshape(key_count, HEADS, CH)
    key_points = key_points.reshape(key_count, 3, HEADS, QP + VP)
    key_pts = key_points[..., :QP]
    value_pts = key_points[..., QP:]
    scaled = math.sqrt(1.0 / 3.0)
    point_weight = math.sqrt(2.0 / (9.0 * QP))
    point_gain = jax.nn.softplus(head_weights)
    feature_dots = jnp.einsum(
        "ihc,jhc->hij", query_feat, key_feat, preferred_element_type=jnp.float32
    ) / math.sqrt(CH)
    pair_bias = jnp.einsum("ijc,ch->hij", pair_embed, w_bias, preferred_element_type=jnp.float32)
    same_chain = (chain_rows[:, None] == chain_keys[None, :]).astype(jnp.float32)
    query_square = jnp.einsum("iahp,iahp->hi", query_pts, query_pts, precision=highest)
    key_square = jnp.einsum("jahp,jahp->hj", key_pts, key_pts, precision=highest)
    cross_term = jnp.einsum("iahp,jahp->hij", query_pts, key_pts, precision=highest)
    distance = query_square[:, :, None] + key_square[:, None, :] - 2.0 * cross_term
    mask_term = (mask_keys.astype(jnp.float32) - 1.0) * masked_score
    scores = (
        scaled * (feature_dots + pair_bias + chain_bias[:, None, None] * same_chain[None])
        - scaled * point_weight * 0.5 * point_gain[:, None, None] * distance
        + mask_term[None, None, :]
    )
    row_peak = lax.pmax(jnp.max(scores, -1), "col")
    weights = jnp.exp(scores - row_peak[:, :, None])
    denominator = jnp.transpose(jnp.sum(weights, -1))
    rounded = weights.astype(jnp.bfloat16)
    values_out = jnp.einsum(
        "hij,jhc->ihc", rounded, value_feat, preferred_element_type=jnp.float32
    ).reshape(row_count, -1)
    points_out = jnp.einsum("hij,jahv->iahv", weights, value_pts, precision=highest).reshape(
        row_count, -1
    )
    pair_sums = jnp.einsum(
        "hij,ijc->ihc", rounded, pair_embed, preferred_element_type=jnp.float32
    ).reshape(row_count, -1)
    summed = lax.psum((denominator, values_out, points_out, pair_sums), "col")
    node_out, edge_side = node_finish(
        summed[0],
        summed[1],
        summed[2],
        summed[3],
        embedded,
        rot_rows,
        shift_rows,
        mask_rows,
        w_out,
        w_mlp_in,
        w_mlp_out,
        w_edge_in,
    )
    side_all = lax.all_gather(edge_side, "row", axis=0, tiled=True)
    side_rows = lax.dynamic_slice_in_dim(side_all, row_start, row_count, 0)
    side_keys = lax.dynamic_slice_in_dim(side_all, key_start, key_count, 0)
    pre_rows = jnp.dot(side_rows, w_trunk_in[CZ : CZ + NH], preferred_element_type=jnp.float32)
    pre_keys = jnp.dot(side_keys, w_trunk_in[CZ + NH :], preferred_element_type=jnp.float32)
    mask_key_f = mask_keys.astype(jnp.float32)
    block_rows = math.gcd(row_count, 8)
    block_count = row_count // block_rows

    def edge_block(inputs):
        pair_block, pre_block, side_block, keep_block = inputs
        lifted = (
            jnp.einsum(
                "ijc,cd->ijd", pair_block, w_trunk_in[:CZ], preferred_element_type=jnp.float32
            )
            + pre_block[:, None, :]
            + pre_keys[None, :, :]
        )
        hidden_one = jax.nn.relu(lifted).astype(jnp.bfloat16)
        hidden_two = jax.nn.relu(
            jnp.einsum("ijd,de->ije", hidden_one, w_trunk_mid, preferred_element_type=jnp.float32)
        )
        stacked = jnp.concatenate(
            [
                pair_block,
                jnp.broadcast_to(side_block[:, None, :], (block_rows, key_count, NH)),
                jnp.broadcast_to(side_keys[None, :, :], (block_rows, key_count, NH)),
            ],
            -1,
        )
        joined = (hidden_two + stacked.astype(jnp.float32)).astype(jnp.bfloat16)
        edge_out = jnp.einsum("ijd,dc->ijc", joined, w_final, preferred_element_type=jnp.float32)
        pair_keep = keep_block.astype(jnp.float32)[:, None] * mask_key_f[None, :]
        return (layer_norm(edge_out) * pair_keep[:, :, None]).astype(jnp.bfloat16)

    pair_out = lax.map(
        edge_block,
        (
            pair_embed.reshape(block_count, block_rows, key_count, CZ),
            pre_rows.reshape(block_count, block_rows, HID),
            side_rows.reshape(block_count, block_rows, NH),
            mask_rows.reshape(block_count, block_rows),
        ),
    )
    return (node_out, pair_out.reshape(row_count, key_count, CZ))


PAD = 64
GAIN = math.sqrt(1.0 / 3.0)
POINT = math.sqrt(2.0 / (9.0 * QP))
f32 = jnp.float32
bf16 = jnp.bfloat16


def dot(a, b, dims=((1,), (0,)), precision=None):
    return lax.dot_general(a, b, (dims, ((), ())), precision=precision, preferred_element_type=f32)


NT = ((1,), (1,))
TN = ((0,), (0,))


def params(mib):
    return pltpu.CompilerParams(vmem_limit_bytes=mib * 1024 * 1024)


def vmem(count):
    return [pl.BlockSpec(memory_space=pltpu.VMEM)] * count


def stay(*arrays):
    return [pltpu.with_memory_space_constraint(array, pltpu.HBM) for array in arrays]


def bias_kernel(*refs):
    count = (len(refs) - 6) // 2
    pair_hbm, w_hbm, *held_hbm = refs[: 2 + count]
    out_ref, *held_refs, pair_ref, w_ref, sems = refs[2 + count :]
    half = pair_ref.shape[0] // 2
    copies = [pltpu.make_async_copy(w_hbm, w_ref, sems.at[2])]
    for m in range(2):
        at = pl.ds(m * half, half)
        copies.append(pltpu.make_async_copy(pair_hbm.at[at], pair_ref.at[at], sems.at[m]))
    for n, (src, dst) in enumerate(zip(held_hbm, held_refs)):
        if src.shape != dst.shape:
            src = src.at[:, pl.ds(0, dst.shape[1])]
        copies.append(pltpu.make_async_copy(src, dst, sems.at[3 + n]))
    for copy in copies:
        copy.start()
    for copy in copies[:3]:
        copy.wait()
    keys = pair_ref.shape[1]
    weight = w_ref[...]
    gap = jnp.zeros((PAD - keys, CZ), bf16)
    for i in range(half):
        both = jnp.concatenate([pair_ref[i], gap, pair_ref[i + half], gap], 0)
        out_ref[pl.ds(i, HEADS, stride=half), :] = dot(weight, both, NT) * GAIN
    for copy in copies[3:]:
        copy.wait()


def one_hot(shape, source_dim, offset_of):
    src = lax.broadcasted_iota(jnp.int32, shape, source_dim)
    dst = lax.broadcasted_iota(jnp.int32, shape, 1 - source_dim)
    return (src == offset_of(dst)).astype(f32)


def prepare_kernel(
    step_ref, hw_ref, cb_ref, rotation_ref, shift_ref, mask_ref, chain_ref, node_ref, w_time_ref, w_qp_ref, w_kvp_ref, order_ref,
    w_query_ref, w_kv_ref,
    time_ref, own_ref, qk_ref, qpts_ref, w_pts_ref, kfeat_ref, rows_ref, keys_ref, heads_ref, feats_ref,
):
    rows = node_ref.shape[0]
    half = CS // 2
    row = lax.axis_index("row")
    col = lax.axis_index("col")
    feats_ref[...] = jnp.zeros(feats_ref.shape, f32)
    for a in range(3):
        feats_ref[3 * a : 3 * a + 3, :] = rotation_ref[a]
    feats_ref[9:12, :] = shift_ref[...]
    feats_ref[12:13, :] = mask_ref[...].astype(f32)
    feats_ref[13:14, :] = chain_ref[...].astype(f32)
    total = feats_ref.shape[1]
    lane = lax.broadcasted_iota(jnp.int32, (8, half), 1).astype(f32)
    frequency = jnp.exp(-math.log(10000.0) * lane / half)
    angles = step_ref[0].astype(f32) * frequency
    temb = jnp.concatenate([jnp.sin(angles), jnp.cos(angles)], 1).astype(bf16)
    time = dot(temb, w_time_ref[...])
    time_ref[...] = time
    own = (node_ref[...].astype(f32) + time[0:1]).astype(bf16)
    own_ref[...] = own
    feats = feats_ref[...]

    def key_of(dst):
        part = dst // PAD
        inside = dst - part * PAD
        return jnp.where(inside < rows, part * rows + inside, -1)

    kfeat_ref[...] = dot(feats, one_hot((total, 4 * PAD), 0, key_of), precision=highest)
    own_cols = dot(one_hot((rows, total), 1, lambda d: d + row * rows), feats, NT, precision=highest)
    rows_ref[...] = own_cols
    keys_ref[...] = dot(one_hot((rows, total), 1, lambda d: d + col * rows), feats, NT, precision=highest)
    wide = HEADS * QP
    local = dot(own, w_qp_ref[...], NT)
    parts = [local[:, b * wide : (b + 1) * wide] for b in range(3)]
    points = []
    for a in range(3):
        turned = own_cols[:, 9 + a : 10 + a]
        for b in range(3):
            turned = turned + own_cols[:, 3 * a + b : 3 * a + b + 1] * parts[b]
        points.append(turned)
    points = jnp.concatenate(points + [jnp.zeros((rows, wide), f32)], 1)
    lanes = lax.broadcasted_iota(jnp.int32, (1, 4 * wide), 1)
    hw = hw_ref[...]
    gains = GAIN * POINT * 0.5 * (jnp.maximum(hw, 0.0) + jnp.log1p(jnp.exp(-jnp.abs(hw))))
    heads_ref[0:1, :] = gains
    heads_ref[1:2, :] = GAIN * cb_ref[...]
    for h in range(HEADS):
        gain = gains[:, h : h + 1]
        mine = jnp.where((lanes % wide) // QP == h, points, 0.0)
        square = jnp.sum(mine * mine, 1, keepdims=True)
        mine = jnp.where(lanes == 3 * wide, -square, 2.0 * mine) * gain
        high = mine.astype(bf16)
        qpts_ref[0, h * rows : (h + 1) * rows, :] = high
        qpts_ref[1, h * rows : (h + 1) * rows, :] = (mine - high.astype(f32)).astype(bf16)
    group = HEADS * (QP + VP)
    for a in range(3):
        at = slice(a * group, (a + 1) * group)
        w_pts_ref[at, :] = dot(order_ref[...], w_kvp_ref[at, :]).astype(bf16)
    query = dot(own, w_query_ref[...]).astype(bf16)
    for h in range(HEADS):
        taken = dot(query[:, h * CH : (h + 1) * CH], w_kv_ref[:, h * CH : (h + 1) * CH], NT)
        qk_ref[h * rows : (h + 1) * rows, :] = (taken * (GAIN / math.sqrt(CH))).astype(bf16)


def score_kernel(
    heads_ref, own_ref, n1_ref, n2_ref, n3_ref, time_ref, qk_ref, qpts_ref, w_pts_ref, kfeat_ref, rows_ref,
    b0_ref, b1_ref, b2_ref, b3_ref, pair_ref, w_out_ref,
    out_ref, x_ref, prob_ref, vpts_ref, near_ref, opair_ref, bias_ref, w_tail_ref, sem,
):
    tail = HEADS * CH + 4 * HEADS * VP
    copy = pltpu.make_async_copy(w_out_ref.at[pl.ds(tail, HEADS * CZ)], w_tail_ref, sem)
    copy.start()
    rows = own_ref.shape[0]
    half = rows // 2
    row = lax.axis_index("row")
    col = lax.axis_index("col")
    time = time_ref[0:1]
    x_ref[...] = jnp.zeros(x_ref.shape, bf16)
    x_ref[pl.ds(pl.multiple_of(row * PAD, PAD), rows), :] = own_ref[...]
    for k, ref in ((2 + col % 2, n1_ref), (3 - col % 2, n2_ref), (1, n3_ref)):
        place = row ^ k
        x_ref[pl.ds(pl.multiple_of(place * PAD, PAD), rows), :] = (ref[...].astype(f32) + time).astype(bf16)
    for k, ref in enumerate((b0_ref, b1_ref, b2_ref, b3_ref)):
        bias_ref[col ^ k] = ref[...]
    x = x_ref[...]
    keys = x.shape[0]
    kfeat = kfeat_ref[...]
    group = HEADS * (QP + VP)
    wide = HEADS * QP
    local = dot(w_pts_ref[...], x, NT)
    points = []
    for a in range(3):
        turned = kfeat[9 + a : 10 + a]
        for b in range(3):
            turned = turned + kfeat[3 * a + b : 3 * a + b + 1] * local[b * group : (b + 1) * group]
        points.append(turned)
    empty = jnp.zeros((128 - HEADS * VP, keys), f32)
    vpts_ref[...] = jnp.concatenate([part for p in points for part in (p[wide:], empty)], 0)
    key_points = [p[:wide] for p in points]
    exact = jnp.concatenate(key_points + [jnp.ones((wide, keys), f32)], 0)
    high = exact.astype(bf16)
    cross = dot(qpts_ref[0], high) + (dot(qpts_ref[0], (exact - high.astype(f32)).astype(bf16)) + dot(qpts_ref[1], high))
    key_square = key_points[0] * key_points[0] + key_points[1] * key_points[1] + key_points[2] * key_points[2]
    feature = dot(qk_ref[...], x, NT)
    lane = lax.broadcasted_iota(jnp.int32, (1, 128), 1)
    low = lane < PAD
    bias_low, bias_high = [], []
    for n in (0, 2):
        left, right = bias_ref[n], bias_ref[n + 1]
        bias_low.append(jnp.where(low, left, pltpu.roll(right, PAD, 1)))
        bias_high.append(jnp.where(low, pltpu.roll(left, PAD, 1), right))
    bias_low = jnp.concatenate(bias_low, 1)
    bias_high = jnp.concatenate(bias_high, 1)
    key_lane = lax.broadcasted_iota(jnp.int32, (1, keys), 1)
    blocked = jnp.where(key_lane % PAD < rows, (kfeat[12:13] - 1.0) * masked_score, -1e30)
    same = (rows_ref[:, 13:14] == kfeat[13:14]).astype(f32)
    gains = heads_ref[0:1]
    together = heads_ref[1:2]
    for h in range(HEADS):
        at = slice(h * rows, (h + 1) * rows)
        square = jnp.sum(key_square[h * QP : (h + 1) * QP], 0, keepdims=True)
        bias = jnp.concatenate([bias_low[h * half : (h + 1) * half], bias_high[h * half : (h + 1) * half]], 0)
        score = (
            feature[at] + bias + together[:, h : h + 1] * same + cross[at] + (blocked - gains[:, h : h + 1] * square)
        )
        peak = jnp.max(score, 1, keepdims=True)
        weight = jnp.exp(score - peak)
        weight = weight * (1.0 / jnp.sum(weight, 1, keepdims=True))
        prob_ref[at, :] = weight
        side = jnp.where(col >= 2, weight[:, 128:], weight[:, :128])
        near_ref[0, at, :] = jnp.where(low, pltpu.roll(side, (col % 2) * PAD, 1), 0.0)
        near_ref[1, at, :] = jnp.where(low, 0.0, pltpu.roll(side, (1 - col % 2) * PAD, 1))
    gap = jnp.zeros((PAD - pair_ref.shape[1], CZ), bf16)
    blank = jnp.zeros((2 * HEADS, 2 * PAD), f32)
    for i in range(0, rows, 4):
        weight = []
        for n in (i, i + 2):
            weight.append(
                jnp.concatenate([near_ref[m, pl.ds(n + m, HEADS, stride=rows), :] for m in (0, 1)], 0)
            )
        weight = jnp.concatenate(
            [jnp.concatenate([weight[0], blank], 1), jnp.concatenate([blank, weight[1]], 1)], 0
        ).astype(bf16)
        summed = dot(weight, jnp.concatenate([part for n in range(4) for part in (pair_ref[i + n], gap)], 0))
        for n in range(4):
            opair_ref[pl.ds(i + n, HEADS, stride=rows), :] = summed[n * HEADS : (n + 1) * HEADS]
    copy.wait()
    paired = jnp.concatenate([opair_ref[h * rows : (h + 1) * rows, :] for h in range(HEADS)], 1).astype(bf16)
    out_ref[...] = dot(paired, w_tail_ref[...]).astype(out_ref.dtype)


def value_kernel(x_ref, prob_ref, vpts_ref, own_ref, rows_ref, w_kv_ref, w_out_ref, out_ref):
    rows = own_ref.shape[0]
    tail = HEADS * CH
    own_cols = rows_ref[...]
    prob = prob_ref[...]
    mixed = dot(prob.astype(bf16), x_ref[...]).astype(bf16)
    attended = jnp.concatenate(
        [
            dot(mixed[h * rows : (h + 1) * rows], w_kv_ref[:, tail + h * CH : tail + (h + 1) * CH]).astype(bf16)
            for h in range(HEADS)
        ],
        1,
    )
    update = own_ref[...].astype(f32) + dot(attended, w_out_ref[:tail])
    gathered = dot(prob, vpts_ref[...], NT, precision=highest)
    spread = lax.broadcasted_iota(jnp.int32, (1, 3 * 128), 1) % 128 // VP
    kept = jnp.zeros((rows, 3 * 128), f32)
    for h in range(HEADS):
        kept = jnp.where(spread == h, gathered[h * rows : (h + 1) * rows], kept)
    relative = [kept[:, a * 128 : (a + 1) * 128] - own_cols[:, 9 + a : 10 + a] for a in range(3)]
    framed = []
    for b in range(3):
        framed.append(
            own_cols[:, b : b + 1] * relative[0]
            + own_cols[:, 3 + b : 4 + b] * relative[1]
            + own_cols[:, 6 + b : 7 + b] * relative[2]
        )
    length = jnp.sqrt(jnp.maximum(framed[0] * framed[0] + framed[1] * framed[1] + framed[2] * framed[2], 1.0))
    span = HEADS * VP
    for n, part in enumerate(framed + [length]):
        update = update + dot(part[:, :span].astype(bf16), w_out_ref[tail + n * span : tail + (n + 1) * span])
    out_ref[...] = update


def node_kernel(u0_ref, u1_ref, u2_ref, u3_ref, base_ref, rows_ref, w_in_ref, w_back_ref, w_edge_ref, node_ref, side_ref):
    update = (u0_ref[...].astype(f32) + u1_ref[...].astype(f32)) + (u2_ref[...].astype(f32) + u3_ref[...].astype(f32))
    normed = layer_norm(base_ref[...] + update).astype(bf16)
    middle = jnp.maximum(dot(normed, w_in_ref[...]), 0.0).astype(bf16)
    node = layer_norm(normed.astype(f32) + dot(middle, w_back_ref[...]))
    node = (node * rows_ref[:, 12:13]).astype(bf16)
    node_ref[...] = node
    side_ref[...] = dot(node, w_edge_ref[...]).astype(bf16)


def lift_kernel(node_ref, side_ref, pair_ref, w_in_ref, node_hbm, out_ref, sem):
    copy = pltpu.make_async_copy(node_ref, node_hbm, sem)
    copy.start()
    rows, keys = pair_ref.shape[:2]
    step = math.gcd(rows, 16)
    pre_rows = dot(side_ref[...], w_in_ref[CZ : CZ + NH])
    for begin in range(0, rows, step):
        lifted = dot(pair_ref[begin : begin + step].reshape(step * keys, CZ), w_in_ref[:CZ])
        for n in range(step):
            out_ref[begin + n] = lifted[n * keys : (n + 1) * keys] + pre_rows[begin + n : begin + n + 1]
    copy.wait()


def edge_kernel(
    lifted_ref, side_ref, other_ref, rows_ref, keys_ref, pair_ref, w_in_ref, w_mid_ref, w_final_ref, out_hbm, out_ref, sems
):
    rows, keys = pair_ref.shape[:2]
    step = math.gcd(rows, 16)
    pre_keys = dot(other_ref[...], w_in_ref[CZ + NH :])
    side = side_ref[...].astype(f32)
    other = other_ref[...].astype(f32)
    keep_rows = rows_ref[:, 12:13]
    keep_keys = keys_ref[:, 12:13]
    copies = []
    for begin in range(0, rows, step):
        parts = [(begin + n, slice(n * keys, (n + 1) * keys)) for n in range(step)]
        pair = pair_ref[begin : begin + step].reshape(step * keys, CZ)
        first = jnp.concatenate([jnp.maximum(lifted_ref[i] + pre_keys, 0.0).astype(bf16) for i, at in parts], 0)
        second = jnp.maximum(dot(first, w_mid_ref[...]), 0.0)
        joined = jnp.concatenate(
            [
                (second[:, :CZ] + pair.astype(f32)).astype(bf16),
                jnp.concatenate([(second[at, CZ : CZ + NH] + side[i : i + 1]).astype(bf16) for i, at in parts], 0),
                jnp.concatenate([(second[at, CZ + NH :] + other).astype(bf16) for i, at in parts], 0),
            ],
            1,
        )
        edge = layer_norm(dot(joined, w_final_ref[...]))
        for i, at in parts:
            out_ref[i] = (edge[at] * (keep_keys * keep_rows[i : i + 1])).astype(bf16)
        done = pl.ds(begin, step)
        copies.append(pltpu.make_async_copy(out_ref.at[done], out_hbm.at[done], sems.at[begin // step]))
        copies[-1].start()
    for copy in copies:
        copy.wait()


def tile_body(
    node_embed, rotation, translation, pair_embed, chain_index, residue_mask, step_index, w_time, w_query,
    w_query_points, w_kv, w_kvp, w_bias, head_weights, chain_bias, w_out, w_mlp_in, w_mlp_out, w_edge_in,
    w_trunk_in, w_trunk_mid, w_final,
):
    rows = node_embed.shape[0]
    total = residue_mask.shape[0]
    smem = pl.BlockSpec(memory_space=pltpu.SMEM)
    hbm = pl.BlockSpec(memory_space=pltpu.HBM)
    order = [h * (QP + VP) + n for h in range(HEADS) for n in range(QP)]
    order += [h * (QP + VP) + QP + n for h in range(HEADS) for n in range(VP)]
    order = jnp.asarray(np.eye(len(order), dtype=np.float32)[order], bf16)
    held = (
        head_weights[None], chain_bias[None], rotation, translation, residue_mask[None], chain_index[None], node_embed, w_time,
        w_query_points.T, w_kvp.T, order, w_query, w_kv,
    )
    shapes = [jax.ShapeDtypeStruct(array.shape, array.dtype) for array in held]
    shapes[-1] = jax.ShapeDtypeStruct((CS, HEADS * CH), bf16)
    bias, *held, pair = pl.pallas_call(
        bias_kernel,
        out_shape=[jax.ShapeDtypeStruct((HEADS * rows // 2, 2 * PAD), f32)] + shapes
        + [jax.ShapeDtypeStruct(pair_embed.shape, bf16)],
        in_specs=[hbm] * (2 + len(held)),
        out_specs=vmem(2 + len(held)),
        scratch_shapes=[
            pltpu.VMEM((HEADS, CZ), bf16),
            pltpu.SemaphoreType.DMA((3 + len(held),)),
        ],
        compiler_params=params(16),
    )(*stay(pair_embed, w_bias.T, *held))
    near, far = [lax.ppermute(bias, "col", [(i, i ^ k) for i in range(4)]) for k in (1, 2)]
    apart = [(4 * r + c, 4 * (r ^ (3 - c % 2)) + (c ^ 1)) for r in range(4) for c in range(4)]
    fetched = lax.ppermute(node_embed, ("row", "col"), apart)
    beside = lax.ppermute(node_embed, "row", [(i, i ^ 1) for i in range(4)])
    others = [fetched, lax.ppermute(fetched, "col", [(i, i ^ 1) for i in range(4)]), beside]
    biases = [near, far, lax.ppermute(far, "col", [(i, i ^ 1) for i in range(4)])]
    prepared = pl.pallas_call(
        prepare_kernel,
        out_shape=(
            jax.ShapeDtypeStruct((8, CS), f32),
            jax.ShapeDtypeStruct((rows, CS), bf16),
            jax.ShapeDtypeStruct((HEADS * rows, CS), bf16),
            jax.ShapeDtypeStruct((2, HEADS * rows, 4 * HEADS * QP), bf16),
            jax.ShapeDtypeStruct((w_kvp.shape[1], CS), bf16),
            jax.ShapeDtypeStruct((16, 4 * PAD), f32),
            jax.ShapeDtypeStruct((rows, 16), f32),
            jax.ShapeDtypeStruct((rows, 16), f32),
            jax.ShapeDtypeStruct((2, HEADS), f32),
        ),
        in_specs=[smem] + vmem(13),
        out_specs=tuple(vmem(9)),
        scratch_shapes=[pltpu.VMEM((16, total), f32)],
        compiler_params=params(16),
        cost_estimate=pl.CostEstimate(flops=2 * 10**9, bytes_accessed=8 * 10**6, transcendentals=0),
    )(step_index, *held)
    time, own, qk, qpts, w_pts, kfeat, row_cols, key_cols, heads = prepared
    partial, x, prob, vpts = pl.pallas_call(
        score_kernel,
        out_shape=(
            jax.ShapeDtypeStruct((rows, CS), bf16),
            jax.ShapeDtypeStruct((4 * PAD, CS), bf16),
            jax.ShapeDtypeStruct((HEADS * rows, 4 * PAD), f32),
            jax.ShapeDtypeStruct((3 * 128, 4 * PAD), f32),
        ),
        in_specs=vmem(16) + [hbm],
        out_specs=tuple(vmem(4)),
        scratch_shapes=[
            pltpu.VMEM((2, HEADS * rows, 2 * PAD), f32),
            pltpu.VMEM((HEADS * rows, CZ), f32),
            pltpu.VMEM((4,) + bias.shape, f32),
            pltpu.VMEM((HEADS * CZ, CS), bf16),
            pltpu.SemaphoreType.DMA,
        ],
        compiler_params=params(24),
    )(heads, own, *others, time, qk, qpts, w_pts, kfeat, row_cols, bias, *biases, pair, *stay(w_out))
    base = pl.pallas_call(
        value_kernel,
        out_shape=jax.ShapeDtypeStruct((rows, CS), f32),
        in_specs=vmem(7),
        out_specs=pl.BlockSpec(memory_space=pltpu.VMEM),
        compiler_params=params(24),
        cost_estimate=pl.CostEstimate(flops=10**9, bytes_accessed=4 * 10**6, transcendentals=0),
    )(x, prob, vpts, own, row_cols, w_kv, w_out)
    partials = [lax.ppermute(partial, "col", [(i, i ^ k) for i in range(4)]) for k in (1, 2, 3)]
    node, side = pl.pallas_call(
        node_kernel,
        out_shape=(jax.ShapeDtypeStruct((rows, CS), bf16), jax.ShapeDtypeStruct((rows, NH), bf16)),
        in_specs=vmem(9),
        out_specs=tuple(vmem(2)),
        compiler_params=params(16),
    )(partial, *partials, base, row_cols, w_mlp_in, w_mlp_out, w_edge_in)
    turned = []
    for c in range(4):
        far = sorted((r for r in range(4) if r != c), key=lambda r: -abs(r - c))
        turned += [(4 * c + source, 4 * r + c) for r, source in zip(far + [c], (c ^ 1, c, c ^ 2, c ^ 3))]
    other = lax.ppermute(side, ("row", "col"), turned)
    node_out, lifted = pl.pallas_call(
        lift_kernel,
        out_shape=(
            jax.ShapeDtypeStruct(node.shape, bf16),
            jax.ShapeDtypeStruct(pair_embed.shape[:2] + (HID,), f32),
        ),
        in_specs=vmem(4),
        out_specs=(hbm, pl.BlockSpec(memory_space=pltpu.VMEM)),
        scratch_shapes=[pltpu.SemaphoreType.DMA],
        compiler_params=params(16),
        cost_estimate=pl.CostEstimate(flops=2 * rows * rows * CZ * HID, bytes_accessed=4 * 10**6, transcendentals=0),
    )(node, side, pair, w_trunk_in)
    pair_out = pl.pallas_call(
        edge_kernel,
        out_shape=jax.ShapeDtypeStruct(pair_embed.shape, bf16),
        in_specs=vmem(9),
        out_specs=hbm,
        scratch_shapes=[pltpu.VMEM(pair_embed.shape, bf16), pltpu.SemaphoreType.DMA((rows // math.gcd(rows, 16),))],
        compiler_params=params(24),
    )(lifted, side, other, row_cols, key_cols, pair, w_trunk_in, w_trunk_mid, w_final)
    return node_out, pair_out


def dispatch(sizes, *arrays):
    rows, keys = arrays[3].shape[:2]
    square = sizes["row"] == 4 and sizes["col"] == 4 and rows == keys and rows == 48
    return tile_body(*arrays) if square else body(*arrays)


def solution(mesh):
    return jax.shard_map(
        functools.partial(dispatch, dict(mesh.shape)),
        mesh=mesh,
        in_specs=(
            P(("groups", "row"), None),
            P(None, None, "groups"),
            P(None, "groups"),
            P(("groups", "row"), "col", None),
            P("groups"),
            P("groups"),
            P("groups"),
            P(),
            P(),
            P(),
            P(),
            P(),
            P(),
            P(),
            P(),
            P(),
            P(),
            P(),
            P(),
            P(),
            P(),
            P(),
        ),
        out_specs=(P(("groups", "row"), None), P(("groups", "row"), "col", None)),
        check_vma=False,
    )
```
